32 devices in a mesh: dp: 4 (over x, core), seq: 8 (over z, y).
Axes of the slice: x: 2, y: 2, z: 4, core: 2. Of those that a mesh axis runs over, the one named last changes fastest.
Arguments:
- inputs: bfloat16 [4, 1024, 2048], P('dp', 'seq'), may hold values from -6 to 6
- cotangent: bfloat16 [4, 1024, 2048], P('dp', 'seq'), may hold values from -6 to 6
- resets: int32 [4, 1024], P('dp', 'seq'), may hold values from 0 to 1, as said below
- real_mask: int32 [4, 1024], P('dp', 'seq'), may hold values from 0 to 1, as said below
- gain_mix: bfloat16 [2048], P('seq'), may hold values from 0.25 to 1.75
- w_branch_gate: bfloat16 [2048, 2560], P('seq', 'dp'), may hold values from -0.125 to 0.125
- w_branch_x: bfloat16 [2048, 2560], P('seq', 'dp'), may hold values from -0.125 to 0.125
- conv_kernel: bfloat16 [2560, 4], P(('dp', 'seq')), may hold values from -3 to 3
- gate_rate: bfloat16 [2560, 160], P(('dp', 'seq')), may hold values from -0.5 to 0.5
- gate_input: bfloat16 [2560, 160], P(('dp', 'seq')), may hold values from -0.5 to 0.5
- decay_param: bfloat16 [2560], P(('dp', 'seq')), may hold values from -10.375 to -3.890625
- w_mix_out: bfloat16 [2560, 2048], P(('dp', 'seq')), may hold values from -0.3125 to 0.3125
- gain_mlp: bfloat16 [2048], P('seq'), may hold values from 0.25 to 1.75
- w_mlp_gate: bfloat16 [2048, 6144], P('seq', 'dp'), may hold values from -0.125 to 0.125
- w_mlp_up: bfloat16 [2048, 6144], P('seq', 'dp'), may hold values from -0.125 to 0.125
- w_mlp_down: bfloat16 [6144, 2048], P(('dp', 'seq')), may hold values from -0.109375 to 0.109375
Outputs:
- output: bfloat16 [4, 1024, 2048], P('dp', 'seq')
- grad_inputs: bfloat16 [4, 1024, 2048], P('dp', 'seq')
- grad_gain_mix: float32 [2048], P(('dp', 'seq'))
- grad_w_branch_gate: float32 [2048, 2560], P('seq', 'dp')
- grad_w_branch_x: float32 [2048, 2560], P('seq', 'dp')
- grad_conv_kernel: float32 [2560, 4], P(('dp', 'seq'))
- grad_gate_rate: float32 [2560, 160], P(('dp', 'seq'))
- grad_gate_input: float32 [2560, 160], P(('dp', 'seq'))
- grad_decay_param: float32 [2560], P(('dp', 'seq'))
- grad_w_mix_out: float32 [2560, 2048], P(('dp', 'seq'))
- grad_gain_mlp: float32 [2048], P(('dp', 'seq'))
- grad_w_mlp_gate: float32 [2048, 6144], P('seq', 'dp')
- grad_w_mlp_up: float32 [2048, 6144], P('seq', 'dp')
- grad_w_mlp_down: float32 [6144, 2048], P(('dp', 'seq'))
- decay_log: float32 [2560], P(('dp', 'seq'))
The draws below stay inside these ranges and needn't reach their ends.
Inputs may be any that keep to these rules, and one draw needn't show every extreme that they name: `resets`: position 0 starts a document in every row. In each aligned block of 1 row one row, drawn from the seed, has exactly two more starts, one among positions 1 to 127 and one among the last 127 positions but the last one. Every other row has its further starts within two positions of nonzero multiples of 128, at most one near each multiple and at least one in the row. `real_mask`: in each row 1 on a prefix that reaches past the row's last document start, 0 after it.
All inputs are finite; a program needn't handle non-finite values.
Results may differ from the reference program's by a relative error of at most 0.023.
Values may be sent and summed in bfloat16 or wider, within the bound.
A program may use at most 128 MiB of HBM per device.

```python
import jax
import jax.numpy as jnp
from jax import lax

D = 2048
W = 2560
F = 6144
KERNEL = 4
ROWS_DEV = 1
TOK_DEV = 128
BLOCK = 160
LENGTH = 1024
BATCH = 4


def draw_layout(key):
    key_pick, key_first, key_last, key_present, key_force, key_offset = jax.random.split(key, 6)
    groups = BATCH // ROWS_DEV
    spans = LENGTH // TOK_DEV
    pick = jax.random.randint(key_pick, (groups, 1), 0, ROWS_DEV)
    within = jnp.arange(ROWS_DEV, dtype=jnp.int32)[None, :]
    is_long = (within == pick).reshape(BATCH, 1)
    positions = jnp.arange(LENGTH, dtype=jnp.int32)[None, :]
    first_start = jax.random.randint(key_first, (BATCH, 1), 1, TOK_DEV)
    last_start = jax.random.randint(key_last, (BATCH, 1), LENGTH - TOK_DEV + 1, LENGTH - 1)
    long_starts = (positions == 0) | (positions == first_start) | (positions == last_start)
    bounds = jnp.arange(spans, dtype=jnp.int32)[None, :]
    present = jax.random.randint(key_present, (BATCH, spans), 0, 2)
    forced = jax.random.randint(key_force, (BATCH, 1), 1, spans)
    present = jnp.where((bounds == forced) | (present == 1), 1, 0) * (bounds > 0).astype(jnp.int32)
    offsets = jax.random.randint(key_offset, (BATCH, spans), -2, 3)
    marks = jnp.where(present == 1, bounds * TOK_DEV + offsets, -1)
    short_starts = (positions == 0) | jnp.any(positions[:, None, :] == marks[:, :, None], axis=1)
    starts = jnp.where(is_long, long_starts, short_starts)
    return starts.astype(jnp.int32)


def draw_resets(key, part):
    starts = draw_layout(key)
    return starts


def draw_real_mask(key, part):
    starts = draw_layout(key)
    key = jax.random.fold_in(key, 13)
    positions = jnp.arange(LENGTH, dtype=jnp.int32)[None, :]
    last = jnp.max(starts * positions, axis=1, keepdims=True)
    pad_from = last + 1 + jax.random.randint(key, (BATCH, 1), 0, LENGTH - last)
    return (positions < pad_from).astype(jnp.int32)


def shard_levels(rng, shape, cuts, least, high):
    level, own = 1.0, jax.random.fold_in(rng, 6)
    for axis_at, parts in cuts:
        steps = jnp.exp(jax.random.uniform(jax.random.fold_in(own, axis_at), (parts,), jnp.float32, least / len(cuts), high / len(cuts)))
        level = level * jnp.repeat(steps, shape[axis_at] // parts).reshape([-1 if axis == axis_at else 1 for axis in range(len(shape))])
    return level


def gaussian(rng, extent, scale, reach, pieces=(), kind=jnp.bfloat16):
    entries = jax.random.normal(rng, extent, jnp.float32) * scale
    if len(pieces) > 0:
        entries = shard_levels(rng, extent, pieces, -0.22, 0.18) * entries
    return jnp.clip(entries, min=-reach, max=reach).astype(kind)


def setup_inputs(seed: int = 0) -> dict:
    streams_of = jax.random.split(jax.random.key(seed), 17)
    return {
        "inputs": gaussian(streams_of[0], (BATCH, LENGTH, D), 1.0, 6.0, ((0, 4), (1, 8))),
        "cotangent": gaussian(streams_of[1], (BATCH, LENGTH, D), 1.0, 6.0, ((0, 4), (1, 8))),
        "resets": draw_resets(jax.random.fold_in(streams_of[16], 71), 0),
        "real_mask": draw_real_mask(jax.random.fold_in(streams_of[16], 71), 0),
        "gain_mix": jnp.clip(1.0 + 0.15 * jax.random.normal(streams_of[4], (D,), jnp.float32), 0.25, 1.75).astype(jnp.bfloat16),
        "w_branch_gate": gaussian(streams_of[5], (D, W), D ** -0.5, 0.125, ((0, 8), (1, 4))),
        "w_branch_x": gaussian(streams_of[6], (D, W), D ** -0.5, 0.125, ((0, 8), (1, 4))),
        "conv_kernel": gaussian(streams_of[7], (W, KERNEL), KERNEL ** -0.5, 3.0, ((0, 32),)),
        "gate_rate": gaussian(streams_of[8], (W, BLOCK), BLOCK ** -0.5, 0.5, ((0, 32),)),
        "gate_input": gaussian(streams_of[9], (W, BLOCK), BLOCK ** -0.5, 0.5, ((0, 32),)),
        "decay_param": jnp.clip(-10.375 + 6.484375 * jax.random.uniform(streams_of[10], (W,), jnp.float32) ** shard_levels(streams_of[10], (W,), ((0, 32),), -0.2, 0.2), -10.375, -3.890625).astype(jnp.bfloat16),
        "w_mix_out": gaussian(streams_of[11], (W, D), (W // 8) ** -0.5, 0.3125, ((0, 32),)),
        "gain_mlp": jnp.clip(1.0 + 0.15 * jax.random.normal(streams_of[12], (D,), jnp.float32), 0.25, 1.75).astype(jnp.bfloat16),
        "w_mlp_gate": gaussian(streams_of[13], (D, F), D ** -0.5, 0.125, ((0, 8), (1, 4))),
        "w_mlp_up": gaussian(streams_of[14], (D, F), D ** -0.5, 0.125, ((0, 8), (1, 4))),
        "w_mlp_down": gaussian(streams_of[15], (F, D), (F // 2) ** -0.5, 0.109375, ((0, 32),)),
    }


epsilon = 1e-06

@jax.custom_vjp
def low(v):
    return lax.optimization_barrier(v.astype(jnp.bfloat16)).astype(jnp.float32)

@jax.custom_vjp
def low_back(v):
    return v

def low_keep(v):
    return (low(v), None)

def low_pass(kept, grad):
    return (grad,)

def back_keep(v):
    return (v, None)

def back_low(kept, grad):
    return (low(grad),)
low.defvjp(low_keep, low_pass)
low_back.defvjp(back_keep, back_low)

def rms_norm(values, gain):
    return values * lax.rsqrt(lax.optimization_barrier(jnp.mean(values * values, axis=-1, keepdims=True)) + epsilon) * gain

def matmul(left, right):
    return jnp.dot(left, right, precision=lax.Precision.HIGHEST, preferred_element_type=jnp.float32)

def block_mix(values, gate):
    channels, block_size = gate.shape
    blocked = values.reshape(values.shape[:-1] + (channels // block_size, block_size))
    mixed_out = jnp.einsum('...ki,koi->...ko', blocked, gate.reshape(channels // block_size, block_size, block_size), precision=lax.Precision.HIGHEST)
    return mixed_out.reshape(values.shape)

def chain_combine(earlier, later):
    return (later[0] * earlier[0], later[0] * earlier[1] + later[1])

def conv_apply(padded, kernel, keep_mask):
    halo_width = kernel.shape[1] - 1
    length = keep_mask.shape[-1]
    keep_ext = jnp.concatenate([jnp.ones_like(keep_mask[..., :halo_width]), keep_mask], axis=-1)
    valid_mask = jnp.ones_like(keep_mask)
    summed = jnp.zeros(padded.shape[:-2] + (length, padded.shape[-1]), padded.dtype)
    for tap_index in range(kernel.shape[1]):
        offset = halo_width - tap_index
        window = lax.slice_in_dim(padded, offset, offset + length, axis=padded.ndim - 2)
        summed = summed + kernel[:, tap_index] * valid_mask[..., None] * window
        valid_mask = valid_mask * lax.slice_in_dim(keep_ext, offset, offset + length, axis=keep_mask.ndim - 1)
    return summed

def gate_values(conv_value, pre_rate, pre_inlet, decay, reset_values):
    log_rate = -8.0 * jax.nn.sigmoid(pre_rate) * jax.nn.softplus(decay)
    decay_rate = jnp.exp(log_rate)
    multiplier = reset_values + (1.0 - reset_values) * jnp.sqrt(-jnp.expm1(2.0 * log_rate))
    inflow = conv_value * jax.nn.sigmoid(pre_inlet) * multiplier
    return (decay_rate * (1.0 - reset_values), inflow, decay_rate)

def layer(values, gain_mix, w_branch_gate, w_branch_x, conv_kernel, gate_rate, gate_input, decay_param, w_mix_out, gain_mlp, w_mlp_gate, w_mlp_up, w_mlp_down, reset_values, real_values):
    keep_mask = 1.0 - reset_values[:, 0]
    mixer_in = low(rms_norm(values, gain_mix))
    pre_gate = low_back(matmul(mixer_in, w_branch_gate))
    branch = low(low_back(matmul(mixer_in, w_branch_x)))
    halo_width = conv_kernel.shape[1] - 1
    padded = jnp.concatenate([jnp.zeros((halo_width, branch.shape[1]), branch.dtype), branch], axis=0)
    conv_low = low(conv_apply(padded, conv_kernel, keep_mask))
    pre_rate = low_back(block_mix(conv_low, gate_rate))
    pre_inlet = low_back(block_mix(conv_low, gate_input))
    rate_kept, inflow, decay_rate = gate_values(conv_low, pre_rate, pre_inlet, decay_param, reset_values)
    _, states = lax.associative_scan(chain_combine, (rate_kept, inflow), axis=0)
    mixed_low = low(states * jax.nn.gelu(pre_gate))
    middle = values + low_back(matmul(mixed_low, w_mix_out))
    feed_in = low(rms_norm(middle, gain_mlp))
    pre_feed_gate = low_back(matmul(feed_in, w_mlp_gate))
    pre_up = low_back(matmul(feed_in, w_mlp_up))
    hidden = low(jax.nn.gelu(pre_feed_gate) * pre_up)
    result = (middle + low_back(matmul(hidden, w_mlp_down))) * real_values
    return (result, decay_rate)

def reference(inputs, cotangent, resets, real_mask, gain_mix, w_branch_gate, w_branch_x, conv_kernel, gate_rate, gate_input, decay_param, w_mix_out, gain_mlp, w_mlp_gate, w_mlp_up, w_mlp_down):
    params = tuple((weight.astype(jnp.float32) for weight in (gain_mix, w_branch_gate, w_branch_x, conv_kernel, gate_rate, gate_input, decay_param, w_mix_out, gain_mlp, w_mlp_gate, w_mlp_up, w_mlp_down)))

    def row_step(carried, row_data):
        grad_sums, decay_sum, real_count = carried
        row_inputs, row_cotangent, row_resets, row_real = row_data
        reset_values = row_resets.astype(jnp.float32)[:, None]
        real_values = row_real.astype(jnp.float32)[:, None]

        def forward(values, *weights):
            return layer(values, *weights, reset_values, real_values)
        result, row_pull, decay_rate = jax.vjp(forward, row_inputs.astype(jnp.float32), *params, has_aux=True)
        row_grads = row_pull(row_cotangent.astype(jnp.float32))
        grad_sums = tuple((total + piece for total, piece in zip(grad_sums, row_grads[1:])))
        decay_sum = decay_sum + lax.optimization_barrier(jnp.sum(decay_rate * real_values, axis=0))
        real_count = real_count + jnp.sum(real_values)
        return ((grad_sums, decay_sum, real_count), (result.astype(jnp.bfloat16), row_grads[0].astype(jnp.bfloat16)))
    start_sums = tuple((jnp.zeros_like(weight) for weight in params))
    start = (start_sums, jnp.zeros_like(params[6]), jnp.zeros((), jnp.float32))
    finals, outputs = lax.scan(row_step, start, (inputs, cotangent, resets, real_mask))
    grad_sums, decay_sum, real_count = finals
    return (outputs[0], outputs[1], grad_sums[0], grad_sums[1], grad_sums[2], grad_sums[3], grad_sums[4], grad_sums[5], grad_sums[6], grad_sums[7], grad_sums[8], grad_sums[9], grad_sums[10], grad_sums[11], decay_sum / real_count)
```

```python
from functools import partial

import jax
import jax.numpy as jnp
from jax import lax
from jax.experimental import pallas as pl
from jax.experimental.pallas import tpu as pltpu
from jax.sharding import PartitionSpec as P

epsilon = 1e-06
low = jnp.bfloat16
full = jnp.float32
CORES = 2


def ring_of(count):
    deep = 4 if count % 4 == 0 else 1
    wide = count // deep
    walk = [(z, 0) for z in range(deep)]
    for turn, z in enumerate(reversed(range(deep))):
        across = list(range(1, wide))
        walk += [(z, y) for y in (across if turn % 2 == 0 else across[::-1])]
    return [z * wide + y for z, y in walk]


def ring_hop(value, step):
    ring = ring_of(lax.axis_size("seq"))
    count = len(ring)
    return lax.ppermute(value, "seq", [(ring[i], ring[(i + step) % count]) for i in range(count)])


def ring_gather(value):
    count = lax.axis_size("seq")
    half = count // 2
    found = {0: value}
    ahead = behind = value
    for hop in range(1, half):
        behind = ring_hop(behind, 1)
        ahead = ring_hop(ahead, -1)
        found[-hop] = behind
        found[hop] = ahead
    cut = value.shape[0] // 2
    found[half] = jnp.concatenate([ring_hop(behind[:cut], 1), ring_hop(ahead[cut:], -1)], axis=0)
    return found


def ring_scatter(part):
    count = lax.axis_size("seq")
    half = count // 2
    far = part(half)
    cut = far.shape[0] // 2
    right = ring_hop(far[:cut].astype(low), 1).astype(full)
    left = ring_hop(far[cut:].astype(low), -1).astype(full)
    for hop in range(half - 1, 0, -1):
        one, two = part(hop).astype(full), part(-hop).astype(full)
        if hop == half - 1:
            one = jnp.concatenate([one[:cut] + right, one[cut:]], axis=0)
            two = jnp.concatenate([two[:cut], two[cut:] + left], axis=0)
        else:
            one, two = one + right, two + left
        right = ring_hop(one.astype(low), 1).astype(full)
        left = ring_hop(two.astype(low), -1).astype(full)
    return part(0).astype(full) + right + left


def ring_owner(offset):
    ring = ring_of(lax.axis_size("seq"))
    count = len(ring)
    place = [0] * count
    for position, index in enumerate(ring):
        place[index] = position
    mine = jnp.asarray(place, jnp.int32)[lax.axis_index("seq")]
    return jnp.asarray(ring, jnp.int32)[(mine + offset + count) % count]


def in_order(found):
    blocks = [found[offset] for offset in sorted(found)]
    size = blocks[0].shape[0]
    out = jnp.zeros((size * len(blocks),) + blocks[0].shape[1:], blocks[0].dtype)
    for offset in sorted(found):
        out = lax.dynamic_update_slice_in_dim(out, found[offset], ring_owner(offset) * size, 0)
    return out


def core_swap(value):
    count = lax.axis_size("dp")
    return lax.ppermute(value, "dp", [(i, i ^ 1) for i in range(count)])


def chip_shift(value, step):
    count = lax.axis_size("dp") // CORES
    return lax.ppermute(
        value,
        "dp",
        [
            (((x + step) % count) * CORES + core, x * CORES + core)
            for x in range(count)
            for core in range(CORES)
        ],
    )


def chips_gather(value):
    return [value] + [chip_shift(value, k) for k in range(1, lax.axis_size("dp") // CORES)]


def width_gather(value):
    same = chips_gather(value)
    return jnp.concatenate(same + [core_swap(block) for block in same], axis=0)


def chips_scatter(parts):
    total = parts[0].astype(full)
    for k in range(1, len(parts)):
        total = total + chip_shift(parts[k].astype(low), -k).astype(full)
    return total


def width_scatter(part, rows):
    count = lax.axis_size("dp") // CORES
    split = part.reshape((CORES, count * rows) + part.shape[1:])
    chip = split[0].astype(full) + core_swap(split[1].astype(low)).astype(full)
    return chips_scatter([chip[k * rows : (k + 1) * rows] for k in range(count)])


def shifted(value, axis, steps):
    count = lax.axis_size(axis)
    initial, last = (max(0, -steps), min(count, count - steps))
    return lax.ppermute(value, axis, [(source, source + steps) for source in range(initial, last)])


def carry_in(product, value, backward):
    count = lax.axis_size("seq")
    pair = jnp.stack([product, value])
    total, scale = jnp.zeros_like(value), jnp.ones_like(product)
    for k in range(1, count):
        theirs = shifted(pair, "seq", -k if backward else k)
        total = total + scale * theirs[1]
        scale = scale * theirs[0]
    return total


def scan_kernel(backward, rate_ref, value_ref, product_ref, state_ref):
    length, channels = rate_ref.shape[1:]
    groups = length // 8
    rate = rate_ref[0].reshape(groups, 8, channels)
    value = value_ref[0].reshape(groups, 8, channels)
    place = lax.broadcasted_iota(jnp.int32, rate.shape, 1)
    for step in (1, 2, 4):
        if backward:
            keep = place < 8 - step
            move = 8 - step
        else:
            keep = place >= step
            move = step
        earlier_rate = jnp.where(keep, pltpu.roll(rate, move, 1), 1.0)
        earlier_value = jnp.where(keep, pltpu.roll(value, move, 1), 0.0)
        value = value + rate * earlier_value
        rate = rate * earlier_rate
    product_in = jnp.ones((1, channels), full)
    state_in = jnp.zeros((1, channels), full)
    end = 0 if backward else 7
    for group in reversed(range(groups)) if backward else range(groups):
        product = rate[group] * product_in
        state = value[group] + rate[group] * state_in
        product_ref[0, group * 8 : group * 8 + 8, :] = product
        state_ref[0, group * 8 : group * 8 + 8, :] = state
        product_in, state_in = product[end : end + 1], state[end : end + 1]


def local_scan(rate, value, backward):
    rows, length, channels = rate.shape
    block = pl.BlockSpec((1, length, channels), lambda row: (row, 0, 0))
    return pl.pallas_call(
        partial(scan_kernel, backward),
        grid=(rows,),
        in_specs=[block, block],
        out_specs=[block, block],
        out_shape=[jax.ShapeDtypeStruct(rate.shape, full)] * 2,
        compiler_params=pltpu.CompilerParams(vmem_limit_bytes=32 << 20),
        cost_estimate=pl.CostEstimate(flops=30 * rate.size, bytes_accessed=16 * rate.size, transcendentals=0),
    )(rate, value)


def rms_norm(values, gain):
    return values * lax.rsqrt(jnp.mean(values * values, axis=-1, keepdims=True) + epsilon) * gain


def spread_blocks(gate):
    channels, size = gate.shape
    count = channels // size
    blocks = gate.reshape(count, size, size)
    return jnp.concatenate(
        [jnp.pad(blocks[k], ((0, 0), (k * size, channels - (k + 1) * size))) for k in range(count)], axis=0
    )


def gather_blocks(whole, size):
    channels = whole.shape[0]
    return jnp.concatenate(
        [whole[k * size : (k + 1) * size, k * size : (k + 1) * size] for k in range(channels // size)], axis=0
    )


def conv_apply(padded, kernel, keep_mask):
    halo_width = kernel.shape[1] - 1
    length = keep_mask.shape[-1]
    keep_ext = jnp.concatenate([jnp.ones_like(keep_mask[..., :halo_width]), keep_mask], axis=-1)
    valid_mask = jnp.ones_like(keep_mask)
    summed = jnp.zeros(padded.shape[:-2] + (length, padded.shape[-1]), padded.dtype)
    for tap_index in range(kernel.shape[1]):
        offset = halo_width - tap_index
        window = lax.slice_in_dim(padded, offset, offset + length, axis=padded.ndim - 2)
        summed = summed + kernel[:, tap_index] * valid_mask[..., None] * window
        valid_mask = valid_mask * lax.slice_in_dim(keep_ext, offset, offset + length, axis=keep_mask.ndim - 1)
    return summed


def gate_values(conv_value, pre_rate, pre_inlet, decay, reset_values):
    log_rate = -8.0 * jax.nn.sigmoid(pre_rate) * jax.nn.softplus(decay)
    decay_rate = jnp.exp(log_rate)
    multiplier = reset_values + (1.0 - reset_values) * jnp.sqrt(-jnp.expm1(2.0 * log_rate))
    inflow = conv_value * jax.nn.sigmoid(pre_inlet) * multiplier
    return (decay_rate * (1.0 - reset_values), inflow, decay_rate)


def gated_product(gate_pre, up_pre):
    return jax.nn.gelu(gate_pre) * up_pre


def dot(left, right, contract):
    return lax.dot_general(left, right, ((contract[0], contract[1]), ((), ())), preferred_element_type=full)


NN = ((1,), (0,))
NT = ((1,), (1,))
TN = ((0,), (0,))


def on_device(
    inputs,
    cotangent,
    resets,
    real_mask,
    gain_mix,
    w_branch_gate,
    w_branch_x,
    conv_kernel,
    gate_rate,
    gate_input,
    decay_param,
    w_mix_out,
    gain_mlp,
    w_mlp_gate,
    w_mlp_up,
    w_mlp_down,
):
    seq = lax.axis_size("seq")
    chips = lax.axis_size("dp") // CORES
    rows_own, length, depth = inputs.shape
    taps = conv_kernel.shape[1]
    halo_width = taps - 1
    block_size = gate_rate.shape[1]
    part_w = w_branch_x.shape[1]
    part_f = w_mlp_gate.shape[1]
    slice_f = part_f // seq

    marks = (resets + 2 * (1 - real_mask)).astype(low)
    values = width_gather(inputs).astype(full)
    mark_rows = width_gather(marks).astype(full)
    own_channels = gate_rate.shape[0]
    per_channel = jnp.concatenate([gate_rate, gate_input, conv_kernel, decay_param[:, None]], axis=1)
    small = per_channel.size
    shard = w_branch_x.shape[0]
    small_cols = -(-small // shard)
    packed = jnp.pad(per_channel.reshape(-1), (0, small_cols * shard - small)).reshape(shard, small_cols)
    extra = -(-(small_cols + 2) // 128) * 128
    packed = jnp.concatenate(
        [packed, gain_mix[:, None], gain_mlp[:, None], jnp.zeros((shard, extra - small_cols - 2), low)], axis=1
    )
    first = in_order(ring_gather(jnp.concatenate([w_branch_gate, w_branch_x, packed], axis=1)))
    w_branch = first[:, : 2 * part_w]
    packed_all = first[:, 2 * part_w :]
    gain_mix = packed_all[:, small_cols].astype(full)
    gain_mlp = packed_all[:, small_cols + 1].astype(full)
    per_channel = (
        packed_all[:, :small_cols].reshape(seq, -1)[:, :small].reshape(seq * own_channels, per_channel.shape[1])
    )
    gate_rate = spread_blocks(per_channel[:, :block_size])
    gate_input = spread_blocks(per_channel[:, block_size : 2 * block_size])
    conv_kernel = per_channel[:, 2 * block_size : 2 * block_size + taps]
    decay_param = per_channel[:, -1]
    w_mix_out = in_order(ring_gather(w_mix_out))

    def columns(weight):
        turned = lax.all_to_all(
            weight.reshape(shard, seq, slice_f), "seq", split_axis=1, concat_axis=0, tiled=True
        ).reshape(seq * shard, slice_f)
        return jnp.concatenate(chips_gather(turned), axis=1)

    w_gate_up = jnp.concatenate([columns(w_mlp_gate), columns(w_mlp_up)], axis=1)
    w_down = jnp.concatenate(chips_gather(w_mlp_down), axis=0)
    units = w_down.shape[0]

    real_own = real_mask.astype(full)[..., None]
    d_result_own = cotangent.astype(full) * real_own

    offsets = list(range(-(seq // 2 - 1), seq // 2 + 1))
    block = rows_own * length

    def plane_gather(value):
        found = ring_gather(value)
        return jnp.concatenate([each for offset in offsets for each in (found[offset], core_swap(found[offset]))])

    def plane_scatter(left, right):
        def part(offset):
            at = offsets.index(offset) * CORES * block
            both = dot(left[at : at + CORES * block], right[0], right[1])
            return both[:block] + core_swap(both[block:].astype(low)).astype(full)

        return ring_scatter(part)

    d_feed = plane_gather(d_result_own.reshape(-1, depth).astype(low))

    padding = jnp.where(mark_rows > 1.5, 1.0, 0.0)
    reset_float = mark_rows - 2.0 * padding
    keep_mask = 1.0 - reset_float
    reset_values = reset_float[..., None]
    real_values = (1.0 - padding)[..., None]
    rows = values.shape[0]
    tokens = rows * length
    normed_one, norm_one_pull = jax.vjp(rms_norm, values, gain_mix)
    mixer_in = normed_one.astype(low).reshape(tokens, depth)
    both = dot(mixer_in, w_branch, NN)
    pre_gate = both[:, :part_w].reshape(rows, length, part_w)
    branch = both[:, part_w:].astype(low).reshape(rows, length, part_w)
    factors = [jnp.ones_like(keep_mask[:, 0])]
    for shift_by in range(1, halo_width):
        factors.insert(0, factors[0] * keep_mask[:, length - shift_by])
    tail_keep = jnp.stack(factors, axis=1)[..., None]
    tail_rows = branch[:, length - halo_width :] * tail_keep.astype(low)
    prior_rows = shifted(tail_rows, "seq", 1)
    padded = jnp.concatenate([prior_rows, branch], axis=1).astype(full)
    conv_out, conv_pull = jax.vjp(partial(conv_apply, keep_mask=keep_mask), padded, conv_kernel.astype(full))
    conv_low = conv_out.astype(low)
    conv_flat = conv_low.reshape(tokens, part_w)
    pre_rate = dot(conv_flat, gate_rate, NT).reshape(rows, length, part_w)
    pre_inlet = dot(conv_flat, gate_input, NT).reshape(rows, length, part_w)
    (rate_kept, inflow, decay_rate), gate_pull = jax.vjp(
        partial(gate_values, reset_values=reset_values),
        conv_low.astype(full),
        pre_rate,
        pre_inlet,
        decay_param.astype(full),
    )
    cumulative, local_states = local_scan(rate_kept, inflow, False)
    state_in = carry_in(cumulative[:, -1], local_states[:, -1], False)
    states = local_states + cumulative * state_in[:, None]
    gate_branch, gelu_pull = jax.vjp(jax.nn.gelu, pre_gate)
    mixed_low = (states * gate_branch).astype(low).reshape(tokens, part_w)
    mix_part = dot(mixed_low, w_mix_out, NN)
    middle_own = inputs.astype(full) + width_scatter(mix_part.reshape(rows, length, depth), rows_own)

    feed_own, norm_two_pull = jax.vjp(rms_norm, middle_own, gain_mlp)
    feed_in = plane_gather(feed_own.astype(low).reshape(-1, depth))
    pre_both = dot(feed_in, w_gate_up, NN)
    hidden_value, act_pull = jax.vjp(gated_product, pre_both[:, :units], pre_both[:, units:])
    hidden = hidden_value.astype(low)
    d_hidden = dot(d_feed, w_down, NT)
    d_gate_value, d_up_value = act_pull(d_hidden)
    d_both = jnp.concatenate([d_gate_value.astype(low), d_up_value.astype(low)], axis=1)
    d_feed_own = plane_scatter(d_both, (w_gate_up, NT)).reshape(middle_own.shape)
    result_own = (middle_own + plane_scatter(hidden, (w_down, NN)).reshape(middle_own.shape)) * real_own
    output = result_own.astype(low)
    grad_both = dot(feed_in, d_both, TN)
    grad_down = dot(hidden, d_feed, TN)

    def columns_back(grad):
        mine = chips_scatter([grad[:, k * slice_f : (k + 1) * slice_f] for k in range(chips)])
        turned = lax.all_to_all(
            mine.astype(low).reshape(seq, shard, slice_f), "seq", split_axis=0, concat_axis=2, tiled=True
        )
        return turned.reshape(shard, part_f).astype(full)

    grad_feed_gate = columns_back(grad_both[:, :units])
    grad_feed_up = columns_back(grad_both[:, units:])
    down_rows = units // chips
    grad_down = chips_scatter([grad_down[k * down_rows : (k + 1) * down_rows] for k in range(chips)])

    d_middle_norm, gain_mlp_share = norm_two_pull(d_feed_own)
    d_middle_own = d_result_own + d_middle_norm
    d_mix = width_gather(d_middle_own.astype(low)).reshape(tokens, depth)
    d_mixed = dot(d_mix, w_mix_out, NT).reshape(rows, length, part_w)
    grad_mix_out = dot(mixed_low, d_mix, TN)
    d_states = d_mixed * gate_branch
    d_pre_gate = gelu_pull(d_mixed * states)[0].astype(low).reshape(tokens, part_w)
    next_rate = jnp.concatenate([rate_kept[:, 1:], jnp.ones_like(rate_kept[:, :1])], axis=1)
    later_product, local_adjoint = local_scan(next_rate, d_states, True)
    adjoint_in = carry_in(cumulative[:, -1], rate_kept[:, 0] * local_adjoint[:, 0], True)
    adjoint = local_adjoint + later_product * adjoint_in[:, None]
    previous = jnp.concatenate([state_in[:, None], states[:, :-1]], axis=1)
    d_conv_direct, d_rate_value, d_inlet_value, grad_decay = gate_pull(
        (adjoint * previous, adjoint, jnp.zeros_like(decay_rate))
    )
    d_rate = d_rate_value.astype(low).reshape(tokens, part_w)
    d_inlet = d_inlet_value.astype(low).reshape(tokens, part_w)
    grad_rate = gather_blocks(dot(d_rate, conv_flat, TN), block_size)
    grad_inlet = gather_blocks(dot(d_inlet, conv_flat, TN), block_size)
    d_conv = d_conv_direct + (dot(d_rate, gate_rate, NN) + dot(d_inlet, gate_input, NN)).reshape(
        d_conv_direct.shape
    )
    d_padded, grad_kernel = conv_pull(d_conv)
    d_tail = shifted(d_padded[:, :halo_width], "seq", -1)
    d_branch_value = jnp.concatenate(
        [d_padded[:, halo_width:length], d_padded[:, length:] + d_tail * tail_keep], axis=1
    )
    d_branch = d_branch_value.astype(low).reshape(tokens, part_w)
    d_branches = jnp.concatenate([d_pre_gate, d_branch], axis=1)
    grad_branches = dot(mixer_in, d_branches, TN)
    d_mixer_part = dot(d_branches, w_branch, NT).reshape(rows, length, depth)
    d_values_part, gain_mix_part = norm_one_pull(d_mixer_part)
    d_values_own = width_scatter(d_values_part, rows_own)
    grad_inputs = (d_middle_own + d_values_own).astype(low)

    decay_total = jnp.sum(decay_rate * real_values, axis=(0, 1))
    real_count = jnp.sum(real_values)

    def pick(value):
        size = value.shape[0] // seq
        return lambda offset: lax.dynamic_slice_in_dim(value, ring_owner(offset) * size, size, 0)

    grad_branches = ring_scatter(pick(grad_branches))
    grad_mix_out = ring_scatter(pick(grad_mix_out))
    channel_grads = lax.psum_scatter(
        jnp.concatenate([grad_rate, grad_inlet, grad_kernel, grad_decay[:, None], decay_total[:, None]], axis=1),
        "seq",
        scatter_dimension=0,
        tiled=True,
    )
    gains = lax.psum_scatter(
        jnp.stack([gain_mix_part, gain_mlp_share], axis=1), ("dp", "seq"), scatter_dimension=0, tiled=True
    )
    count_all = lax.psum(real_count, "seq")
    return (
        output,
        grad_inputs,
        gains[:, 0],
        grad_branches[:, :part_w],
        grad_branches[:, part_w:],
        channel_grads[:, 2 * block_size : 2 * block_size + taps],
        channel_grads[:, :block_size],
        channel_grads[:, block_size : 2 * block_size],
        channel_grads[:, 2 * block_size + taps],
        grad_mix_out,
        gains[:, 1],
        grad_feed_gate,
        grad_feed_up,
        grad_down,
        channel_grads[:, 2 * block_size + taps + 1] / count_all,
    )


def solution(mesh):
    placed = (
        P("dp", "seq", None),
        P("dp", "seq", None),
        P("dp", "seq"),
        P("dp", "seq"),
        P("seq"),
        P("seq", "dp"),
        P("seq", "dp"),
        P(("dp", "seq"), None),
        P(("dp", "seq"), None),
        P(("dp", "seq"), None),
        P(("dp", "seq")),
        P(("dp", "seq"), None),
        P("seq"),
        P("seq", "dp"),
        P("seq", "dp"),
        P(("dp", "seq"), None),
    )
    return jax.shard_map(
        on_device,
        mesh=mesh,
        in_specs=placed,
        out_specs=(
            P("dp", "seq", None),
            P("dp", "seq", None),
            P(("dp", "seq")),
            P("seq", "dp"),
            P("seq", "dp"),
            P(("dp", "seq"), None),
            P(("dp", "seq"), None),
            P(("dp", "seq"), None),
            P(("dp", "seq")),
            P(("dp", "seq"), None),
            P(("dp", "seq")),
            P("seq", "dp"),
            P("seq", "dp"),
            P(("dp", "seq"), None),
            P(("dp", "seq")),
        ),
        check_vma=False,
    )
```

```python
from functools import partial

import jax
import jax.numpy as jnp
from jax import lax
from jax.experimental import pallas as pl
from jax.experimental.pallas import tpu as pltpu
from jax.sharding import PartitionSpec as P

epsilon = 1e-06
low = jnp.bfloat16
full = jnp.float32
CORES = 2


def ring_of(count):
    deep = 4 if count % 4 == 0 else 1
    wide = count // deep
    walk = [(z, 0) for z in range(deep)]
    for turn, z in enumerate(reversed(range(deep))):
        across = list(range(1, wide))
        walk += [(z, y) for y in (across if turn % 2 == 0 else across[::-1])]
    return [z * wide + y for z, y in walk]


NT = ((1,), (1,))
TN = ((0,), (0,))


MESH = pl.DeviceIdType.MESH


def pick_from(table, index):
    found = table[0]
    for at in range(1, len(table)):
        found = jnp.where(index == at, table[at], found)
    return found


def ring_sides(count):
    ring = ring_of(count)
    place = {index: position for position, index in enumerate(ring)}
    mine = lax.axis_index("seq")
    after = pick_from([ring[(place[index] + 1) % count] for index in range(count)], mine)
    before = pick_from([ring[(place[index] - 1) % count] for index in range(count)], mine)
    return {"seq": after}, {"seq": before}


def core_mate():
    mine = lax.axis_index("dp")
    return {"dp": mine + 1 - 2 * lax.rem(mine, 2)}


def greet(*devices):
    barrier = pltpu.get_barrier_semaphore()
    for device in devices:
        pl.semaphore_signal(barrier, inc=1, device_id=device, device_id_type=MESH)
    pl.semaphore_wait(barrier, len(devices))


def send(source, target, sems, device):
    return pltpu.make_async_remote_copy(
        src_ref=source, dst_ref=target, send_sem=sems[0], recv_sem=sems[1], device_id=device, device_id_type=MESH
    )


def gelu_and_slope(value):
    scale = 0.7978845608028654
    square = value * value
    bent = jnp.tanh(scale * value * (1.0 + 0.044715 * square))
    half = 0.5 * (1.0 + bent)
    slope = half + 0.5 * value * (1.0 - bent * bent) * (scale * (1.0 + 3.0 * 0.044715 * square))
    return value * half, slope


def ring_index(count, offset):
    ring = ring_of(count)
    place = {index: position for position, index in enumerate(ring)}
    mine = lax.axis_index("seq")
    return pick_from([ring[(place[index] + offset) % count] for index in range(count)], mine)


def chip_mates(width, ahead=False):
    chips = width // CORES
    mine = lax.axis_index("dp")
    return [{"dp": lax.rem(mine + (k if ahead else chips - k) * CORES, width)} for k in range(1, chips)]


class RingSum:
    def __init__(self, count, refs, sems, after, before, mate):
        self.half, self.far = count // 2, count - 1
        self.stash, self.core_out, self.core_in, self.right_in, self.left_in = refs
        self.core_sems, self.right_sems, self.left_sems = sems[0:2], sems[2:4], sems[4:6]
        self.after, self.before, self.mate = after, before, mate
        self.held = self.core_out.shape[0]
        self.block = self.stash.shape[1]
        self.cut = self.block // 2

    @staticmethod
    def scratch(count, block, depth):
        half = count // 2
        dma = pltpu.SemaphoreType.DMA
        return [
            pltpu.VMEM((count, block, depth), low),
            pltpu.VMEM((4, block, depth), low),
            pltpu.VMEM((count, block, depth), low),
            pltpu.VMEM((half, block, depth), low),
            pltpu.VMEM((half, block, depth), low),
            dma((4,)), dma((count,)), dma((half,)), dma((half,)), dma((half,)), dma((half,)),
        ]

    def core_copy(self, slot):
        place = slot % self.held
        sems = (self.core_sems[0].at[place], self.core_sems[1].at[slot])
        return send(self.core_out.at[place], self.core_in.at[slot], sems, self.mate)

    def side_copy(self, way, slot, step):
        target, sems = ((self.right_in, self.right_sems), (self.left_in, self.left_sems))[way]
        sems = (sems[0].at[step], sems[1].at[step])
        return send(self.stash.at[slot], target.at[step], sems, (self.after, self.before)[way])

    def far_copy(self, way):
        rows = pl.ds(way * self.cut, self.cut)
        target, sems = ((self.right_in, self.right_sems), (self.left_in, self.left_sems))[way]
        sems = (sems[0].at[0], sems[1].at[0])
        return send(self.stash.at[self.far, rows], target.at[0, rows], sems, (self.after, self.before)[way])

    def offer(self, slot, part, again):
        part = part.astype(low)
        self.stash[slot] = part[: self.block]

        @pl.when(again)
        def _():
            self.core_copy(slot).wait_send()

        self.core_out[slot % self.held] = part[self.block :]
        self.core_copy(slot).start()

    def pair(self, slot):
        self.core_copy(slot).wait_recv()
        return self.stash[slot].astype(full) + self.core_in[slot].astype(full)

    def begin(self):
        self.stash[self.far] = self.pair(self.far).astype(low)
        self.far_copy(0).start()
        self.far_copy(1).start()

    def step(self, step):
        one = 2 * (self.half - step)
        for way, slot, arrived in ((0, one, self.right_in), (1, one - 1, self.left_in)):
            mine = self.pair(slot)
            if step == 1:
                rows = slice(0, self.cut) if way == 0 else slice(self.cut, self.block)
                self.stash[slot] = mine.astype(low)
                self.far_copy(way).wait_recv()
                self.stash[slot, rows] = (mine[rows] + arrived[0, rows].astype(full)).astype(low)
            else:
                self.side_copy(way, slot, step - 1).wait_recv()
                self.stash[slot] = (mine + arrived[step - 1].astype(full)).astype(low)
            self.side_copy(way, slot, step).start()

    def finish(self):
        mine = self.pair(0)
        last = self.half - 1
        self.side_copy(0, 0, last).wait_recv()
        self.side_copy(1, 0, last).wait_recv()
        return mine + self.right_in[last].astype(full) + self.left_in[last].astype(full)

    def drain(self):
        for slot in range(self.held):
            self.core_copy(slot).wait_send()
        for way in range(2):
            self.far_copy(way).wait_send()
            for step in range(1, self.half):
                self.side_copy(way, 0, step).wait_send()


class RingGather:
    def __init__(self, count, own, found, sems, after, before, mate, keep_sem=None):
        self.half, self.far = count // 2, count - 1
        self.own, self.found, self.sems, self.keep_sem = own, found, sems, keep_sem
        self.after, self.before, self.mate = after, before, mate
        self.cut = own.shape[0] // 2

    @staticmethod
    def scratch(count):
        dma = pltpu.SemaphoreType.DMA
        return [dma((count,)), dma((count,)), dma((2,)), dma((2,)), dma((count,)), dma((count,))]

    def onward(self, slot, to):
        source = self.own if slot is None else self.found.at[slot, 0]
        sems = (self.sems[0].at[to], self.sems[1].at[to])
        return send(source, self.found.at[to, 0], sems, self.after if to % 2 else self.before)

    def far_half(self, slot, way):
        rows = pl.ds(way * self.cut, self.cut)
        sems = (self.sems[2].at[way], self.sems[3].at[way])
        source, target = self.found.at[slot, 0, rows], self.found.at[self.far, 0, rows]
        return send(source, target, sems, (self.after, self.before)[way])

    def to_mate(self, slot):
        sems = (self.sems[4].at[slot], self.sems[5].at[slot])
        source = self.own if isinstance(slot, int) and slot == 0 else self.found.at[slot, 0]
        return send(source, self.found.at[slot, 1], sems, self.mate)

    def start(self):
        self.onward(None, 1).start()
        self.onward(None, 2).start()
        self.to_mate(0).start()
        if self.keep_sem is None:
            self.found[0, 0] = self.own[...]
        else:
            self.keep().start()

    def keep(self):
        return pltpu.make_async_copy(self.own, self.found.at[0, 0], self.keep_sem)

    def hop(self, h):
        for way, slot in ((0, 2 * h - 1), (1, 2 * h)):
            self.onward(slot, slot).wait_recv()
            if h < self.half - 1:
                self.onward(slot, slot + 2).start()
            else:
                self.far_half(slot, way).start()
            self.to_mate(slot).start()

    def last(self):
        self.far_half(self.far, 0).wait_recv()
        self.far_half(self.far, 1).wait_recv()
        self.to_mate(self.far).start()

    def drain(self):
        for slot in range(self.far + 1):
            self.to_mate(slot).wait_send()
        for slot in range(1, self.far):
            self.onward(0, slot).wait_send()
        self.far_half(0, 0).wait_send()
        self.far_half(0, 1).wait_send()
        if self.keep_sem is not None:
            self.keep().wait()


class RingTurn:
    def __init__(self, count, source, target, transit, sems, after, before):
        self.count, self.half = count, count // 2
        self.source, self.target, self.transit, self.sems = source, target, transit, sems
        self.after, self.before = after, before
        self.cut = source.shape[1] // 2

    @staticmethod
    def scratch(count, rows, columns):
        half = count // 2
        dma = pltpu.SemaphoreType.DMA
        return [
            pltpu.VMEM((2, half * (half - 1) // 2, rows, columns), low),
            dma((2, half * (half + 1) // 2)),
            dma((2, half * (half + 1) // 2)),
        ]

    def copy(self, way, hop, away):
        sign = 1 - 2 * way
        number = sum(range(hop)) if hop == 0 else sum(self.half - j + 1 for j in range(1, hop)) + away - hop
        if hop == 1:
            source = self.source.at[ring_index(self.count, sign * away)]
        else:
            source = self.transit.at[way, sum(self.half - j for j in range(1, hop - 1)) + away - hop]
        if away == hop:
            target = self.target.at[ring_index(self.count, sign * (1 - hop))]
        else:
            target = self.transit.at[way, sum(self.half - j for j in range(1, hop)) + away - hop - 1]
        if away == self.half:
            rows = pl.ds(way * self.cut, self.cut)
            source, target = source.at[rows], target.at[rows]
        sems = (self.sems[0].at[way, number], self.sems[1].at[way, number])
        return send(source, target, sems, (self.after, self.before)[way])

    def start(self):
        for away in range(self.half, 0, -1):
            for way in range(2):
                self.copy(way, 1, away).start()

    def hop(self, hop):
        for away in range(self.half, hop - 1, -1):
            for way in range(2):
                self.copy(way, hop, away).wait_recv()
                if away > hop:
                    self.copy(way, hop + 1, away).start()

    def drain(self):
        for hop in range(1, self.half + 1):
            for away in range(hop, self.half + 1):
                for way in range(2):
                    self.copy(way, hop, away).wait_send()


class RingScatter:
    def __init__(self, count, items, sems, after, before):
        self.count, self.half = count, count // 2
        self.items, self.sems = items, sems
        self.after, self.before = after, before

    @staticmethod
    def scratch(count, shapes):
        half = count // 2
        dma = pltpu.SemaphoreType.DMA
        arrived = [pltpu.VMEM((2, half) + shape, kind) for shape, kind in shapes]
        leaving = [pltpu.VMEM((2, 2) + shape, kind) for shape, kind in shapes]
        return arrived + leaving + [dma((len(shapes), 2, half)), dma((len(shapes), 2, half))]

    def columns(self, item, way):
        _, arrived, _, ways = self.items[item]
        wide = arrived.shape[-1]
        return pl.ds(way * (wide // 2), wide // 2) if len(ways) == 2 else pl.ds(0, wide)

    def copy(self, item, way, step):
        _, arrived, leaving, _ = self.items[item]
        source, target = leaving.at[way, step % 2], arrived.at[way, step]
        if step == 0:
            columns = self.columns(item, way)
            source, target = source.at[:, columns], target.at[:, columns]
        sems = (self.sems[0].at[item, way, step], self.sems[1].at[item, way, step])
        return send(source, target, sems, (self.after, self.before)[way])

    def begin(self):
        index = ring_index(self.count, self.half)
        for item, (value, _, leaving, ways) in enumerate(self.items):
            far = value(index).astype(leaving.dtype)
            for way in ways:
                leaving[way, 0] = far
                self.copy(item, way, 0).start()

    def onward(self, step):
        for item, (value, arrived, leaving, ways) in enumerate(self.items):
            for way in range(2):
                offset = self.half - step
                mine = value(ring_index(self.count, offset if way == 0 else -offset))
                if step > 1:
                    self.copy(item, way, step - 1).wait_recv()
                    mine = mine + arrived[way, step - 1].astype(full)
                if step > 2 or (step == 2 and way in ways):
                    self.copy(item, way, step - 2).wait_send()
                leaving[way, step % 2] = mine.astype(leaving.dtype)
                if step == 1 and way in ways:
                    self.copy(item, way, 0).wait_recv()
                    columns = self.columns(item, way)
                    leaving[way, 1, :, columns] = (
                        leaving[way, 1, :, columns].astype(full) + arrived[way, 0, :, columns].astype(full)
                    ).astype(leaving.dtype)
                self.copy(item, way, step).start()

    def finish(self, item):
        value, arrived, _, _ = self.items[item]
        total = value(lax.axis_index("seq"))
        for way in range(2):
            self.copy(item, way, self.half - 1).wait_recv()
            total = total + arrived[way, self.half - 1].astype(full)
        return total

    def drain(self):
        for item, (_, _, _, ways) in enumerate(self.items):
            for way in range(2):
                for step in range(self.half - 2, self.half):
                    if step > 0 or way in ways:
                        self.copy(item, way, step).wait_send()


def feed_kernel(
    count, width, own, w_both, w_down, cotangent, hidden, total, feed_sum, down_own, down_others, feed, d_both,
    cot_rows, down_total, feed_others, feed_in, cot_sem, cross_out, cross_in, *rest
):
    gather_sems, rest = rest[:6], rest[6:]
    ring_refs, ring_sems = rest[:5], rest[5:]
    half, chips = count // 2, width // CORES
    far = count - 1
    block, depth = own.shape
    units = w_down.shape[0]
    slice_f = units // chips
    tokens = count * 2 * block
    after, before = ring_sides(count)
    mate = core_mate()
    back, ahead = chip_mates(width), chip_mates(width, True)
    greet(after, before, mate, *back)
    gather = RingGather(count, own, feed, gather_sems, after, before, mate)
    ring = RingSum(count, ring_refs, ring_sems, after, before, mate)

    def cross(k):
        sems = (cross_out.at[k], cross_in.at[k])
        return send(feed_others.at[k - 1], feed_in.at[k - 1], sems, ahead[k - 1])

    def fetch(slot):
        return pltpu.make_async_copy(cotangent.at[slot], cot_rows.at[slot % 2], cot_sem.at[slot % 2])

    def fetched(slot):
        fetch(slot).wait()

        @pl.when(slot < far)
        def _():
            fetch(slot + 1).start()

        return cot_rows[slot % 2].reshape(2 * block, depth)

    def work(slot):
        back_all = lax.dot_general(fetched(slot), w_down[...], (NT, ((), ())), preferred_element_type=full)
        gather.to_mate(slot).wait_recv()
        rows = feed[slot].reshape(2 * block, depth)
        before_act = jnp.dot(rows, w_both[...], preferred_element_type=full)
        forth, back_parts = [], []
        for k in range(chips):
            start = 2 * k * slice_f
            gate, up = before_act[:, start : start + slice_f], before_act[:, start + slice_f : start + 2 * slice_f]
            active, slope = gelu_and_slope(gate)
            back = back_all[:, k * slice_f : (k + 1) * slice_f]
            forth.append(active * up)
            back_parts += [back * up * slope, back * active]
        hidden[slot] = jnp.concatenate(forth, axis=1).astype(low).reshape(2, block, units)
        d_rows = jnp.concatenate(back_parts, axis=1).astype(low)
        for k in range(chips):
            d_both[k, slot] = d_rows[:, 2 * k * slice_f : 2 * (k + 1) * slice_f].reshape(2, block, 2 * slice_f)
        part = lax.dot_general(d_rows, w_both[...], (NT, ((), ())), preferred_element_type=full)
        ring.offer(slot, part, slot >= ring.held)

    fetch(0).start()
    gather.start()
    gather.hop(1)
    work(0)
    for h in range(2, half):
        gather.hop(h)
        pl.loop(2 * h - 3, 2 * h - 1)(work)
    pl.loop(2 * half - 3, 2 * half - 1)(work)
    gather.last()
    work(far)

    pieces = 4
    wide = depth // pieces

    def grads(first, last):
        @pl.loop(first, last)
        def _(at):
            columns = pl.ds(pl.multiple_of((at % pieces) * wide, wide), wide)
            k = chips - 1 - at // pieces
            part = lax.dot_general(
                feed[:, :, :, columns].reshape(tokens, wide),
                d_both[k].reshape(tokens, 2 * slice_f),
                (TN, ((), ())),
                preferred_element_type=full,
            ).astype(low)

            @pl.when(k == 0)
            def _():
                feed_sum[columns] = part

            @pl.when(k > 0)
            def _():
                feed_others[jnp.maximum(k - 1, 0), columns] = part

    def down(slot):
        rows = fetched(slot)
        part = lax.dot_general(
            hidden[slot].reshape(2 * block, units), rows, (TN, ((), ())), preferred_element_type=full
        )

        @pl.when(slot == 0)
        def _():
            down_total[...] = part

        @pl.when(slot > 0)
        def _():
            down_total[...] += part

    fetch(0).start()
    ring.begin()
    grads(0, (chips - 1) * pieces)
    for k in range(1, chips):
        cross(k).start()
    ring.step(1)
    grads((chips - 1) * pieces, chips * pieces)
    if half > 2:
        ring.step(2)
    pl.loop(0, count // 2)(down)
    for step in range(3, half):
        ring.step(step)
    pl.loop(count // 2, count)(down)
    down_own[...] = down_total[:slice_f].astype(low)
    for k in range(1, chips):
        down_others[k - 1] = down_total[k * slice_f : (k + 1) * slice_f].astype(low)
    total[...] = ring.finish()
    for k in range(1, chips):
        cross(k).wait_recv()
    for at in range(pieces):
        rows = slice(at * wide, (at + 1) * wide)
        part = feed_sum[rows].astype(full)
        for k in range(1, chips):
            part = part + feed_in[k - 1, rows].astype(full)
        feed_sum[rows] = part.astype(low)
    gather.drain()
    ring.drain()
    for k in range(1, chips):
        cross(k).wait_send()


def feed_forward(own, w_both, w_down, cotangent):
    count, width = lax.axis_size("seq"), lax.axis_size("dp")
    chips = width // CORES
    block, depth = own.shape
    units = w_down.shape[0]
    slice_f = units // chips
    whole = pl.BlockSpec(memory_space=pltpu.VMEM)
    dma = pltpu.SemaphoreType.DMA
    shapes = [
        ((count, 2, block, units), low), ((block, depth), full), ((depth, 2 * slice_f), low),
        ((slice_f, depth), low), ((chips - 1, slice_f, depth), low),
    ]
    return pl.pallas_call(
        partial(feed_kernel, count, width),
        in_specs=[whole] * 3 + [pl.BlockSpec(memory_space=pl.ANY)],
        out_specs=[whole] * len(shapes),
        out_shape=[jax.ShapeDtypeStruct(*shape) for shape in shapes],
        scratch_shapes=[
            pltpu.VMEM((count, 2, block, depth), low),
            pltpu.VMEM((chips, count, 2, block, 2 * slice_f), low),
            pltpu.VMEM((2, 2, block, depth), low),
            pltpu.VMEM((units, depth), full),
            pltpu.VMEM((chips - 1, depth, 2 * slice_f), low),
            pltpu.VMEM((chips - 1, depth, 2 * slice_f), low),
            dma((2,)), dma((chips,)), dma((chips,)),
            *RingGather.scratch(count),
            *RingSum.scratch(count, block, depth),
        ],
        compiler_params=pltpu.CompilerParams(collective_id=1, has_side_effects=True, vmem_limit_bytes=63 << 20),
        cost_estimate=pl.CostEstimate(
            flops=2 * 2 * count * block * depth * units * 9, bytes_accessed=40 << 20, transcendentals=0
        ),
    )(own, w_both, w_down, cotangent)


def seq_peer(count, step):
    place = lax.rem(lax.axis_index("seq") + (step + count), count)
    return {"seq": place}, place


def keep_column(marks, row):
    mark = jnp.broadcast_to(marks[row, :1], marks.shape[1:])
    padding = jnp.where(mark > 1.5, 1.0, 0.0)
    keep = 1.0 - (mark - 2.0 * padding)
    return jnp.transpose(keep)[:, :1], jnp.transpose(1.0 - padding)[:, :1]


def gate_terms(pre_rate, pre_inlet, soft):
    rate, inlet = jax.nn.sigmoid(pre_rate), jax.nn.sigmoid(pre_inlet)
    twice = -16.0 * rate * soft
    decay = jnp.exp(0.5 * twice)
    near = -twice * (
        1.0 + twice * (1 / 2 + twice * (1 / 6 + twice * (1 / 24 + twice * (1 / 120 + twice * (1 / 720)))))
    )
    rest = jnp.where(twice > -0.25, near, 1.0 - decay * decay)
    return rate, inlet, decay, rest, jnp.sqrt(rest)


def scan_rows(rate, value, backward):
    length, channels = rate.shape
    groups = length // 8
    rate = rate.reshape(groups, 8, channels)
    value = value.reshape(groups, 8, channels)
    place = lax.broadcasted_iota(jnp.int32, rate.shape, 1)
    for step in (1, 2, 4):
        keep = place < 8 - step if backward else place >= step
        move = 8 - step if backward else step
        earlier_rate = jnp.where(keep, pltpu.roll(rate, move, 1), 1.0)
        earlier_value = jnp.where(keep, pltpu.roll(value, move, 1), 0.0)
        value = value + rate * earlier_value
        rate = rate * earlier_rate
    product_in = jnp.ones((1, channels), full)
    state_in = jnp.zeros((1, channels), full)
    end = 0 if backward else 7
    products, states = [None] * groups, [None] * groups
    for group in reversed(range(groups)) if backward else range(groups):
        states[group] = value[group] + rate[group] * state_in
        products[group] = rate[group] * product_in
        product_in, state_in = products[group][end : end + 1], states[group][end : end + 1]
    return jnp.concatenate(products, axis=0), jnp.concatenate(states, axis=0)


def fold_states(count, arrived, backward):
    mine = lax.axis_index("seq")
    total = jnp.zeros(arrived.shape[2:], full)
    scale = jnp.ones(arrived.shape[2:], full)
    for step in range(1, count):
        there = (mine + step < count) if backward else (mine >= step)
        total = total + jnp.where(there, scale * arrived[step, 1], 0.0)
        scale = scale * arrived[step, 0]
    return total


def stack_rows(ref):
    pieces, rows, columns = ref.shape
    if rows % 16 == 0:
        return ref[...].reshape(pieces * rows, columns)
    return jnp.concatenate([ref[piece].astype(full) for piece in range(pieces)], axis=0).astype(ref.dtype)


def tail_factor(column, taps):
    length = column.shape[0]
    place = lax.broadcasted_iota(jnp.int32, (8, 1), 0)
    factor, run = jnp.where(place == 7, 1.0, 0.0), jnp.ones((1, 1), full)
    for back in range(1, taps - 1):
        run = run * column[length - back : length - back + 1]
        factor = jnp.where(place == 7 - back, run, factor)
    return factor


def front_kernel(
    count, width, own, cot_raw, resets, real_mask, gain_mix, gain_mlp, conv_kernel, decay_param, gate_rate, gate_input,
    w_gate, w_x, w_mix, w_feed_gate, w_feed_up, w_down,
    marks_all, w_both, gains, chan, cotangent, middle, feed_own, halo, ends, cot_all, down_all,
    gate_far, x_far, normed_far, pre_gate_far, branch_far, w_mix_far, conv_far, pre_rate_far, pre_inlet_far, rate_far,
    inlet_far, states_far, mixed_far,
    gate_all, x_all, normed, pre_gate, branch, w_mix_all, conv_low, pre_rate, pre_inlet, rate_mat, inlet_mat, states,
    mixed, save_sem, own_marks, small, small_all, own_gates, gates_all, mix_all, rows_all, x_total, scale, turned, arrived,
    keep, product, state, ext, halo_out, halo_in, state_out, state_all, core_out, core_in, chip_out, chip_in,
    ring_out, ring_in, last_out, last_in, rows_out, rows_in, mate_out, mate_in, cross_out, cross_in, down_out, down_in,
    halo_sem, state_out_sem, state_in_sem, core_out_sem, core_in_sem, chip_out_sem, chip_in_sem, cot_sem, *rest
):
    gather_sems, turn_refs = rest[:6], rest[6:]
    half = count // 2
    chips = width // CORES
    block, depth = own.shape
    shard, channels = w_gate.shape
    own_channels, size = gate_rate.shape
    taps = conv_kernel.shape[1]
    slice_f = w_down.shape[0]
    mine = lax.axis_index("seq")
    after, before = ring_sides(count)
    mate = core_mate()
    back, ahead = chip_mates(width), chip_mates(width, True)
    peers = [None] + [seq_peer(count, step)[0] for step in range(1, count)]
    greet(mate, *back, *peers[1:])
    gather = RingGather(count, cotangent, cot_all, gather_sems, after, before, mate, cot_sem.at[0])
    turn = RingTurn(count, turned, arrived.at[0], turn_refs[0], turn_refs[1:], after, before)
    saves = [
        pltpu.make_async_copy(source, target, save_sem.at[at])
        for at, (source, target) in enumerate(
            (
                (gate_all, gate_far), (x_all, x_far), (normed, normed_far), (pre_gate, pre_gate_far),
                (branch, branch_far), (w_mix_all, w_mix_far), (conv_low, conv_far), (pre_rate, pre_rate_far),
                (pre_inlet, pre_inlet_far), (rate_mat, rate_far), (inlet_mat, inlet_far), (states, states_far),
                (mixed, mixed_far), (w_down, down_all.at[0]),
            )
        )
    ]
    moved = ((w_gate, gate_all), (small, small_all), (w_x, x_all), (own_gates, gates_all), (w_mix, mix_all))
    shared = ((0,), (0,), (1,), (1,), (0, 1))

    def rows_copy(what, k):
        source, target = ((own, rows_all), (own_marks, marks_all))[what]
        return send(source, target.at[k], (rows_out.at[what, k], rows_in.at[what, k]), back[k - 1])

    def mate_copy(what, k):
        source, target = ((own, rows_all), (own_marks, marks_all))[what]
        source = source if k == 0 else target.at[k]
        return send(source, target.at[chips + k], (mate_out.at[what, k], mate_in.at[what, k]), mate)

    def ring_copy(way, hop, item):
        source, target = moved[item]
        index = mine if hop == 1 else ring_index(count, (1 - hop) if way == 0 else (hop - 1))
        return send(
            source if hop == 1 else target.at[index],
            target.at[index],
            (ring_out.at[way, hop, item], ring_in.at[way, hop, item]),
            after if way == 0 else before,
        )

    def last_copy(way, item):
        index = ring_index(count, (1 - half) if way == 0 else (half - 1))
        ref = moved[item][1].at[index]
        if len(shared[item]) == 2:
            ref = ref.at[:, pl.ds(way * (depth // 2), depth // 2)]
        return send(ref, ref, (last_out.at[way, item], last_in.at[way, item]), after if way == 0 else before)

    def cross(slot, k):
        offset = half if slot == count - 1 else (slot + 1) // 2 * (1 - 2 * (slot % 2))
        origin = ring_index(count, offset)
        sems = (cross_out.at[k, slot], cross_in.at[k, slot])
        return send(arrived.at[0, origin], arrived.at[k, origin], sems, back[k - 1])

    def cross_down(k):
        return send(w_down, down_all.at[k], (down_out.at[k], down_in.at[k]), back[k - 1])

    def halo_copy():
        return send(halo_out, halo_in, (halo_sem.at[0], halo_sem.at[1]), peers[1])

    def state_copy(step):
        return send(state_out, state_all.at[step], (state_out_sem.at[step], state_in_sem.at[step]), peers[step])

    def core_copy(k):
        return send(core_out.at[k], core_in.at[k], (core_out_sem.at[k], core_in_sem.at[k]), mate)

    def chip_copy(k):
        return send(chip_out.at[k], chip_in.at[k], (chip_out_sem.at[k], chip_in_sem.at[k]), ahead[k - 1])

    def send_item(item):
        ring_copy(0, 1, item).start()
        ring_copy(1, 1, item).start()
        moved[item][1][mine] = moved[item][0][...]

    send_item(0)
    mate_copy(0, 0).start()
    for k in range(1, chips):
        rows_copy(0, k).start()
    real = real_mask[...].astype(full)
    own_marks[...] = jnp.broadcast_to(resets[...].astype(full) + 2.0 * (1.0 - real), own_marks.shape)
    mate_copy(1, 0).start()
    for k in range(1, chips):
        rows_copy(1, k).start()
    turned_taps = jnp.transpose(conv_kernel[...].astype(full))
    padding = jnp.zeros((1, shard - own_channels), full)
    pieces = [jnp.concatenate([turned_taps[tap : tap + 1], padding], axis=1) for tap in range(taps)]
    pieces.append(jnp.concatenate([decay_param[...].astype(full), padding], axis=1))
    pieces += [gain_mix[...].astype(full), gain_mlp[...].astype(full)]
    place = lax.broadcasted_iota(jnp.int32, (16, shard), 0)
    total = jnp.zeros((16, shard), full)
    for at, piece in enumerate(pieces):
        total = jnp.where(place == at, piece, total)
    small[...] = total.astype(low)
    send_item(1)
    send_item(2)
    own_gates[...] = jnp.concatenate([gate_rate[...].astype(full), gate_input[...].astype(full)], axis=1).astype(low)
    send_item(3)
    send_item(4)
    rows_all[0] = own[...]
    marks_all[0] = own_marks[...]
    _, real = keep_column(marks_all, 0)
    cotangent[...] = (cot_raw[...].astype(full) * real).astype(low)
    saves[13].start()
    for k in range(1, chips):
        cross_down(k).start()
    for k in range(1, chips):
        for what in range(2):
            rows_copy(what, k).wait_recv()
            mate_copy(what, k).start()
    for k in range(chips):
        for what in range(2):
            mate_copy(what, k).wait_recv()
    for row in range(width):
        values = rows_all[row].astype(full)
        scale[row] = lax.rsqrt(jnp.mean(values * values, axis=-1, keepdims=True) + epsilon)

    def work(index, first):
        columns = pl.ds(pl.multiple_of(index * shard, shard), shard)
        gain = small_all[index].astype(full)[taps + 1 : taps + 2]
        values = rows_all[:, :, columns].astype(full)
        part = (values * scale[...] * gain).astype(low).reshape(width * block, shard)
        normed[:, columns] = part
        for weight, target in ((gate_all, pre_gate), (x_all, x_total)):
            term = jnp.dot(part, weight[index], preferred_element_type=full).reshape(width, block, channels)
            if first:
                target[...] = term
            else:
                target[...] += term

    work(mine, True)
    for at in range(count):
        columns = slice(at * slice_f, (at + 1) * slice_f)
        turned[at] = jnp.concatenate(
            [w_feed_gate[:, columns].astype(full), w_feed_up[:, columns].astype(full)], axis=1
        ).astype(low)
    arrived[0, mine] = turned[mine]
    for k in range(1, chips):
        cross(0, k).start()
    for hop in range(1, half):
        for item in range(len(moved)):
            for way in range(2):
                ring_copy(way, hop, item).wait_recv()
                if hop < half - 1:
                    ring_copy(way, hop + 1, item).start()
                elif way in shared[item]:
                    last_copy(way, item).start()
            if item == 2:
                for way in range(2):
                    work(ring_index(count, -hop if way == 0 else hop), False)
    turn.start()
    gather.start()
    for item in range(3):
        last_copy(shared[item][0], item).wait_recv()
    work(ring_index(count, half), False)
    branch[...] = x_total[...].astype(low)
    for item in range(3, len(moved)):
        for way in shared[item]:
            last_copy(way, item).wait_recv()

    for row in range(width):
        column, _ = keep_column(marks_all, row)
        keep[row, :8] = jnp.ones((8, 1), full)
        keep[row, 8:] = column
        halo_out[row] = branch[row, block - 16 :].astype(full)[8:] * tail_factor(column, taps)
    halo_copy().start()
    entries = jnp.concatenate([small_all[at].astype(full)[:8, :own_channels] for at in range(count)], axis=1)
    place = lax.broadcasted_iota(jnp.int32, entries.shape, 0)
    decay_row = entries[taps : taps + 1]
    entries = jnp.where(place == taps, jax.nn.softplus(decay_row), entries)
    chan[...] = jnp.where(place == taps + 1, jax.nn.sigmoid(decay_row), entries)
    entries = jnp.concatenate([small_all[at].astype(full)[:8] for at in range(count)], axis=1)
    gains[...] = jnp.concatenate([entries[taps + 1 : taps + 3], jnp.zeros((6, depth), full)], axis=0)
    w_mix_all[...] = stack_rows(mix_all)
    for copy in saves[:6]:
        copy.start()
    entries = stack_rows(gates_all)
    for at in range(channels // size):
        rows = slice(at * size, (at + 1) * size)
        for target, first in ((rate_mat, 0), (inlet_mat, size)):
            parts = [entries[rows].astype(full)[:, first : first + size]]
            if at > 0:
                parts.insert(0, jnp.zeros((size, at * size), full))
            if at + 1 < channels // size:
                parts.append(jnp.zeros((size, channels - (at + 1) * size), full))
            target[rows] = jnp.concatenate(parts, axis=1).astype(low)

    halo_copy().wait_recv()
    soft = chan[taps : taps + 1]
    state_out[...] = jnp.zeros_like(state_out)

    @pl.loop(0, width)
    def _(row):
        from_before = jnp.where(mine > 0, halo_in[row], 0.0)
        halo[row] = from_before
        ext[:8] = from_before
        ext[8:] = branch[row].astype(full)
        valid = jnp.ones((block, 1), full)
        total = jnp.zeros((block, channels), full)
        for tap in range(taps):
            total = total + chan[tap : tap + 1] * valid * ext[8 - tap : 8 - tap + block]
            valid = valid * keep[row, 8 - tap : 8 - tap + block]
        conv = total.astype(low)
        conv_low[row] = conv
        rate_in = lax.dot_general(conv, rate_mat[...], (NT, ((), ())), preferred_element_type=full)
        inlet_in = lax.dot_general(conv, inlet_mat[...], (NT, ((), ())), preferred_element_type=full)
        pre_rate[row] = rate_in
        pre_inlet[row] = inlet_in
        _, inlet, decay, _, root = gate_terms(rate_in, inlet_in, soft)
        kept = keep[row, 8:]
        inflow = conv.astype(full) * inlet * ((1.0 - kept) + kept * root)
        row_product, row_state = scan_rows(decay * kept, inflow, False)
        product[row] = row_product
        state[row] = row_state
        state_out[0, pl.ds(row, 1)] = row_product[block - 1 :]
        state_out[1, pl.ds(row, 1)] = row_state[block - 1 :]

    for copy in saves[6:11]:
        copy.start()

    def background(h):
        turn.hop(h)
        for slot in (2 * h - 1, 2 * h) if h < half else (count - 1,):
            for k in range(1, chips):
                cross(slot, k).start()
        if h < half:
            gather.hop(h)
        else:
            gather.last()

    for step in range(1, count):
        state_copy(step).start()
    background(1)
    for step in range(1, count):
        state_copy(step).wait_recv()
    ends[0] = fold_states(count, state_all, False)
    ends[1] = state_out[0]

    def close(row):
        row_states = state[row] + product[row] * ends[0, pl.ds(row, 1)]
        states[row] = row_states
        active, _ = gelu_and_slope(pre_gate[row])
        row_mixed = (row_states * active).astype(low)
        mixed[row] = row_mixed
        return jnp.dot(row_mixed, w_mix_all[...], preferred_element_type=full)

    @pl.loop(0, chips)
    def _(at):
        k = chips - 1 - at
        core_out[k] = close(chips + k).astype(low)
        core_copy(k).start()

    @pl.loop(0, chips - 1)
    def _(at):
        k = chips - 1 - at
        part = close(k)
        core_copy(k).wait_recv()
        chip_out[k] = (part + core_in[k].astype(full)).astype(low)

    for k in range(chips - 1, 0, -1):
        chip_copy(k).start()
    part = close(0)
    background(2)
    core_copy(0).wait_recv()
    total = part + core_in[0].astype(full) + own[...].astype(full)
    for k in range(1, chips):
        chip_copy(k).wait_recv()
        total = total + chip_in[k].astype(full)
    for copy in saves[11:13]:
        copy.start()
    middle[...] = total
    scaled = total * lax.rsqrt(jnp.mean(total * total, axis=-1, keepdims=True) + epsilon)
    feed_own[...] = (scaled * gains[1:2]).astype(low)
    for h in range(3, half + 1):
        background(h)
    for k in range(chips):
        if k > 0:
            cross_down(k).wait_recv()
            for slot in range(count):
                cross(slot, k).wait_recv()
        w_both[:, 2 * k * slice_f : 2 * (k + 1) * slice_f] = arrived[k].reshape(depth, 2 * slice_f)
    for slot in range(count):
        gather.to_mate(slot).wait_recv()

    for copy in saves:
        copy.wait()
    for item in range(len(moved)):
        for way in range(2):
            for hop in range(1, half):
                ring_copy(way, hop, item).wait_send()
            if way in shared[item]:
                last_copy(way, item).wait_send()
    for what in range(2):
        for k in range(chips):
            mate_copy(what, k).wait_send()
        for k in range(1, chips):
            rows_copy(what, k).wait_send()
    for k in range(1, chips):
        cross_down(k).wait_send()
        chip_copy(k).wait_send()
        for slot in range(count):
            cross(slot, k).wait_send()
    for k in range(chips):
        core_copy(k).wait_send()
    for step in range(1, count):
        state_copy(step).wait_send()
    halo_copy().wait_send()
    turn.drain()
    gather.drain()


def forward(own, cotangent, resets, real_mask, *weights):
    conv_kernel, gate_rate, w_gate, w_mix, w_down = weights[2], weights[4], weights[6], weights[8], weights[11]
    count, width = lax.axis_size("seq"), lax.axis_size("dp")
    half, chips = count // 2, width // CORES
    block, depth = own.shape
    shard, part = w_gate.shape
    own_channels, size = gate_rate.shape
    channels = count * own_channels
    slice_f = w_down.shape[0]
    whole = pl.BlockSpec(memory_space=pltpu.VMEM)
    dma = pltpu.SemaphoreType.DMA
    rows = (width, block, channels)
    shapes = [
        ((width, 8, block), full), ((depth, 2 * chips * slice_f), low), ((8, depth), full), ((8, channels), full),
        ((block, depth), low), ((block, depth), full), ((block, depth), low), ((width, 8, channels), full),
        ((2, 8, channels), full), ((count, 2, block, depth), low), ((chips,) + w_down.shape, low),
    ]
    saved = [
        ((count, shard, part), low), ((count, shard, part), low), ((width * block, depth), low), (rows, full),
        (rows, low), ((channels, depth), low), (rows, low), (rows, full), (rows, full), ((channels, channels), low),
        ((channels, channels), low), (rows, full), (rows, low),
    ]
    return pl.pallas_call(
        partial(front_kernel, count, width),
        in_specs=[whole] * (4 + len(weights)),
        out_specs=[whole] * (len(shapes) - 2) + [pl.BlockSpec(memory_space=pl.ANY)] * (len(saved) + 2),
        out_shape=[jax.ShapeDtypeStruct(*shape) for shape in shapes + saved],
        scratch_shapes=[
            *[pltpu.VMEM(*shape) for shape in saved],
            dma((len(saved) + 1,)),
            pltpu.VMEM((8, block), full),
            pltpu.VMEM((16, shard), low),
            pltpu.VMEM((count, 16, shard), low),
            pltpu.VMEM((own_channels, 2 * size), low),
            pltpu.VMEM((count, own_channels, 2 * size), low),
            pltpu.VMEM((count,) + w_mix.shape, low),
            pltpu.VMEM((width, block, depth), low),
            pltpu.VMEM(rows, full),
            pltpu.VMEM((width, block, 1), full),
            pltpu.VMEM((count, shard, 2 * slice_f), low),
            pltpu.VMEM((chips, count, shard, 2 * slice_f), low),
            pltpu.VMEM((width, 8 + block, 1), full),
            pltpu.VMEM(rows, full),
            pltpu.VMEM(rows, full),
            pltpu.VMEM((8 + block, channels), full),
            pltpu.VMEM((width, 8, channels), full),
            pltpu.VMEM((width, 8, channels), full),
            pltpu.VMEM((2, 8, channels), full),
            pltpu.VMEM((count, 2, 8, channels), full),
            *[pltpu.VMEM((chips, block, depth), low)] * 4,
            dma((2, half, 5)), dma((2, half, 5)), dma((2, 5)), dma((2, 5)),
            dma((2, chips)), dma((2, chips)), dma((2, chips)), dma((2, chips)),
            dma((chips, count)), dma((chips, count)), dma((chips,)), dma((chips,)),
            dma((2,)), dma((count,)), dma((count,)), dma((chips,)), dma((chips,)), dma((chips,)), dma((chips,)), dma((1,)),
            *RingGather.scratch(count),
            *RingTurn.scratch(count, shard, 2 * slice_f),
        ],
        compiler_params=pltpu.CompilerParams(collective_id=2, has_side_effects=True, vmem_limit_bytes=63 << 20),
        cost_estimate=pl.CostEstimate(
            flops=6 * width * block * depth * channels, bytes_accessed=60 << 20, transcendentals=0
        ),
    )(own, cotangent, resets, real_mask, *weights)


def back_kernel(
    count, width, taps, d_feed, middle, cotangent, gains, marks, chan, halo, ends, w_down,
    w_mix_far, mixed_far, rate_far, inlet_far, conv_far, down_far,
    pre_gate, pre_rate, pre_inlet, states, branch, hidden, down_others,
    output, d_middle, d_pre_gate, d_branch, grad_mix, gate_grads, small_grads, gain_share, down_sum,
    w_mix, mixed, rate_mat, inlet_mat, conv_low, down_own, gate_rows, rate_rows, inlet_rows, state_rows, branch_rows,
    hidden_rows, keep, mix_rows, mix_grads, later, local, shift, ext, d_rate, d_inlet, sums, halo_out, halo_in,
    state_out, state_all, down_in, late_sem, row_sem, hidden_sem, *rest
):
    ring_refs, rest = rest[:5], rest[5:]
    ring_sems, rest = rest[:6], rest[6:]
    (arrived, leaving), mix_sems, rest = rest[:2], rest[2:4], rest[4:]
    halo_sem, state_out_sem, state_in_sem, chip_out, chip_in, mate_out, mate_in, cross_out, cross_in = rest
    half = count // 2
    chips = width // CORES
    far = count - 1
    block, depth = middle.shape
    channels = chan.shape[1]
    own_channels = channels // count
    size = gate_grads.shape[-1] // 2
    mine = lax.axis_index("seq")
    after, before = ring_sides(count)
    mate = core_mate()
    back, ahead = chip_mates(width), chip_mates(width, True)
    peers = [None] + [seq_peer(count, -step)[0] for step in range(1, count)]
    greet(mate, *back, *peers[1:])
    ring = RingSum(count, ring_refs, ring_sems, after, before, mate)
    items = [(lambda index: mix_grads[index].astype(full), arrived, leaving, (0, 1))]
    scatter = RingScatter(count, items, mix_sems, after, before)

    def chips_copy(k):
        return send(mix_rows.at[0], mix_rows.at[k], (chip_out.at[k], chip_in.at[k]), back[k - 1])

    def mate_copy(k):
        return send(mix_rows.at[k], mix_rows.at[chips + k], (mate_out.at[k], mate_in.at[k]), mate)

    def cross(k):
        return send(down_others.at[k - 1], down_in.at[k - 1], (cross_out.at[k], cross_in.at[k]), ahead[k - 1])

    late = [
        pltpu.make_async_copy(source, target, late_sem.at[at])
        for at, (source, target) in enumerate(
            (
                (mixed_far, mixed), (w_mix_far, w_mix), (rate_far, rate_mat), (inlet_far, inlet_mat),
                (conv_far, conv_low), (down_far, down_own),
            )
        )
    ]
    streams = (
        ((pre_gate, gate_rows), (pre_rate, rate_rows), (states, state_rows)),
        ((pre_rate, rate_rows), (pre_inlet, inlet_rows), (states, state_rows), (branch, branch_rows)),
    )

    def row_copies(which, row):
        return [
            pltpu.make_async_copy(source.at[row], target.at[row % 2], row_sem.at[at, row % 2])
            for at, (source, target) in enumerate(streams[which])
        ]

    def row_start(which, row):
        for copy in row_copies(which, row):
            copy.start()

    def row_ready(which, row):
        for copy in row_copies(which, row):
            copy.wait()

        @pl.when(row + 1 < width)
        def _():
            row_start(which, row + 1)

        return row % 2

    def halo_copy():
        return send(halo_out, halo_in, (halo_sem.at[0], halo_sem.at[1]), peers[1])

    def state_copy(step):
        return send(state_out, state_all.at[step], (state_out_sem.at[step], state_in_sem.at[step]), peers[step])

    def fetch(at):
        return pltpu.make_async_copy(hidden.at[far - at], hidden_rows.at[at % 2], hidden_sem.at[at % 2])

    fetch(0).start()
    for copy in late:
        copy.start()
    row_start(0, 0)

    values, arriving = middle[...], d_feed[...]
    scale = lax.rsqrt(jnp.mean(values * values, axis=-1, keepdims=True) + epsilon)
    normed = values * scale
    scaled = arriving * gains[1:2]
    gain_share[...] = jnp.sum(arriving * normed, axis=0, keepdims=True)
    total = cotangent[...].astype(full) + scale * (
        scaled - normed * jnp.mean(scaled * normed, axis=-1, keepdims=True)
    )
    d_middle[...] = total
    mix_rows[0] = total.astype(low)
    for k in range(1, chips):
        chips_copy(k).start()
    mate_copy(0).start()

    def offer(at):
        slot = far - at
        fetch(at).wait()

        @pl.when(at < far)
        def _():
            fetch(at + 1).start()

        rows = hidden_rows[at % 2].reshape(2 * block, hidden.shape[-1])
        ring.offer(slot, jnp.dot(rows, w_down[...], preferred_element_type=full), at >= ring.held)

    pl.loop(0, 3)(offer)
    ring.begin()
    pl.loop(3, count)(offer)
    for k in range(1, chips):
        chips_copy(k).wait_recv()
        mate_copy(k).start()
    for k in range(1, chips):
        cross(k).start()
    ring.step(1)
    for copy in late[:2]:
        copy.wait()
    for k in range(chips):
        mate_copy(k).wait_recv()
    tokens = width * block
    rows = mixed[...].reshape(tokens, channels)
    wide = depth // 4
    for at in range(4):
        part = lax.dot_general(
            rows,
            mix_rows[:, :, at * wide : (at + 1) * wide].reshape(tokens, wide),
            (TN, ((), ())),
            preferred_element_type=full,
        )
        for piece in range(count):
            mix_grads[piece, :, at * wide : (at + 1) * wide] = part[
                piece * own_channels : (piece + 1) * own_channels
            ].astype(low)
    scatter.begin()

    soft, soft_slope = chan[taps : taps + 1], chan[taps + 1 : taps + 2]
    state_out[0] = ends[1]
    state_out[1] = jnp.zeros_like(ends[1])
    sums[...] = jnp.zeros_like(sums)

    def adjoint_row(row):
        at = row_ready(0, row)
        column, real = keep_column(marks, row)
        keep[row, :8] = jnp.ones((8, 1), full)
        keep[row, 8:] = column
        sums[taps + 2 : taps + 3] += jnp.sum(real)
        d_mixed = lax.dot_general(mix_rows[row], w_mix[...], (NT, ((), ())), preferred_element_type=full)
        active, slope = gelu_and_slope(gate_rows[at])
        d_pre_gate[row] = (d_mixed * state_rows[at] * slope).astype(low)
        decay = jnp.exp(-8.0 * jax.nn.sigmoid(rate_rows[at]) * soft)
        sums[taps + 1 : taps + 2] += jnp.sum(decay * real, axis=0, keepdims=True)
        shift[:block] = decay * column
        shift[block:] = jnp.ones((8, channels), full)
        row_later, row_local = scan_rows(shift[1 : block + 1], d_mixed * active, True)
        later[row] = row_later
        local[row] = row_local
        state_out[1, pl.ds(row, 1)] = shift[:1] * row_local[:1]

    pl.loop(0, width // 2)(adjoint_row)
    if half > 2:
        ring.step(2)
    pl.loop(width // 2, width)(adjoint_row)
    row_start(1, 0)
    for step in range(1, count):
        state_copy(step).start()
    scatter.onward(1)
    for copy in late[2:]:
        copy.wait()
    for step in range(1, count):
        state_copy(step).wait_recv()
    sums[8:16] = fold_states(count, state_all, True)

    def gate_row(row):
        at = row_ready(1, row)
        column = keep[row, 8:]
        rate, inlet, decay, _, root = gate_terms(rate_rows[at], inlet_rows[at], soft)
        conv = conv_low[row].astype(full)
        adjoint = local[row] + later[row] * sums[pl.ds(8 + row, 1)]
        shift[:8] = jnp.broadcast_to(ends[0, pl.ds(row, 1)], (8, channels))
        shift[8:] = state_rows[at]
        previous = shift[7 : 7 + block]
        mult = (1.0 - column) + column * root
        d_log = adjoint * column * (decay * previous - conv * inlet * decay * decay / root)
        rate_part = (d_log * (-8.0 * soft) * rate * (1.0 - rate)).astype(low)
        inlet_part = (adjoint * conv * mult * inlet * (1.0 - inlet)).astype(low)
        d_rate[row] = rate_part
        d_inlet[row] = inlet_part
        sums[taps : taps + 1] += jnp.sum(d_log * (-8.0 * rate), axis=0, keepdims=True) * soft_slope
        through = (
            adjoint * inlet * mult
            + jnp.dot(rate_part, rate_mat[...], preferred_element_type=full)
            + jnp.dot(inlet_part, inlet_mat[...], preferred_element_type=full)
        )
        ext[:8] = halo[row]
        ext[8:] = branch_rows[at].astype(full)
        place = lax.broadcasted_iota(jnp.int32, (8, 1), 0)
        valid = jnp.ones((block, 1), full)
        branch_part = jnp.zeros((block, channels), full)
        tail = jnp.zeros((8, channels), full)
        for tap in range(taps):
            moved = valid * through
            sums[tap : tap + 1] += jnp.sum(moved * ext[8 - tap : 8 - tap + block], axis=0, keepdims=True)
            moved = moved * chan[tap : tap + 1]
            if tap == 0:
                branch_part = moved
            else:
                shift[:block] = moved
                shift[block:] = jnp.zeros((8, channels), full)
                branch_part = branch_part + shift[tap : tap + block]
                for j in range(1, tap + 1):
                    tail = tail + jnp.where(place == 8 - j, moved[tap - j : tap - j + 1], 0.0)
            valid = valid * keep[row, 8 - tap : 8 - tap + block]
        local[row] = branch_part
        halo_out[row] = tail

    pl.loop(0, width // 2)(gate_row)
    for step in range(3, half):
        ring.step(step)
    if half > 2:
        scatter.onward(2)
    pl.loop(width // 2, width)(gate_row)
    halo_copy().start()
    rows = conv_low[...].reshape(tokens, channels)
    both = [
        lax.dot_general(part[...].reshape(tokens, channels), rows, (TN, ((), ())), preferred_element_type=full)
        for part in (d_rate, d_inlet)
    ]
    for piece in range(count):
        first = piece * own_channels
        at = first // size * size
        gate_grads[piece] = jnp.concatenate(
            [part[first : first + own_channels, at : at + size] for part in both], axis=1
        ).astype(low)
    halo_copy().wait_recv()

    @pl.loop(0, width)
    def _(row):
        column = keep[row, 8:]
        arriving = jnp.where(mine < count - 1, halo_in[row] * tail_factor(column, taps), 0.0)
        local[row, block - 8 :] += arriving
        d_branch[row] = local[row].astype(low)

    for piece in range(count):
        entries = sums[:8, piece * own_channels : (piece + 1) * own_channels]
        small_grads[piece] = jnp.concatenate([entries, jnp.zeros((8, 128 - own_channels), full)], axis=1)
    for step in range(3, half):
        scatter.onward(step)
    total = down_own[...].astype(full)
    for k in range(1, chips):
        cross(k).wait_recv()
        total = total + down_in[k - 1].astype(full)
    down_sum[...] = total
    _, real = keep_column(marks, 0)
    output[...] = ((middle[...] + ring.finish()) * real).astype(low)

    grad_mix[...] = scatter.finish(0)
    ring.drain()
    scatter.drain()
    halo_copy().wait_send()
    for step in range(1, count):
        state_copy(step).wait_send()
    for k in range(chips):
        mate_copy(k).wait_send()
    for k in range(1, chips):
        chips_copy(k).wait_send()
        cross(k).wait_send()


def mix_back(taps, size, near, late, rows, hidden, down_others):
    (d_feed, middle, _, _, _, chan, *_) = near
    count, width = lax.axis_size("seq"), lax.axis_size("dp")
    chips = width // CORES
    block, depth = middle.shape
    channels = chan.shape[1]
    own_channels = channels // count
    whole = pl.BlockSpec(memory_space=pltpu.VMEM)
    far = pl.BlockSpec(memory_space=pl.ANY)
    dma = pltpu.SemaphoreType.DMA
    all_rows = (width, block, channels)
    shapes = [
        ((block, depth), low), ((block, depth), full), (all_rows, low), (all_rows, low),
        ((own_channels, depth), full), ((count, own_channels, 2 * size), low), ((count, 8, 128), full),
        ((1, depth), full), (late[-1].shape, full),
    ]
    operands = (*near, *late, *rows, hidden, down_others)
    return pl.pallas_call(
        partial(back_kernel, count, width, taps),
        in_specs=[whole] * len(near) + [far] * (len(operands) - len(near)),
        out_specs=[whole] * len(shapes),
        out_shape=[jax.ShapeDtypeStruct(*shape) for shape in shapes],
        scratch_shapes=[
            *[pltpu.VMEM(each.shape, each.dtype) for each in (late[0], late[1], *late[2:])],
            *[pltpu.VMEM((2,) + each.shape[1:], each.dtype) for each in (*rows, hidden)],
            pltpu.VMEM((width, 8 + block, 1), full),
            pltpu.VMEM((width, block, depth), low),
            pltpu.VMEM((count, own_channels, depth), low),
            pltpu.VMEM(all_rows, full),
            pltpu.VMEM(all_rows, full),
            pltpu.VMEM((block + 8, channels), full),
            pltpu.VMEM((block + 8, channels), full),
            pltpu.VMEM(all_rows, low),
            pltpu.VMEM(all_rows, low),
            pltpu.VMEM((16, channels), full),
            pltpu.VMEM((width, 8, channels), full),
            pltpu.VMEM((width, 8, channels), full),
            pltpu.VMEM((2, 8, channels), full),
            pltpu.VMEM((count, 2, 8, channels), full),
            pltpu.VMEM(down_others.shape, low),
            dma((len(late),)), dma((4, 2)), dma((2,)),
            *RingSum.scratch(count, block, depth),
            *RingScatter.scratch(count, [((own_channels, depth), low)]),
            dma((2,)), dma((count,)), dma((count,)), dma((chips,)), dma((chips,)), dma((chips,)), dma((chips,)),
            dma((chips,)), dma((chips,)),
        ],
        compiler_params=pltpu.CompilerParams(collective_id=4, has_side_effects=True, vmem_limit_bytes=63 << 20),
        cost_estimate=pl.CostEstimate(
            flops=4 * width * block * channels * (depth + 2 * channels), bytes_accessed=60 << 20, transcendentals=0
        ),
    )(*operands)


def close_kernel(
    count, width, own, d_middle, gains, gain_share, normed, d_pre_gate, d_branch, gate_grads, small_grads,
    w_gate_far, w_x_far, feed_sum, d_inputs, out_gate, out_x, out_gates, out_small, feed_gate, feed_up, out_gains,
    w_gate, w_x, out_feed, late_sem, *rest
):
    travel, rest = rest[:10], rest[10:]
    core_out, core_in, chip_out, chip_in, gain_out, gain_width, gain_total, gain_seq = rest[:8]
    core_out_sem, core_in_sem, chip_out_sem, chip_in_sem, width_out, width_in, seq_out, seq_in = rest[8:16]
    turn_refs = rest[16:]
    half = count // 2
    chips = width // CORES
    block, depth = own.shape
    shard = out_gate.shape[0]
    share = depth // width
    mine = lax.axis_index("seq")
    my_width = lax.axis_index("dp")
    after, before = ring_sides(count)
    mate = core_mate()
    ahead = chip_mates(width, True)
    peers = [None] + [seq_peer(count, step) for step in range(1, count)]
    others = [None] + [lax.rem(my_width + step, width) for step in range(1, width)]
    greet(*[peer for peer, _ in peers[1:]], *[{"dp": place} for place in others[1:]])

    def product(grads):
        def at(index):
            columns = pl.ds(pl.multiple_of(index * shard, shard), shard)
            return lax.dot_general(normed[:, columns], grads[...], (TN, ((), ())), preferred_element_type=full)

        return at

    def stored(grads):
        return lambda index: grads[index].astype(full)

    values = (product(d_pre_gate), product(d_branch), stored(gate_grads), stored(small_grads))
    results = (out_gate, out_x, out_gates, out_small)
    items = list(zip(values, travel[:4], travel[4:8], ((0,), (1,), (1,), (0,))))
    scatter = RingScatter(count, items, travel[8:], after, before)
    turn = RingTurn(count, feed_sum, out_feed, turn_refs[0], turn_refs[1:], after, before)

    late = [
        pltpu.make_async_copy(source, target, late_sem.at[at])
        for at, (source, target) in enumerate(
            ((w_gate_far, w_gate), (w_x_far, w_x), (feed_sum.at[mine], out_feed.at[mine]))
        )
    ]

    def core_copy(k):
        return send(core_out.at[k], core_in.at[k], (core_out_sem.at[k], core_in_sem.at[k]), mate)

    def chip_copy(k):
        return send(chip_out.at[k], chip_in.at[k], (chip_out_sem.at[k], chip_in_sem.at[k]), ahead[k - 1])

    def width_copy(step):
        columns = pl.ds(pl.multiple_of(others[step] * share, share), share)
        sems = (width_out.at[step], width_in.at[step])
        return send(gain_out.at[:, columns], gain_width.at[step], sems, {"dp": others[step]})

    def seq_copy(step):
        return send(gain_total, gain_seq.at[step], (seq_out.at[step], seq_in.at[step]), peers[step][0])

    def through(row):
        return lax.dot_general(
            d_pre_gate[pl.ds(pl.multiple_of(row * block, block), block)],
            w_gate[...],
            (NT, ((), ())),
            preferred_element_type=full,
        ) + lax.dot_general(
            d_branch[pl.ds(pl.multiple_of(row * block, block), block)],
            w_x[...],
            (NT, ((), ())),
            preferred_element_type=full,
        )

    scatter.begin()
    turn.start()
    for copy in late:
        copy.start()
    for copy in late:
        copy.wait()

    @pl.loop(0, chips)
    def _(at):
        k = chips - 1 - at
        core_out[k] = through(chips + k).astype(low)
        core_copy(k).start()

    scatter.onward(1)
    turn.hop(1)

    @pl.loop(0, chips - 1)
    def _(at):
        k = chips - 1 - at
        part = through(k)
        core_copy(k).wait_recv()
        chip_out[k] = (part + core_in[k].astype(full)).astype(low)

    for k in range(chips - 1, 0, -1):
        chip_copy(k).start()
    part = through(0)
    core_copy(0).wait_recv()
    total = part + core_in[0].astype(full)
    for k in range(1, chips):
        chip_copy(k).wait_recv()
        total = total + chip_in[k].astype(full)
    rows = own[...].astype(full)
    scale = lax.rsqrt(jnp.mean(rows * rows, axis=-1, keepdims=True) + epsilon)
    rows = rows * scale
    scaled = total * gains[:1]
    d_inputs[...] = (
        d_middle[...] + scale * (scaled - rows * jnp.mean(scaled * rows, axis=-1, keepdims=True))
    ).astype(low)
    gain_out[...] = jnp.zeros_like(gain_out)
    gain_out[:1] = jnp.sum(total * rows, axis=0, keepdims=True)
    gain_out[1:2] = gain_share[...]
    for step in range(1, width):
        width_copy(step).start()
    if half > 2:
        scatter.onward(2)
    turn.hop(2)
    columns = pl.ds(pl.multiple_of(my_width * share, share), share)
    gain_sum = gain_out[:, columns]
    for step in range(1, width):
        width_copy(step).wait_recv()
        gain_sum = gain_sum + gain_width[step]
    gain_total[...] = gain_sum
    for step in range(1, count):
        seq_copy(step).start()
    for step in range(3, half):
        scatter.onward(step)
        turn.hop(step)
    for step in range(1, count):
        seq_copy(step).wait_recv()
        gain_sum = gain_sum + gain_seq[step]
    out_gains[...] = gain_sum
    for item, result in enumerate(results):
        result[...] = scatter.finish(item)
    if half > 2:
        turn.hop(half)
    wide = out_feed.shape[-1] // 2
    for target, columns in ((feed_gate, slice(0, wide)), (feed_up, slice(wide, 2 * wide))):
        parts = [out_feed[at].astype(full)[:, columns] for at in range(count)]
        target[...] = jnp.concatenate(parts, axis=1).astype(low)

    scatter.drain()
    turn.drain()
    for step in range(1, count):
        seq_copy(step).wait_send()
    for step in range(1, width):
        width_copy(step).wait_send()
    for k in range(chips):
        core_copy(k).wait_send()
    for k in range(1, chips):
        chip_copy(k).wait_send()


def close(operands):
    own, _, _, _, normed, d_pre_gate, _, gate_grads, small_grads, w_gate, w_x, feed_sum = operands
    count, width = lax.axis_size("seq"), lax.axis_size("dp")
    chips = width // CORES
    block, depth = own.shape
    channels = d_pre_gate.shape[1]
    shard, share = depth // count, depth // width
    whole = pl.BlockSpec(memory_space=pltpu.VMEM)
    dma = pltpu.SemaphoreType.DMA
    items = [
        ((shard, channels), low), ((shard, channels), low), (gate_grads.shape[1:], low), (small_grads.shape[1:], full),
    ]
    shapes = [
        ((block, depth), low), *[(shape, full) for shape, _ in items],
        *[((shard, feed_sum.shape[2] // 2 * count), low)] * 2, ((8, share), full),
    ]
    return pl.pallas_call(
        partial(close_kernel, count, width),
        in_specs=[whole] * (len(operands) - 3) + [pl.BlockSpec(memory_space=pl.ANY)] * 3,
        out_specs=[whole] * len(shapes),
        out_shape=[jax.ShapeDtypeStruct(*shape) for shape in shapes],
        scratch_shapes=[
            *[pltpu.VMEM(each.shape, low) for each in (w_gate, w_x, feed_sum)],
            dma((3,)),
            *RingScatter.scratch(count, items),
            *[pltpu.VMEM((chips, block, depth), low)] * 4,
            pltpu.VMEM((8, depth), full),
            pltpu.VMEM((width, 8, share), full),
            pltpu.VMEM((8, share), full),
            pltpu.VMEM((count, 8, share), full),
            dma((chips,)), dma((chips,)), dma((chips,)), dma((chips,)),
            dma((width,)), dma((width,)), dma((count,)), dma((count,)),
            *RingTurn.scratch(count, *feed_sum.shape[1:]),
        ],
        compiler_params=pltpu.CompilerParams(collective_id=5, has_side_effects=True, vmem_limit_bytes=63 << 20),
        cost_estimate=pl.CostEstimate(
            flops=8 * normed.shape[0] * depth * channels, bytes_accessed=40 << 20, transcendentals=0
        ),
    )(*operands)


def on_device(
    inputs,
    cotangent,
    resets,
    real_mask,
    gain_mix,
    w_branch_gate,
    w_branch_x,
    conv_kernel,
    gate_rate,
    gate_input,
    decay_param,
    w_mix_out,
    gain_mlp,
    w_mlp_gate,
    w_mlp_up,
    w_mlp_down,
):
    seq = lax.axis_size("seq")
    rows_own, length, depth = inputs.shape
    taps = conv_kernel.shape[1]
    block = rows_own * length
    tokens = block * lax.axis_size("dp")
    own_channels, size = gate_rate.shape
    shard, part_w = w_branch_x.shape
    rows = inputs.reshape(block, depth)
    (
        marks, w_both, gains, chan, cot_low, middle, feed_own, halo, ends, d_feed, w_down,
        w_gate_all, w_x_all, mixer_in, pre_gate, branch, w_mix_out, conv_low, pre_rate, pre_inlet, rate_mat, inlet_mat,
        states, mixed,
    ) = forward(
        rows, cotangent.reshape(block, depth), resets, real_mask, gain_mix[None], gain_mlp[None], conv_kernel,
        decay_param[None], gate_rate, gate_input, w_branch_gate, w_branch_x, w_mix_out, w_mlp_gate, w_mlp_up,
        w_mlp_down,
    )
    w_down = w_down.reshape(-1, depth)

    hidden, d_feed_own, feed_sum, down_own, down_others = feed_forward(feed_own, w_both, w_down, d_feed)

    (
        output, d_middle, d_pre_gate, d_branch, grad_mix_out, gate_grads, small_grads, gain_share, grad_down,
    ) = mix_back(
        taps,
        size,
        (d_feed_own, middle, cot_low, gains, marks, chan, halo, ends, w_down),
        (w_mix_out, mixed, rate_mat, inlet_mat, conv_low, down_own),
        (pre_gate, pre_rate, pre_inlet, states, branch),
        hidden,
        down_others,
    )

    grad_inputs, grad_gate, grad_x, grad_gates, grad_small, feed_gate, feed_up, gains = close(
        (
            rows, d_middle, gains, gain_share, mixer_in, d_pre_gate.reshape(tokens, part_w),
            d_branch.reshape(tokens, part_w), gate_grads, small_grads, w_gate_all.reshape(depth, part_w),
            w_x_all.reshape(depth, part_w), feed_sum.reshape(seq, shard, -1),
        )
    )
    own_share = gains.shape[1] // seq
    gains = lax.dynamic_slice_in_dim(gains, lax.axis_index("seq") * own_share, own_share, 1)
    grad_small = grad_small[:, :own_channels]
    return (
        output[None],
        grad_inputs[None],
        gains[0],
        grad_gate,
        grad_x,
        grad_small[:taps].T,
        grad_gates[:, :size],
        grad_gates[:, size:],
        grad_small[taps],
        grad_mix_out,
        gains[1],
        feed_gate.astype(full),
        feed_up.astype(full),
        grad_down,
        grad_small[taps + 1] / grad_small[taps + 2],
    )


def solution(mesh):
    placed = (
        P("dp", "seq", None),
        P("dp", "seq", None),
        P("dp", "seq"),
        P("dp", "seq"),
        P("seq"),
        P("seq", "dp"),
        P("seq", "dp"),
        P(("dp", "seq"), None),
        P(("dp", "seq"), None),
        P(("dp", "seq"), None),
        P(("dp", "seq")),
        P(("dp", "seq"), None),
        P("seq"),
        P("seq", "dp"),
        P("seq", "dp"),
        P(("dp", "seq"), None),
    )
    return jax.shard_map(
        on_device,
        mesh=mesh,
        in_specs=placed,
        out_specs=(
            P("dp", "seq", None),
            P("dp", "seq", None),
            P(("dp", "seq")),
            P("seq", "dp"),
            P("seq", "dp"),
            P(("dp", "seq"), None),
            P(("dp", "seq"), None),
            P(("dp", "seq"), None),
            P(("dp", "seq")),
            P(("dp", "seq"), None),
            P(("dp", "seq")),
            P("seq", "dp"),
            P("seq", "dp"),
            P(("dp", "seq"), None),
            P(("dp", "seq")),
        ),
        check_vma=False,
    )
```

```python
from functools import partial

import jax
import jax.numpy as jnp
from jax import lax
from jax.experimental import pallas as pl
from jax.experimental.pallas import tpu as pltpu
from jax.sharding import PartitionSpec as P

epsilon = 1e-06
low = jnp.bfloat16
full = jnp.float32
CORES = 2


def ring_of(count):
    deep = 4 if count % 4 == 0 else 1
    wide = count // deep
    walk = [(z, 0) for z in range(deep)]
    for turn, z in enumerate(reversed(range(deep))):
        across = list(range(1, wide))
        walk += [(z, y) for y in (across if turn % 2 == 0 else across[::-1])]
    return [z * wide + y for z, y in walk]


NT = ((1,), (1,))
TN = ((0,), (0,))


MESH = pl.DeviceIdType.MESH


def pick_from(table, index):
    found = table[0]
    for at in range(1, len(table)):
        found = jnp.where(index == at, table[at], found)
    return found


def ring_sides(count):
    ring = ring_of(count)
    place = {index: position for position, index in enumerate(ring)}
    mine = lax.axis_index("seq")
    after = pick_from([ring[(place[index] + 1) % count] for index in range(count)], mine)
    before = pick_from([ring[(place[index] - 1) % count] for index in range(count)], mine)
    return {"seq": after}, {"seq": before}


def core_mate():
    mine = lax.axis_index("dp")
    return {"dp": mine + 1 - 2 * lax.rem(mine, 2)}


def greet(*devices):
    barrier = pltpu.get_barrier_semaphore()
    for device in devices:
        pl.semaphore_signal(barrier, inc=1, device_id=device, device_id_type=MESH)
    pl.semaphore_wait(barrier, len(devices))


def send(source, target, sems, device):
    return pltpu.make_async_remote_copy(
        src_ref=source, dst_ref=target, send_sem=sems[0], recv_sem=sems[1], device_id=device, device_id_type=MESH
    )


def gelu_and_slope(value):
    scale = 0.7978845608028654
    square = value * value
    bent = jnp.tanh(scale * value * (1.0 + 0.044715 * square))
    half = 0.5 * (1.0 + bent)
    slope = half + 0.5 * value * (1.0 - bent * bent) * (scale * (1.0 + 3.0 * 0.044715 * square))
    return value * half, slope


def ring_index(count, offset):
    ring = ring_of(count)
    place = {index: position for position, index in enumerate(ring)}
    mine = lax.axis_index("seq")
    return pick_from([ring[(place[index] + offset) % count] for index in range(count)], mine)


def chip_mates(width, ahead=False):
    chips = width // CORES
    mine = lax.axis_index("dp")
    return [{"dp": lax.rem(mine + (k if ahead else chips - k) * CORES, width)} for k in range(1, chips)]


class RingSum:
    def __init__(self, count, refs, sems, after, before, mate):
        self.half, self.far = count // 2, count - 1
        self.stash, self.core_out, self.core_in, self.right_in, self.left_in = refs
        self.core_sems, self.right_sems, self.left_sems = sems[0:2], sems[2:4], sems[4:6]
        self.after, self.before, self.mate = after, before, mate
        self.held = self.core_out.shape[0]
        self.block = self.stash.shape[1]
        self.cut = self.block // 2

    @staticmethod
    def scratch(count, block, depth):
        half = count // 2
        dma = pltpu.SemaphoreType.DMA
        return [
            pltpu.VMEM((count, block, depth), low),
            pltpu.VMEM((4, block, depth), low),
            pltpu.VMEM((count, block, depth), low),
            pltpu.VMEM((half, block, depth), low),
            pltpu.VMEM((half, block, depth), low),
            dma((4,)), dma((count,)), dma((half, 2)), dma((half, 2)), dma((half, 2)), dma((half, 2)),
        ]

    def core_copy(self, slot):
        place = slot % self.held
        sems = (self.core_sems[0].at[place], self.core_sems[1].at[slot])
        return send(self.core_out.at[place], self.core_in.at[slot], sems, self.mate)

    def rows(self, part):
        return pl.ds(part * self.cut, self.cut)

    def side_copy(self, way, slot, step, part):
        target, sems = ((self.right_in, self.right_sems), (self.left_in, self.left_sems))[way]
        sems = (sems[0].at[step, part], sems[1].at[step, part])
        rows = self.rows(part)
        return send(self.stash.at[slot, rows], target.at[step, rows], sems, (self.after, self.before)[way])

    def offer(self, slot, part, again):
        part = part.astype(low)
        self.stash[slot] = part[: self.block]

        @pl.when(again)
        def _():
            self.core_copy(slot).wait_send()

        self.core_out[slot % self.held] = part[self.block :]
        self.core_copy(slot).start()

    def begin(self):
        self.core_copy(self.far).wait_recv()
        for way in range(2):
            rows = self.rows(way)
            total = self.stash[self.far, rows].astype(full) + self.core_in[self.far, rows].astype(full)
            self.stash[self.far, rows] = total.astype(low)
            self.side_copy(way, self.far, 0, way).start()

    def step(self, step, turn):
        for way, arrived in ((0, self.right_in), (1, self.left_in)):
            slot = 2 * (self.half - step) - way
            part = 1 - way if turn == 0 else way
            rows = self.rows(part)
            if turn == 0:
                self.core_copy(slot).wait_recv()
            total = self.stash[slot, rows].astype(full) + self.core_in[slot, rows].astype(full)
            if step > 1 or turn == 1:
                self.side_copy(way, slot, step - 1, part).wait_recv()
                total = total + arrived[step - 1, rows].astype(full)
            self.stash[slot, rows] = total.astype(low)
            self.side_copy(way, slot, step, part).start()

    def finish(self):
        self.core_copy(0).wait_recv()
        total = self.stash[0].astype(full) + self.core_in[0].astype(full)
        last = self.half - 1
        for way in range(2):
            for part in range(2):
                self.side_copy(way, 0, last, part).wait_recv()
        return total + self.right_in[last].astype(full) + self.left_in[last].astype(full)

    def drain(self):
        for slot in range(self.held):
            self.core_copy(slot).wait_send()
        for way in range(2):
            self.side_copy(way, 0, 0, way).wait_send()
            for step in range(1, self.half):
                for part in range(2):
                    self.side_copy(way, 0, step, part).wait_send()


class RingGather:
    def __init__(self, count, own, found, sems, after, before, mate, keep_sem=None):
        self.half, self.far = count // 2, count - 1
        self.own, self.found, self.sems, self.keep_sem = own, found, sems, keep_sem
        self.after, self.before, self.mate = after, before, mate
        self.cut = own.shape[0] // 2

    @staticmethod
    def scratch(count):
        dma = pltpu.SemaphoreType.DMA
        return [dma((count, 2)), dma((count, 2)), dma((count,)), dma((count,))]

    def onward(self, way, slot, to, part):
        rows = pl.ds(part * self.cut, self.cut)
        source = self.own.at[rows] if slot is None else self.found.at[slot, 0, rows]
        sems = (self.sems[0].at[to, part], self.sems[1].at[to, part])
        return send(source, self.found.at[to, 0, rows], sems, (self.after, self.before)[way])

    def to_mate(self, slot):
        sems = (self.sems[2].at[slot], self.sems[3].at[slot])
        source = self.own if isinstance(slot, int) and slot == 0 else self.found.at[slot, 0]
        return send(source, self.found.at[slot, 1], sems, self.mate)

    def start(self):
        for turn in range(2):
            for way in range(2):
                self.onward(way, None, 1 + way, way if turn == 0 else 1 - way).start()
        self.to_mate(0).start()
        if self.keep_sem is None:
            self.found[0, 0] = self.own[...]
        else:
            self.keep().start()

    def keep(self):
        return pltpu.make_async_copy(self.own, self.found.at[0, 0], self.keep_sem)

    def hop(self, h, turn, last):
        for way in range(2):
            slot = 2 * h - 1 + way
            part = way if turn == 0 else 1 - way
            self.onward(way, slot, slot, part).wait_recv()
            if not last:
                self.onward(way, slot, slot + 2, part).start()
            elif turn == 0:
                self.onward(way, slot, self.far, part).start()
            if turn == 1:
                self.to_mate(slot).start()

    def last(self):
        for way in range(2):
            self.onward(way, self.far, self.far, way).wait_recv()
        self.to_mate(self.far).start()

    def drain(self):
        for slot in range(self.far + 1):
            self.to_mate(slot).wait_send()
        for slot in range(1, self.far + 1):
            for part in range(2):
                self.onward(0, self.far, slot, part).wait_send()
        if self.keep_sem is not None:
            self.keep().wait()


class RingTurn:
    def __init__(self, count, source, target, transit, sems, after, before):
        self.count, self.half = count, count // 2
        self.source, self.target, self.transit, self.sems = source, target, transit, sems
        self.after, self.before = after, before
        self.cut = source.shape[1] // 2

    @staticmethod
    def scratch(count, rows, columns):
        half = count // 2
        dma = pltpu.SemaphoreType.DMA
        return [
            pltpu.VMEM((2, half * (half - 1) // 2, rows, columns), low),
            dma((2, half * (half + 1) // 2)),
            dma((2, half * (half + 1) // 2)),
        ]

    def copy(self, way, hop, away):
        sign = 1 - 2 * way
        number = sum(range(hop)) if hop == 0 else sum(self.half - j + 1 for j in range(1, hop)) + away - hop
        if hop == 1:
            source = self.source.at[ring_index(self.count, sign * away)]
        else:
            source = self.transit.at[way, sum(self.half - j for j in range(1, hop - 1)) + away - hop]
        if away == hop:
            target = self.target.at[ring_index(self.count, sign * (1 - hop))]
        else:
            target = self.transit.at[way, sum(self.half - j for j in range(1, hop)) + away - hop - 1]
        if away == self.half:
            rows = pl.ds(way * self.cut, self.cut)
            source, target = source.at[rows], target.at[rows]
        sems = (self.sems[0].at[way, number], self.sems[1].at[way, number])
        return send(source, target, sems, (self.after, self.before)[way])

    def start(self):
        for away in range(self.half, 0, -1):
            for way in range(2):
                self.copy(way, 1, away).start()

    def hop(self, hop):
        for away in range(self.half, hop - 1, -1):
            for way in range(2):
                self.copy(way, hop, away).wait_recv()
                if away > hop:
                    self.copy(way, hop + 1, away).start()

    def drain(self):
        for hop in range(1, self.half + 1):
            for away in range(hop, self.half + 1):
                for way in range(2):
                    self.copy(way, hop, away).wait_send()


class RingScatter:
    def __init__(self, count, items, sems, after, before):
        self.count, self.half = count, count // 2
        self.items, self.sems = items, sems
        self.after, self.before = after, before

    @staticmethod
    def scratch(count, shapes):
        half = count // 2
        dma = pltpu.SemaphoreType.DMA
        arrived = [pltpu.VMEM((2, half) + shape, kind) for shape, kind in shapes]
        leaving = [pltpu.VMEM((2, 2) + shape, kind) for shape, kind in shapes]
        return arrived + leaving + [dma((len(shapes), 2, half)), dma((len(shapes), 2, half))]

    def columns(self, item, way):
        _, arrived, _, ways = self.items[item]
        wide = arrived.shape[-1]
        return pl.ds(way * (wide // 2), wide // 2) if len(ways) == 2 else pl.ds(0, wide)

    def copy(self, item, way, step):
        _, arrived, leaving, _ = self.items[item]
        source, target = leaving.at[way, step % 2], arrived.at[way, step]
        if step == 0:
            columns = self.columns(item, way)
            source, target = source.at[:, columns], target.at[:, columns]
        sems = (self.sems[0].at[item, way, step], self.sems[1].at[item, way, step])
        return send(source, target, sems, (self.after, self.before)[way])

    def begin(self):
        index = ring_index(self.count, self.half)
        for item, (value, _, leaving, ways) in enumerate(self.items):
            far = value(index).astype(leaving.dtype)
            for way in ways:
                leaving[way, 0] = far
                self.copy(item, way, 0).start()

    def onward(self, step):
        for item, (value, arrived, leaving, ways) in enumerate(self.items):
            for way in range(2):
                offset = self.half - step
                mine = value(ring_index(self.count, offset if way == 0 else -offset))
                if step > 1:
                    self.copy(item, way, step - 1).wait_recv()
                    mine = mine + arrived[way, step - 1].astype(full)
                if step > 2 or (step == 2 and way in ways):
                    self.copy(item, way, step - 2).wait_send()
                leaving[way, step % 2] = mine.astype(leaving.dtype)
                if step == 1 and way in ways:
                    self.copy(item, way, 0).wait_recv()
                    columns = self.columns(item, way)
                    leaving[way, 1, :, columns] = (
                        leaving[way, 1, :, columns].astype(full) + arrived[way, 0, :, columns].astype(full)
                    ).astype(leaving.dtype)
                self.copy(item, way, step).start()

    def finish(self, item):
        value, arrived, _, _ = self.items[item]
        total = value(lax.axis_index("seq"))
        for way in range(2):
            self.copy(item, way, self.half - 1).wait_recv()
            total = total + arrived[way, self.half - 1].astype(full)
        return total

    def drain(self):
        for item, (_, _, _, ways) in enumerate(self.items):
            for way in range(2):
                for step in range(self.half - 2, self.half):
                    if step > 0 or way in ways:
                        self.copy(item, way, step).wait_send()


def feed_kernel(
    count, width, own, w_both_far, w_down_far, cotangent, total, feed_sum, down_own, down_others, hidden_far,
    w_both, w_down, hidden, feed, d_both, cot_rows, down_total, feed_others, feed_in, late_sem, cot_sem, cross_out,
    cross_in, *rest
):
    gather_sems, rest = rest[:4], rest[4:]
    ring_refs, ring_sems = rest[:5], rest[5:]
    half, chips = count // 2, width // CORES
    far = count - 1
    block, depth = own.shape
    units = w_down.shape[0]
    slice_f = units // chips
    tokens = count * 2 * block
    after, before = ring_sides(count)
    mate = core_mate()
    back, ahead = chip_mates(width), chip_mates(width, True)
    greet(after, before, mate, *back)
    gather = RingGather(count, own, feed, gather_sems, after, before, mate)
    ring = RingSum(count, ring_refs, ring_sems, after, before, mate)
    late = [
        pltpu.make_async_copy(w_both_far, w_both, late_sem.at[0]),
        pltpu.make_async_copy(w_down_far, w_down, late_sem.at[1]),
    ]
    save_hidden = pltpu.make_async_copy(hidden, hidden_far, late_sem.at[2])

    def cross(k):
        sems = (cross_out.at[k], cross_in.at[k])
        return send(feed_others.at[k - 1], feed_in.at[k - 1], sems, ahead[k - 1])

    def fetch(slot):
        return pltpu.make_async_copy(cotangent.at[slot], cot_rows.at[slot % 2], cot_sem.at[slot % 2])

    def fetched(slot):
        fetch(slot).wait()

        @pl.when(slot < far)
        def _():
            fetch(slot + 1).start()

        return cot_rows[slot % 2].reshape(2 * block, depth)

    def work(slot):
        back_all = lax.dot_general(fetched(slot), w_down[...], (NT, ((), ())), preferred_element_type=full)
        gather.to_mate(slot).wait_recv()
        rows = feed[slot].reshape(2 * block, depth)
        before_act = jnp.dot(rows, w_both[...], preferred_element_type=full)
        forth, back_parts = [], []
        for k in range(chips):
            start = 2 * k * slice_f
            gate, up = before_act[:, start : start + slice_f], before_act[:, start + slice_f : start + 2 * slice_f]
            active, slope = gelu_and_slope(gate)
            back = back_all[:, k * slice_f : (k + 1) * slice_f]
            forth.append(active * up)
            back_parts += [back * up * slope, back * active]
        hidden[slot] = jnp.concatenate(forth, axis=1).astype(low).reshape(2, block, units)
        d_rows = jnp.concatenate(back_parts, axis=1).astype(low)
        for k in range(chips):
            d_both[k, slot] = d_rows[:, 2 * k * slice_f : 2 * (k + 1) * slice_f].reshape(2, block, 2 * slice_f)
        part = lax.dot_general(d_rows, w_both[...], (NT, ((), ())), preferred_element_type=full)
        ring.offer(slot, part, slot >= ring.held)

    gather.start()
    for copy in late:
        copy.start()
    fetch(0).start()
    gather.hop(1, 0, half == 2)
    for copy in late:
        copy.wait()
    gather.hop(1, 1, half == 2)
    work(0)

    def advance(h, last):
        gather.hop(h, 0, last)
        work(2 * h - 3)
        gather.hop(h, 1, last)
        work(2 * h - 2)

    @pl.loop(2, half - 1)
    def _(h):
        advance(h, False)

    if half > 2:
        advance(half - 1, True)
    pl.loop(far - 2, far - 1)(work)
    gather.last()
    pl.loop(far - 1, far + 1)(work)
    save_hidden.start()

    pieces = 4
    wide = depth // pieces

    def grads(first, last):
        @pl.loop(first, last)
        def _(at):
            columns = pl.ds(pl.multiple_of((at % pieces) * wide, wide), wide)
            k = chips - 1 - at // pieces
            part = lax.dot_general(
                feed[:, :, :, columns].reshape(tokens, wide),
                d_both[k].reshape(tokens, 2 * slice_f),
                (TN, ((), ())),
                preferred_element_type=full,
            ).astype(low)

            @pl.when(k == 0)
            def _():
                feed_sum[columns] = part

            @pl.when(k > 0)
            def _():
                feed_others[jnp.maximum(k - 1, 0), columns] = part

    def down(slot):
        rows = fetched(slot)
        part = lax.dot_general(
            hidden[slot].reshape(2 * block, units), rows, (TN, ((), ())), preferred_element_type=full
        )

        @pl.when(slot == 0)
        def _():
            down_total[...] = part

        @pl.when(slot > 0)
        def _():
            down_total[...] += part

    fetch(0).start()
    ring.begin()
    ring.step(1, 0)
    grads(0, (chips - 1) * pieces)
    for k in range(1, chips):
        cross(k).start()
    ring.step(1, 1)
    steps = [(step, turn) for step in range(2, half) for turn in range(2)]
    ring_step = iter(steps)

    def next_step():
        for step, turn in [next(ring_step, (0, 0))]:
            if step > 0:
                ring.step(step, turn)

    next_step()
    grads((chips - 1) * pieces, chips * pieces)
    next_step()
    pl.loop(0, count // 2)(down)
    for _ in range(len(steps)):
        next_step()
    pl.loop(count // 2, count)(down)
    down_own[...] = down_total[:slice_f].astype(low)
    for k in range(1, chips):
        down_others[k - 1] = down_total[k * slice_f : (k + 1) * slice_f].astype(low)
    total[...] = ring.finish()
    for k in range(1, chips):
        cross(k).wait_recv()
    for at in range(pieces):
        rows = slice(at * wide, (at + 1) * wide)
        part = feed_sum[rows].astype(full)
        for k in range(1, chips):
            part = part + feed_in[k - 1, rows].astype(full)
        feed_sum[rows] = part.astype(low)
    save_hidden.wait()
    gather.drain()
    ring.drain()
    for k in range(1, chips):
        cross(k).wait_send()


def feed_forward(own, w_both, w_down, cotangent):
    count, width = lax.axis_size("seq"), lax.axis_size("dp")
    chips = width // CORES
    block, depth = own.shape
    units = w_down.shape[0]
    slice_f = units // chips
    whole = pl.BlockSpec(memory_space=pltpu.VMEM)
    dma = pltpu.SemaphoreType.DMA
    shapes = [
        ((block, depth), full), ((depth, 2 * slice_f), low), ((slice_f, depth), low),
        ((chips - 1, slice_f, depth), low), ((count, 2, block, units), low),
    ]
    far = pl.BlockSpec(memory_space=pl.ANY)
    return pl.pallas_call(
        partial(feed_kernel, count, width),
        in_specs=[whole, far, far, far],
        out_specs=[whole] * 4 + [far],
        out_shape=[jax.ShapeDtypeStruct(*shape) for shape in shapes],
        scratch_shapes=[
            pltpu.VMEM(w_both.shape, low),
            pltpu.VMEM(w_down.shape, low),
            pltpu.VMEM((count, 2, block, units), low),
            pltpu.VMEM((count, 2, block, depth), low),
            pltpu.VMEM((chips, count, 2, block, 2 * slice_f), low),
            pltpu.VMEM((2, 2, block, depth), low),
            pltpu.VMEM((units, depth), full),
            pltpu.VMEM((chips - 1, depth, 2 * slice_f), low),
            pltpu.VMEM((chips - 1, depth, 2 * slice_f), low),
            dma((3,)), dma((2,)), dma((chips,)), dma((chips,)),
            *RingGather.scratch(count),
            *RingSum.scratch(count, block, depth),
        ],
        compiler_params=pltpu.CompilerParams(collective_id=1, has_side_effects=True, vmem_limit_bytes=63 << 20),
        cost_estimate=pl.CostEstimate(
            flops=2 * 2 * count * block * depth * units * 9, bytes_accessed=40 << 20, transcendentals=0
        ),
    )(own, w_both, w_down, cotangent)


def seq_peer(count, step):
    place = lax.rem(lax.axis_index("seq") + (step + count), count)
    return {"seq": place}, place


def keep_column(marks, row):
    mark = jnp.broadcast_to(marks[row, :1], marks.shape[1:])
    padding = jnp.where(mark > 1.5, 1.0, 0.0)
    keep = 1.0 - (mark - 2.0 * padding)
    return jnp.transpose(keep)[:, :1], jnp.transpose(1.0 - padding)[:, :1]


def gate_terms(pre_rate, pre_inlet, soft):
    rate, inlet = jax.nn.sigmoid(pre_rate), jax.nn.sigmoid(pre_inlet)
    twice = -16.0 * rate * soft
    decay = jnp.exp(0.5 * twice)
    near = -twice * (
        1.0 + twice * (1 / 2 + twice * (1 / 6 + twice * (1 / 24 + twice * (1 / 120 + twice * (1 / 720)))))
    )
    rest = jnp.where(twice > -0.25, near, 1.0 - decay * decay)
    return rate, inlet, decay, rest, jnp.sqrt(rest)


def scan_rows(rate, value, backward):
    length, channels = rate.shape
    groups = length // 8
    rate = rate.reshape(groups, 8, channels)
    value = value.reshape(groups, 8, channels)
    place = lax.broadcasted_iota(jnp.int32, rate.shape, 1)
    for step in (1, 2, 4):
        keep = place < 8 - step if backward else place >= step
        move = 8 - step if backward else step
        earlier_rate = jnp.where(keep, pltpu.roll(rate, move, 1), 1.0)
        earlier_value = jnp.where(keep, pltpu.roll(value, move, 1), 0.0)
        value = value + rate * earlier_value
        rate = rate * earlier_rate
    product_in = jnp.ones((1, channels), full)
    state_in = jnp.zeros((1, channels), full)
    end = 0 if backward else 7
    products, states = [None] * groups, [None] * groups
    for group in reversed(range(groups)) if backward else range(groups):
        states[group] = value[group] + rate[group] * state_in
        products[group] = rate[group] * product_in
        product_in, state_in = products[group][end : end + 1], states[group][end : end + 1]
    return jnp.concatenate(products, axis=0), jnp.concatenate(states, axis=0)


def fold_states(count, arrived, backward):
    mine = lax.axis_index("seq")
    total = jnp.zeros(arrived.shape[2:], full)
    scale = jnp.ones(arrived.shape[2:], full)
    for step in range(1, count):
        there = (mine + step < count) if backward else (mine >= step)
        total = total + jnp.where(there, scale * arrived[step, 1], 0.0)
        scale = scale * arrived[step, 0]
    return total


def stack_rows(ref):
    pieces, rows, columns = ref.shape
    if rows % 16 == 0:
        return ref[...].reshape(pieces * rows, columns)
    return jnp.concatenate([ref[piece].astype(full) for piece in range(pieces)], axis=0).astype(ref.dtype)


def tail_factor(column, taps):
    length = column.shape[0]
    place = lax.broadcasted_iota(jnp.int32, (8, 1), 0)
    factor, run = jnp.where(place == 7, 1.0, 0.0), jnp.ones((1, 1), full)
    for back in range(1, taps - 1):
        run = run * column[length - back : length - back + 1]
        factor = jnp.where(place == 7 - back, run, factor)
    return factor


def front_kernel(
    count, width, own, cot_raw, resets, real_mask, gain_mix, gain_mlp, conv_kernel, decay_param, gate_rate, gate_input,
    w_gate, w_x, w_mix, w_feed_gate, w_feed_up, w_down,
    marks_all, w_both, gains, chan, cotangent, middle, feed_own, halo, ends, cot_all, down_all,
    gate_far, x_far, normed_far, pre_gate_far, branch_far, w_mix_far, conv_far, pre_rate_far, pre_inlet_far, rate_far,
    inlet_far, states_far, mixed_far,
    gate_all, x_all, normed, pre_gate, branch, w_mix_all, conv_low, pre_rate, pre_inlet, rate_mat, inlet_mat, states,
    mixed, save_sem, own_marks, small, small_all, own_gates, gates_all, mix_all, rows_all, x_total, scale, turned, arrived,
    keep, product, state, ext, halo_out, halo_in, state_out, state_all, core_out, core_in, chip_out, chip_in,
    ring_out, ring_in, last_out, last_in, rows_out, rows_in, mate_out, mate_in, cross_out, cross_in, down_out, down_in,
    halo_sem, state_out_sem, state_in_sem, core_out_sem, core_in_sem, chip_out_sem, chip_in_sem, cot_sem, *rest
):
    gather_sems, turn_refs = rest[:4], rest[4:]
    half = count // 2
    chips = width // CORES
    block, depth = own.shape
    shard, channels = w_gate.shape
    own_channels, size = gate_rate.shape
    taps = conv_kernel.shape[0]
    slice_f = w_down.shape[0]
    mine = lax.axis_index("seq")
    after, before = ring_sides(count)
    mate = core_mate()
    back, ahead = chip_mates(width), chip_mates(width, True)
    peers = [None] + [seq_peer(count, step)[0] for step in range(1, count)]
    greet(mate, *back, *peers[1:])
    gather = RingGather(count, cotangent, cot_all, gather_sems, after, before, mate, cot_sem.at[0])
    turn = RingTurn(count, turned, arrived.at[0], turn_refs[0], turn_refs[1:], after, before)
    saves = [
        pltpu.make_async_copy(source, target, save_sem.at[at])
        for at, (source, target) in enumerate(
            (
                (gate_all, gate_far), (x_all, x_far), (normed, normed_far), (pre_gate, pre_gate_far),
                (branch, branch_far), (w_mix_all, w_mix_far), (conv_low, conv_far), (pre_rate, pre_rate_far),
                (pre_inlet, pre_inlet_far), (rate_mat, rate_far), (inlet_mat, inlet_far), (states, states_far),
                (mixed, mixed_far), (w_down, down_all.at[0]),
            )
        )
    ]
    moved = ((w_gate, gate_all), (small, small_all), (w_x, x_all), (own_gates, gates_all), (w_mix, mix_all))
    shared = ((0,), (0,), (1,), (1,), (0, 1))

    def rows_copy(what, k):
        source, target = ((own, rows_all), (own_marks, marks_all))[what]
        return send(source, target.at[k], (rows_out.at[what, k], rows_in.at[what, k]), back[k - 1])

    def mate_copy(what, k):
        source, target = ((own, rows_all), (own_marks, marks_all))[what]
        source = source if k == 0 else target.at[k]
        return send(source, target.at[chips + k], (mate_out.at[what, k], mate_in.at[what, k]), mate)

    def ring_copy(way, hop, item):
        source, target = moved[item]
        index = mine if hop == 1 else ring_index(count, (1 - hop) if way == 0 else (hop - 1))
        return send(
            source if hop == 1 else target.at[index],
            target.at[index],
            (ring_out.at[way, hop, item], ring_in.at[way, hop, item]),
            after if way == 0 else before,
        )

    def last_copy(way, item):
        index = ring_index(count, (1 - half) if way == 0 else (half - 1))
        ref = moved[item][1].at[index]
        if len(shared[item]) == 2:
            ref = ref.at[:, pl.ds(way * (depth // 2), depth // 2)]
        return send(ref, ref, (last_out.at[way, item], last_in.at[way, item]), after if way == 0 else before)

    def cross(slot, k):
        offset = half if slot == count - 1 else (slot + 1) // 2 * (1 - 2 * (slot % 2))
        origin = ring_index(count, offset)
        sems = (cross_out.at[k, slot], cross_in.at[k, slot])
        return send(arrived.at[0, origin], arrived.at[k, origin], sems, back[k - 1])

    def cross_down(k):
        return send(w_down, down_all.at[k], (down_out.at[k], down_in.at[k]), back[k - 1])

    def halo_copy():
        return send(halo_out, halo_in, (halo_sem.at[0], halo_sem.at[1]), peers[1])

    def state_copy(step):
        return send(state_out, state_all.at[step], (state_out_sem.at[step], state_in_sem.at[step]), peers[step])

    def core_copy(k):
        return send(core_out.at[k], core_in.at[k], (core_out_sem.at[k], core_in_sem.at[k]), mate)

    def chip_copy(k):
        return send(chip_out.at[k], chip_in.at[k], (chip_out_sem.at[k], chip_in_sem.at[k]), ahead[k - 1])

    def send_item(item):
        ring_copy(0, 1, item).start()
        ring_copy(1, 1, item).start()
        moved[item][1][mine] = moved[item][0][...]

    send_item(0)
    mate_copy(0, 0).start()
    for k in range(1, chips):
        rows_copy(0, k).start()
    real = real_mask[...].astype(full)
    own_marks[...] = jnp.broadcast_to(resets[...].astype(full) + 2.0 * (1.0 - real), own_marks.shape)
    mate_copy(1, 0).start()
    for k in range(1, chips):
        rows_copy(1, k).start()
    tap_rows = conv_kernel[...].astype(full)
    padding = jnp.zeros((1, shard - own_channels), full)
    pieces = [jnp.concatenate([tap_rows[tap : tap + 1], padding], axis=1) for tap in range(taps)]
    pieces.append(jnp.concatenate([decay_param[...].astype(full), padding], axis=1))
    pieces += [gain_mix[...].astype(full).reshape(1, shard), gain_mlp[...].astype(full).reshape(1, shard)]
    place = lax.broadcasted_iota(jnp.int32, (16, shard), 0)
    total = jnp.zeros((16, shard), full)
    for at, piece in enumerate(pieces):
        total = jnp.where(place == at, piece, total)
    small[...] = total.astype(low)
    send_item(1)
    send_item(2)
    own_gates[...] = jnp.concatenate([gate_rate[...].astype(full), gate_input[...].astype(full)], axis=1).astype(low)
    send_item(3)
    send_item(4)
    rows_all[0] = own[...]
    marks_all[0] = own_marks[...]
    _, real = keep_column(marks_all, 0)
    cotangent[...] = (cot_raw[...].astype(full) * real).astype(low)
    saves[13].start()
    for k in range(1, chips):
        cross_down(k).start()
    for k in range(1, chips):
        for what in range(2):
            rows_copy(what, k).wait_recv()
            mate_copy(what, k).start()
    for k in range(chips):
        for what in range(2):
            mate_copy(what, k).wait_recv()
    for row in range(width):
        values = rows_all[row].astype(full)
        scale[row] = lax.rsqrt(jnp.mean(values * values, axis=-1, keepdims=True) + epsilon)

    def work(index, first):
        columns = pl.ds(pl.multiple_of(index * shard, shard), shard)
        gain = small_all[index].astype(full)[taps + 1 : taps + 2]
        values = rows_all[:, :, columns].astype(full)
        part = (values * scale[...] * gain).astype(low).reshape(width * block, shard)
        normed[:, columns] = part
        for weight, target in ((gate_all, pre_gate), (x_all, x_total)):
            term = jnp.dot(part, weight[index], preferred_element_type=full).reshape(width, block, channels)
            if first:
                target[...] = term
            else:
                target[...] += term

    work(mine, True)
    for at in range(count):
        columns = slice(at * slice_f, (at + 1) * slice_f)
        turned[at] = jnp.concatenate(
            [w_feed_gate[:, columns].astype(full), w_feed_up[:, columns].astype(full)], axis=1
        ).astype(low)
    arrived[0, mine] = turned[mine]
    for k in range(1, chips):
        cross(0, k).start()
    for hop in range(1, half):
        for item in range(len(moved)):
            for way in range(2):
                ring_copy(way, hop, item).wait_recv()
                if hop < half - 1:
                    ring_copy(way, hop + 1, item).start()
                elif way in shared[item]:
                    last_copy(way, item).start()
            if item == 2:
                for way in range(2):
                    work(ring_index(count, -hop if way == 0 else hop), False)
    turn.start()
    gather.start()
    for item in range(3):
        last_copy(shared[item][0], item).wait_recv()
    work(ring_index(count, half), False)
    branch[...] = x_total[...].astype(low)
    for item in range(3, len(moved)):
        for way in shared[item]:
            last_copy(way, item).wait_recv()

    for row in range(width):
        column, _ = keep_column(marks_all, row)
        keep[row, :8] = jnp.ones((8, 1), full)
        keep[row, 8:] = column
        halo_out[row] = branch[row, block - 16 :].astype(full)[8:] * tail_factor(column, taps)
    halo_copy().start()
    entries = jnp.concatenate([small_all[at].astype(full)[:8, :own_channels] for at in range(count)], axis=1)
    place = lax.broadcasted_iota(jnp.int32, entries.shape, 0)
    decay_row = entries[taps : taps + 1]
    entries = jnp.where(place == taps, jax.nn.softplus(decay_row), entries)
    chan[...] = jnp.where(place == taps + 1, jax.nn.sigmoid(decay_row), entries)
    entries = jnp.concatenate([small_all[at].astype(full)[:8] for at in range(count)], axis=1)
    gains[...] = jnp.concatenate([entries[taps + 1 : taps + 3], jnp.zeros((6, depth), full)], axis=0)
    w_mix_all[...] = stack_rows(mix_all)
    for copy in saves[:6]:
        copy.start()
    entries = stack_rows(gates_all)
    for at in range(channels // size):
        rows = slice(at * size, (at + 1) * size)
        for target, first in ((rate_mat, 0), (inlet_mat, size)):
            parts = [entries[rows].astype(full)[:, first : first + size]]
            if at > 0:
                parts.insert(0, jnp.zeros((size, at * size), full))
            if at + 1 < channels // size:
                parts.append(jnp.zeros((size, channels - (at + 1) * size), full))
            target[rows] = jnp.concatenate(parts, axis=1).astype(low)

    halo_copy().wait_recv()
    soft = chan[taps : taps + 1]
    state_out[...] = jnp.zeros_like(state_out)

    @pl.loop(0, width)
    def _(row):
        from_before = jnp.where(mine > 0, halo_in[row], 0.0)
        halo[row] = from_before
        ext[:8] = from_before
        ext[8:] = branch[row].astype(full)
        valid = jnp.ones((block, 1), full)
        total = jnp.zeros((block, channels), full)
        for tap in range(taps):
            total = total + chan[tap : tap + 1] * valid * ext[8 - tap : 8 - tap + block]
            valid = valid * keep[row, 8 - tap : 8 - tap + block]
        conv = total.astype(low)
        conv_low[row] = conv
        rate_in = lax.dot_general(conv, rate_mat[...], (NT, ((), ())), preferred_element_type=full)
        inlet_in = lax.dot_general(conv, inlet_mat[...], (NT, ((), ())), preferred_element_type=full)
        pre_rate[row] = rate_in
        pre_inlet[row] = inlet_in
        _, inlet, decay, _, root = gate_terms(rate_in, inlet_in, soft)
        kept = keep[row, 8:]
        inflow = conv.astype(full) * inlet * ((1.0 - kept) + kept * root)
        row_product, row_state = scan_rows(decay * kept, inflow, False)
        product[row] = row_product
        state[row] = row_state
        state_out[0, pl.ds(row, 1)] = row_product[block - 1 :]
        state_out[1, pl.ds(row, 1)] = row_state[block - 1 :]

    for copy in saves[6:11]:
        copy.start()

    def background(h):
        turn.hop(h)
        for slot in (2 * h - 1, 2 * h) if h < half else (count - 1,):
            for k in range(1, chips):
                cross(slot, k).start()
        if h < half:
            gather.hop(h, 0, h == half - 1)
            gather.hop(h, 1, h == half - 1)
        else:
            gather.last()

    for step in range(1, count):
        state_copy(step).start()
    background(1)
    for step in range(1, count):
        state_copy(step).wait_recv()
    ends[0] = fold_states(count, state_all, False)
    ends[1] = state_out[0]

    def close(row):
        row_states = state[row] + product[row] * ends[0, pl.ds(row, 1)]
        states[row] = row_states
        active, _ = gelu_and_slope(pre_gate[row])
        row_mixed = (row_states * active).astype(low)
        mixed[row] = row_mixed
        return jnp.dot(row_mixed, w_mix_all[...], preferred_element_type=full)

    @pl.loop(0, chips)
    def _(at):
        k = chips - 1 - at
        core_out[k] = close(chips + k).astype(low)
        core_copy(k).start()

    @pl.loop(0, chips - 1)
    def _(at):
        k = chips - 1 - at
        part = close(k)
        core_copy(k).wait_recv()
        chip_out[k] = (part + core_in[k].astype(full)).astype(low)

    for k in range(chips - 1, 0, -1):
        chip_copy(k).start()
    part = close(0)
    background(2)
    core_copy(0).wait_recv()
    total = part + core_in[0].astype(full) + own[...].astype(full)
    for k in range(1, chips):
        chip_copy(k).wait_recv()
        total = total + chip_in[k].astype(full)
    for copy in saves[11:13]:
        copy.start()
    middle[...] = total
    scaled = total * lax.rsqrt(jnp.mean(total * total, axis=-1, keepdims=True) + epsilon)
    feed_own[...] = (scaled * gains[1:2]).astype(low)
    for h in range(3, half + 1):
        background(h)
    for k in range(chips):
        if k > 0:
            cross_down(k).wait_recv()
            for slot in range(count):
                cross(slot, k).wait_recv()
        w_both[:, 2 * k * slice_f : 2 * (k + 1) * slice_f] = arrived[k].reshape(depth, 2 * slice_f)
    for slot in range(count):
        gather.to_mate(slot).wait_recv()

    for copy in saves:
        copy.wait()
    for item in range(len(moved)):
        for way in range(2):
            for hop in range(1, half):
                ring_copy(way, hop, item).wait_send()
            if way in shared[item]:
                last_copy(way, item).wait_send()
    for what in range(2):
        for k in range(chips):
            mate_copy(what, k).wait_send()
        for k in range(1, chips):
            rows_copy(what, k).wait_send()
    for k in range(1, chips):
        cross_down(k).wait_send()
        chip_copy(k).wait_send()
        for slot in range(count):
            cross(slot, k).wait_send()
    for k in range(chips):
        core_copy(k).wait_send()
    for step in range(1, count):
        state_copy(step).wait_send()
    halo_copy().wait_send()
    turn.drain()
    gather.drain()


def forward(own, cotangent, resets, real_mask, *weights):
    conv_kernel, gate_rate, w_gate, w_mix, w_down = weights[2], weights[4], weights[6], weights[8], weights[11]
    count, width = lax.axis_size("seq"), lax.axis_size("dp")
    half, chips = count // 2, width // CORES
    block, depth = own.shape
    shard, part = w_gate.shape
    own_channels, size = gate_rate.shape
    channels = count * own_channels
    slice_f = w_down.shape[0]
    whole = pl.BlockSpec(memory_space=pltpu.VMEM)
    dma = pltpu.SemaphoreType.DMA
    rows = (width, block, channels)
    shapes = [
        ((width, 8, block), full), ((depth, 2 * chips * slice_f), low), ((8, depth), full), ((8, channels), full),
        ((block, depth), low), ((block, depth), full), ((block, depth), low), ((width, 8, channels), full),
        ((2, 8, channels), full), ((count, 2, block, depth), low), ((chips,) + w_down.shape, low),
    ]
    saved = [
        ((count, shard, part), low), ((count, shard, part), low), ((width * block, depth), low), (rows, full),
        (rows, low), ((channels, depth), low), (rows, low), (rows, full), (rows, full), ((channels, channels), low),
        ((channels, channels), low), (rows, full), (rows, low),
    ]
    return pl.pallas_call(
        partial(front_kernel, count, width),
        in_specs=[whole] * (4 + len(weights)),
        out_specs=[whole] * (len(shapes) - 2) + [pl.BlockSpec(memory_space=pl.ANY)] * (len(saved) + 2),
        out_shape=[jax.ShapeDtypeStruct(*shape) for shape in shapes + saved],
        scratch_shapes=[
            *[pltpu.VMEM(*shape) for shape in saved],
            dma((len(saved) + 1,)),
            pltpu.VMEM((8, block), full),
            pltpu.VMEM((16, shard), low),
            pltpu.VMEM((count, 16, shard), low),
            pltpu.VMEM((own_channels, 2 * size), low),
            pltpu.VMEM((count, own_channels, 2 * size), low),
            pltpu.VMEM((count,) + w_mix.shape, low),
            pltpu.VMEM((width, block, depth), low),
            pltpu.VMEM(rows, full),
            pltpu.VMEM((width, block, 1), full),
            pltpu.VMEM((count, shard, 2 * slice_f), low),
            pltpu.VMEM((chips, count, shard, 2 * slice_f), low),
            pltpu.VMEM((width, 8 + block, 1), full),
            pltpu.VMEM(rows, full),
            pltpu.VMEM(rows, full),
            pltpu.VMEM((8 + block, channels), full),
            pltpu.VMEM((width, 8, channels), full),
            pltpu.VMEM((width, 8, channels), full),
            pltpu.VMEM((2, 8, channels), full),
            pltpu.VMEM((count, 2, 8, channels), full),
            *[pltpu.VMEM((chips, block, depth), low)] * 4,
            dma((2, half, 5)), dma((2, half, 5)), dma((2, 5)), dma((2, 5)),
            dma((2, chips)), dma((2, chips)), dma((2, chips)), dma((2, chips)),
            dma((chips, count)), dma((chips, count)), dma((chips,)), dma((chips,)),
            dma((2,)), dma((count,)), dma((count,)), dma((chips,)), dma((chips,)), dma((chips,)), dma((chips,)), dma((1,)),
            *RingGather.scratch(count),
            *RingTurn.scratch(count, shard, 2 * slice_f),
        ],
        compiler_params=pltpu.CompilerParams(collective_id=2, has_side_effects=True, vmem_limit_bytes=63 << 20),
        cost_estimate=pl.CostEstimate(
            flops=6 * width * block * depth * channels, bytes_accessed=60 << 20, transcendentals=0
        ),
    )(own, cotangent, resets, real_mask, *weights)


def back_kernel(
    count, width, taps, d_feed, middle, cotangent, gains, marks, chan, halo, ends, w_down,
    w_mix_far, mixed_far, rate_far, inlet_far, conv_far, down_far,
    pre_gate, pre_rate, pre_inlet, states, branch, hidden, down_others, feed_sum,
    output, d_middle, d_pre_gate, d_branch, grad_mix, gate_grads, small_grads, gain_share, down_sum, feed_gate, feed_up,
    w_mix, mixed, rate_mat, inlet_mat, conv_low, down_own, gate_rows, rate_rows, inlet_rows, state_rows, branch_rows,
    hidden_rows, keep, mix_rows, mix_grads, later, local, shift, ext, d_rate, d_inlet, sums, halo_out, halo_in,
    state_out, state_all, down_in, feed_parts, late_sem, row_sem, hidden_sem, *rest
):
    ring_refs, rest = rest[:5], rest[5:]
    ring_sems, rest = rest[:6], rest[6:]
    (arrived, leaving), mix_sems, rest = rest[:2], rest[2:4], rest[4:]
    halo_sem, state_out_sem, state_in_sem, chip_out, chip_in, mate_out, mate_in, cross_out, cross_in = rest[:9]
    turn_refs = rest[9:]
    half = count // 2
    chips = width // CORES
    far = count - 1
    block, depth = middle.shape
    channels = chan.shape[1]
    own_channels = channels // count
    size = gate_grads.shape[-1] // 2
    mine = lax.axis_index("seq")
    after, before = ring_sides(count)
    mate = core_mate()
    back, ahead = chip_mates(width), chip_mates(width, True)
    peers = [None] + [seq_peer(count, -step)[0] for step in range(1, count)]
    greet(mate, *back, *peers[1:])
    ring = RingSum(count, ring_refs, ring_sems, after, before, mate)
    items = [(lambda index: mix_grads[index].astype(full), arrived, leaving, (0, 1))]
    scatter = RingScatter(count, items, mix_sems, after, before)
    turn = RingTurn(count, feed_sum, feed_parts, turn_refs[0], turn_refs[1:], after, before)

    def chips_copy(k):
        return send(mix_rows.at[0], mix_rows.at[k], (chip_out.at[k], chip_in.at[k]), back[k - 1])

    def mate_copy(k):
        return send(mix_rows.at[k], mix_rows.at[chips + k], (mate_out.at[k], mate_in.at[k]), mate)

    def cross(k):
        return send(down_others.at[k - 1], down_in.at[k - 1], (cross_out.at[k], cross_in.at[k]), ahead[k - 1])

    late = [
        pltpu.make_async_copy(source, target, late_sem.at[at])
        for at, (source, target) in enumerate(
            (
                (mixed_far, mixed), (w_mix_far, w_mix), (rate_far, rate_mat), (inlet_far, inlet_mat),
                (conv_far, conv_low), (down_far, down_own), (feed_sum.at[mine], feed_parts.at[mine]),
            )
        )
    ]
    streams = (
        ((pre_gate, gate_rows), (pre_rate, rate_rows), (states, state_rows)),
        ((pre_rate, rate_rows), (pre_inlet, inlet_rows), (states, state_rows), (branch, branch_rows)),
    )

    def row_copies(which, row):
        return [
            pltpu.make_async_copy(source.at[row], target.at[row % 2], row_sem.at[at, row % 2])
            for at, (source, target) in enumerate(streams[which])
        ]

    def row_start(which, row):
        for copy in row_copies(which, row):
            copy.start()

    def row_ready(which, row):
        for copy in row_copies(which, row):
            copy.wait()

        @pl.when(row + 1 < width)
        def _():
            row_start(which, row + 1)

        return row % 2

    def halo_copy():
        return send(halo_out, halo_in, (halo_sem.at[0], halo_sem.at[1]), peers[1])

    def state_copy(step):
        return send(state_out, state_all.at[step], (state_out_sem.at[step], state_in_sem.at[step]), peers[step])

    def fetch(at):
        return pltpu.make_async_copy(hidden.at[far - at], hidden_rows.at[at % 2], hidden_sem.at[at % 2])

    fetch(0).start()
    for copy in late:
        copy.start()
    row_start(0, 0)
    turn.start()

    values, arriving = middle[...], d_feed[...]
    scale = lax.rsqrt(jnp.mean(values * values, axis=-1, keepdims=True) + epsilon)
    normed = values * scale
    scaled = arriving * gains[1:2]
    gain_share[...] = jnp.sum(arriving * normed, axis=0, keepdims=True)
    total = cotangent[...].astype(full) + scale * (
        scaled - normed * jnp.mean(scaled * normed, axis=-1, keepdims=True)
    )
    d_middle[...] = total
    mix_rows[0] = total.astype(low)
    for k in range(1, chips):
        chips_copy(k).start()
    mate_copy(0).start()

    def offer(at):
        slot = far - at
        fetch(at).wait()

        @pl.when(at < far)
        def _():
            fetch(at + 1).start()

        rows = hidden_rows[at % 2].reshape(2 * block, hidden.shape[-1])
        ring.offer(slot, jnp.dot(rows, w_down[...], preferred_element_type=full), at >= ring.held)

    pl.loop(0, 3)(offer)
    ring.begin()
    ring.step(1, 0)
    pl.loop(3, count)(offer)
    for k in range(1, chips):
        chips_copy(k).wait_recv()
        mate_copy(k).start()
    for k in range(1, chips):
        cross(k).start()
    ring.step(1, 1)
    turn.hop(1)
    for copy in late[:2]:
        copy.wait()
    for k in range(chips):
        mate_copy(k).wait_recv()
    tokens = width * block
    rows = mixed[...].reshape(tokens, channels)
    wide = depth // 4
    for at in range(4):
        part = lax.dot_general(
            rows,
            mix_rows[:, :, at * wide : (at + 1) * wide].reshape(tokens, wide),
            (TN, ((), ())),
            preferred_element_type=full,
        )
        for piece in range(count):
            mix_grads[piece, :, at * wide : (at + 1) * wide] = part[
                piece * own_channels : (piece + 1) * own_channels
            ].astype(low)
    scatter.begin()

    soft, soft_slope = chan[taps : taps + 1], chan[taps + 1 : taps + 2]
    state_out[0] = ends[1]
    state_out[1] = jnp.zeros_like(ends[1])
    sums[...] = jnp.zeros_like(sums)

    def adjoint_row(row):
        at = row_ready(0, row)
        column, real = keep_column(marks, row)
        keep[row, :8] = jnp.ones((8, 1), full)
        keep[row, 8:] = column
        sums[taps + 2 : taps + 3] += jnp.sum(real)
        d_mixed = lax.dot_general(mix_rows[row], w_mix[...], (NT, ((), ())), preferred_element_type=full)
        active, slope = gelu_and_slope(gate_rows[at])
        d_pre_gate[row] = (d_mixed * state_rows[at] * slope).astype(low)
        decay = jnp.exp(-8.0 * jax.nn.sigmoid(rate_rows[at]) * soft)
        sums[taps + 1 : taps + 2] += jnp.sum(decay * real, axis=0, keepdims=True)
        shift[:block] = decay * column
        shift[block:] = jnp.ones((8, channels), full)
        row_later, row_local = scan_rows(shift[1 : block + 1], d_mixed * active, True)
        later[row] = row_later
        local[row] = row_local
        state_out[1, pl.ds(row, 1)] = shift[:1] * row_local[:1]

    if half > 2:
        ring.step(2, 0)
    pl.loop(0, width // 2)(adjoint_row)
    if half > 2:
        ring.step(2, 1)
    pl.loop(width // 2, width)(adjoint_row)
    row_start(1, 0)
    for step in range(1, count):
        state_copy(step).start()
    turn.hop(2)
    scatter.onward(1)
    for copy in late[2:]:
        copy.wait()
    for step in range(1, count):
        state_copy(step).wait_recv()
    sums[8:16] = fold_states(count, state_all, True)

    def gate_row(row):
        at = row_ready(1, row)
        column = keep[row, 8:]
        rate, inlet, decay, _, root = gate_terms(rate_rows[at], inlet_rows[at], soft)
        conv = conv_low[row].astype(full)
        adjoint = local[row] + later[row] * sums[pl.ds(8 + row, 1)]
        shift[:8] = jnp.broadcast_to(ends[0, pl.ds(row, 1)], (8, channels))
        shift[8:] = state_rows[at]
        previous = shift[7 : 7 + block]
        mult = (1.0 - column) + column * root
        d_log = adjoint * column * (decay * previous - conv * inlet * decay * decay / root)
        rate_part = (d_log * (-8.0 * soft) * rate * (1.0 - rate)).astype(low)
        inlet_part = (adjoint * conv * mult * inlet * (1.0 - inlet)).astype(low)
        d_rate[row] = rate_part
        d_inlet[row] = inlet_part
        sums[taps : taps + 1] += jnp.sum(d_log * (-8.0 * rate), axis=0, keepdims=True) * soft_slope
        through = (
            adjoint * inlet * mult
            + jnp.dot(rate_part, rate_mat[...], preferred_element_type=full)
            + jnp.dot(inlet_part, inlet_mat[...], preferred_element_type=full)
        )
        ext[:8] = halo[row]
        ext[8:] = branch_rows[at].astype(full)
        place = lax.broadcasted_iota(jnp.int32, (8, 1), 0)
        valid = jnp.ones((block, 1), full)
        branch_part = jnp.zeros((block, channels), full)
        tail = jnp.zeros((8, channels), full)
        for tap in range(taps):
            moved = valid * through
            sums[tap : tap + 1] += jnp.sum(moved * ext[8 - tap : 8 - tap + block], axis=0, keepdims=True)
            moved = moved * chan[tap : tap + 1]
            if tap == 0:
                branch_part = moved
            else:
                shift[:block] = moved
                shift[block:] = jnp.zeros((8, channels), full)
                branch_part = branch_part + shift[tap : tap + block]
                for j in range(1, tap + 1):
                    tail = tail + jnp.where(place == 8 - j, moved[tap - j : tap - j + 1], 0.0)
            valid = valid * keep[row, 8 - tap : 8 - tap + block]
        local[row] = branch_part
        halo_out[row] = tail

    pl.loop(0, width // 2)(gate_row)
    for step in range(3, half):
        ring.step(step, 0)
        ring.step(step, 1)
    if half > 2:
        scatter.onward(2)
        turn.hop(3)
    pl.loop(width // 2, width)(gate_row)
    halo_copy().start()
    rows = conv_low[...].reshape(tokens, channels)
    both = [
        lax.dot_general(part[...].reshape(tokens, channels), rows, (TN, ((), ())), preferred_element_type=full)
        for part in (d_rate, d_inlet)
    ]
    for piece in range(count):
        first = piece * own_channels
        at = first // size * size
        gate_grads[piece] = jnp.concatenate(
            [part[first : first + own_channels, at : at + size] for part in both], axis=1
        ).astype(low)
    halo_copy().wait_recv()

    @pl.loop(0, width)
    def _(row):
        column = keep[row, 8:]
        arriving = jnp.where(mine < count - 1, halo_in[row] * tail_factor(column, taps), 0.0)
        local[row, block - 8 :] += arriving
        d_branch[row] = local[row].astype(low)

    for piece in range(count):
        entries = sums[:8, piece * own_channels : (piece + 1) * own_channels]
        small_grads[piece] = jnp.concatenate([entries, jnp.zeros((8, 128 - own_channels), full)], axis=1)
    for step in range(3, half):
        scatter.onward(step)
        turn.hop(step + 1)
    total = down_own[...].astype(full)
    for k in range(1, chips):
        cross(k).wait_recv()
        total = total + down_in[k - 1].astype(full)
    down_sum[...] = total
    _, real = keep_column(marks, 0)
    output[...] = ((middle[...] + ring.finish()) * real).astype(low)

    wide = feed_parts.shape[-1] // 2
    for target, columns in ((feed_gate, slice(0, wide)), (feed_up, slice(wide, 2 * wide))):
        parts = [feed_parts[at].astype(full)[:, columns] for at in range(count)]
        target[...] = jnp.concatenate(parts, axis=1).astype(low)
    grad_mix[...] = scatter.finish(0)
    ring.drain()
    scatter.drain()
    turn.drain()
    halo_copy().wait_send()
    for step in range(1, count):
        state_copy(step).wait_send()
    for k in range(chips):
        mate_copy(k).wait_send()
    for k in range(1, chips):
        chips_copy(k).wait_send()
        cross(k).wait_send()


def mix_back(taps, size, near, late, rows, hidden, down_others, feed_sum):
    (d_feed, middle, _, _, _, chan, *_) = near
    count, width = lax.axis_size("seq"), lax.axis_size("dp")
    chips = width // CORES
    block, depth = middle.shape
    channels = chan.shape[1]
    own_channels = channels // count
    whole = pl.BlockSpec(memory_space=pltpu.VMEM)
    far = pl.BlockSpec(memory_space=pl.ANY)
    dma = pltpu.SemaphoreType.DMA
    all_rows = (width, block, channels)
    shapes = [
        ((block, depth), low), ((block, depth), full), (all_rows, low), (all_rows, low),
        ((own_channels, depth), full), ((count, own_channels, 2 * size), low), ((count, 8, 128), full),
        ((1, depth), full), (late[-1].shape, full),
        *[((feed_sum.shape[1], feed_sum.shape[2] // 2 * count), low)] * 2,
    ]
    operands = (*near, *late, *rows, hidden, down_others, feed_sum)
    return pl.pallas_call(
        partial(back_kernel, count, width, taps),
        in_specs=[whole] * len(near) + [far] * (len(operands) - len(near)),
        out_specs=[whole] * len(shapes),
        out_shape=[jax.ShapeDtypeStruct(*shape) for shape in shapes],
        scratch_shapes=[
            *[pltpu.VMEM(each.shape, each.dtype) for each in (late[0], late[1], *late[2:])],
            *[pltpu.VMEM((2,) + each.shape[1:], each.dtype) for each in (*rows, hidden)],
            pltpu.VMEM((width, 8 + block, 1), full),
            pltpu.VMEM((width, block, depth), low),
            pltpu.VMEM((count, own_channels, depth), low),
            pltpu.VMEM(all_rows, full),
            pltpu.VMEM(all_rows, full),
            pltpu.VMEM((block + 8, channels), full),
            pltpu.VMEM((block + 8, channels), full),
            pltpu.VMEM(all_rows, low),
            pltpu.VMEM(all_rows, low),
            pltpu.VMEM((16, channels), full),
            pltpu.VMEM((width, 8, channels), full),
            pltpu.VMEM((width, 8, channels), full),
            pltpu.VMEM((2, 8, channels), full),
            pltpu.VMEM((count, 2, 8, channels), full),
            pltpu.VMEM(down_others.shape, low),
            pltpu.VMEM(feed_sum.shape, low),
            dma((len(late) + 1,)), dma((4, 2)), dma((2,)),
            *RingSum.scratch(count, block, depth),
            *RingScatter.scratch(count, [((own_channels, depth), low)]),
            dma((2,)), dma((count,)), dma((count,)), dma((chips,)), dma((chips,)), dma((chips,)), dma((chips,)),
            dma((chips,)), dma((chips,)),
            *RingTurn.scratch(count, *feed_sum.shape[1:]),
        ],
        compiler_params=pltpu.CompilerParams(collective_id=4, has_side_effects=True, vmem_limit_bytes=63 << 20),
        cost_estimate=pl.CostEstimate(
            flops=4 * width * block * channels * (depth + 2 * channels), bytes_accessed=60 << 20, transcendentals=0
        ),
    )(*operands)


def close_kernel(
    count, width, own, d_middle, gains, gain_share, normed, d_pre_gate, d_branch, gate_grads, small_grads,
    w_gate_far, w_x_far, d_inputs, out_gate, out_x, out_gates, out_small, out_gains, w_gate, w_x, late_sem, *rest
):
    travel, rest = rest[:10], rest[10:]
    core_out, core_in, chip_out, chip_in, gain_out, gain_width, gain_total, gain_seq = rest[:8]
    core_out_sem, core_in_sem, chip_out_sem, chip_in_sem, width_out, width_in, seq_out, seq_in = rest[8:16]
    half = count // 2
    chips = width // CORES
    block, depth = own.shape
    shard = out_gate.shape[0]
    share = depth // width
    my_width = lax.axis_index("dp")
    after, before = ring_sides(count)
    mate = core_mate()
    ahead = chip_mates(width, True)
    peers = [None] + [seq_peer(count, step) for step in range(1, count)]
    others = [None] + [lax.rem(my_width + step, width) for step in range(1, width)]
    greet(*[peer for peer, _ in peers[1:]], *[{"dp": place} for place in others[1:]])

    def product(grads):
        def at(index):
            columns = pl.ds(pl.multiple_of(index * shard, shard), shard)
            return lax.dot_general(normed[:, columns], grads[...], (TN, ((), ())), preferred_element_type=full)

        return at

    def stored(grads):
        return lambda index: grads[index].astype(full)

    values = (product(d_pre_gate), product(d_branch), stored(gate_grads), stored(small_grads))
    results = (out_gate, out_x, out_gates, out_small)
    items = list(zip(values, travel[:4], travel[4:8], ((0,), (1,), (1,), (0,))))
    scatter = RingScatter(count, items, travel[8:], after, before)

    late = [
        pltpu.make_async_copy(source, target, late_sem.at[at])
        for at, (source, target) in enumerate(((w_gate_far, w_gate), (w_x_far, w_x)))
    ]

    def core_copy(k):
        return send(core_out.at[k], core_in.at[k], (core_out_sem.at[k], core_in_sem.at[k]), mate)

    def chip_copy(k):
        return send(chip_out.at[k], chip_in.at[k], (chip_out_sem.at[k], chip_in_sem.at[k]), ahead[k - 1])

    def width_copy(step):
        columns = pl.ds(pl.multiple_of(others[step] * share, share), share)
        sems = (width_out.at[step], width_in.at[step])
        return send(gain_out.at[:, columns], gain_width.at[step], sems, {"dp": others[step]})

    def seq_copy(step):
        return send(gain_total, gain_seq.at[step], (seq_out.at[step], seq_in.at[step]), peers[step][0])

    def through(row):
        return lax.dot_general(
            d_pre_gate[pl.ds(pl.multiple_of(row * block, block), block)],
            w_gate[...],
            (NT, ((), ())),
            preferred_element_type=full,
        ) + lax.dot_general(
            d_branch[pl.ds(pl.multiple_of(row * block, block), block)],
            w_x[...],
            (NT, ((), ())),
            preferred_element_type=full,
        )

    scatter.begin()
    for copy in late:
        copy.start()
    for copy in late:
        copy.wait()

    @pl.loop(0, chips)
    def _(at):
        k = chips - 1 - at
        core_out[k] = through(chips + k).astype(low)
        core_copy(k).start()

    scatter.onward(1)

    @pl.loop(0, chips - 1)
    def _(at):
        k = chips - 1 - at
        part = through(k)
        core_copy(k).wait_recv()
        chip_out[k] = (part + core_in[k].astype(full)).astype(low)

    for k in range(chips - 1, 0, -1):
        chip_copy(k).start()
    part = through(0)
    core_copy(0).wait_recv()
    total = part + core_in[0].astype(full)
    for k in range(1, chips):
        chip_copy(k).wait_recv()
        total = total + chip_in[k].astype(full)
    rows = own[...].astype(full)
    scale = lax.rsqrt(jnp.mean(rows * rows, axis=-1, keepdims=True) + epsilon)
    rows = rows * scale
    scaled = total * gains[:1]
    d_inputs[...] = (
        d_middle[...] + scale * (scaled - rows * jnp.mean(scaled * rows, axis=-1, keepdims=True))
    ).astype(low)
    gain_out[...] = jnp.zeros_like(gain_out)
    gain_out[:1] = jnp.sum(total * rows, axis=0, keepdims=True)
    gain_out[1:2] = gain_share[...]
    for step in range(1, width):
        width_copy(step).start()
    if half > 2:
        scatter.onward(2)
    columns = pl.ds(pl.multiple_of(my_width * share, share), share)
    gain_sum = gain_out[:, columns]
    for step in range(1, width):
        width_copy(step).wait_recv()
        gain_sum = gain_sum + gain_width[step]
    gain_total[...] = gain_sum
    for step in range(1, count):
        seq_copy(step).start()
    for step in range(3, half):
        scatter.onward(step)
    for step in range(1, count):
        seq_copy(step).wait_recv()
        gain_sum = gain_sum + gain_seq[step]
    out_gains[...] = gain_sum
    for item, result in enumerate(results):
        result[...] = scatter.finish(item)
    scatter.drain()
    for step in range(1, count):
        seq_copy(step).wait_send()
    for step in range(1, width):
        width_copy(step).wait_send()
    for k in range(chips):
        core_copy(k).wait_send()
    for k in range(1, chips):
        chip_copy(k).wait_send()


def close(operands):
    own, _, _, _, normed, d_pre_gate, _, gate_grads, small_grads, w_gate, w_x = operands
    count, width = lax.axis_size("seq"), lax.axis_size("dp")
    chips = width // CORES
    block, depth = own.shape
    channels = d_pre_gate.shape[1]
    shard, share = depth // count, depth // width
    whole = pl.BlockSpec(memory_space=pltpu.VMEM)
    dma = pltpu.SemaphoreType.DMA
    items = [
        ((shard, channels), low), ((shard, channels), low), (gate_grads.shape[1:], low), (small_grads.shape[1:], full),
    ]
    shapes = [
        ((block, depth), low), *[(shape, full) for shape, _ in items],
        ((8, share), full),
    ]
    return pl.pallas_call(
        partial(close_kernel, count, width),
        in_specs=[whole] * (len(operands) - 2) + [pl.BlockSpec(memory_space=pl.ANY)] * 2,
        out_specs=[whole] * len(shapes),
        out_shape=[jax.ShapeDtypeStruct(*shape) for shape in shapes],
        scratch_shapes=[
            *[pltpu.VMEM(each.shape, low) for each in (w_gate, w_x)],
            dma((2,)),
            *RingScatter.scratch(count, items),
            *[pltpu.VMEM((chips, block, depth), low)] * 4,
            pltpu.VMEM((8, depth), full),
            pltpu.VMEM((width, 8, share), full),
            pltpu.VMEM((8, share), full),
            pltpu.VMEM((count, 8, share), full),
            dma((chips,)), dma((chips,)), dma((chips,)), dma((chips,)),
            dma((width,)), dma((width,)), dma((count,)), dma((count,)),
        ],
        compiler_params=pltpu.CompilerParams(collective_id=5, has_side_effects=True, vmem_limit_bytes=63 << 20),
        cost_estimate=pl.CostEstimate(
            flops=8 * normed.shape[0] * depth * channels, bytes_accessed=40 << 20, transcendentals=0
        ),
    )(*operands)


def lay_out_kernel(count, taps, *refs):
    for source, target in zip(refs[:8], refs[11:19]):
        target[...] = source[...].astype(target.dtype)
    gates, small, gains = refs[8:11]
    taps_out, rate_out, input_out, decay_out, log_out, mix_out, mlp_out = refs[19:]
    size = rate_out.shape[1]
    channels, share = decay_out.shape[1], mix_out.shape[1]
    rate_out[...] = gates[:, :size]
    input_out[...] = gates[:, size:]
    taps_out[...] = small[:taps, :channels]
    decay_out[...] = small[taps : taps + 1, :channels]
    log_out[...] = small[taps + 1 : taps + 2, :channels] / small[taps + 2 : taps + 3, :channels]
    mine = lax.axis_index("seq")
    total = jnp.zeros((8, share), full)
    for at in range(count):
        total = jnp.where(mine == at, gains[:, at * share : (at + 1) * share], total)
    mix_out[...] = total[:1]
    mlp_out[...] = total[1:2]


def lay_out(taps, arrays, gates, small, gains):
    count = lax.axis_size("seq")
    steps = 4

    def block(shape, by_rows):
        if by_rows:
            return pl.BlockSpec((shape[0] // steps, shape[1]), lambda at: (at, 0))
        return pl.BlockSpec((shape[0], shape[1] // steps), lambda at: (0, at))

    def whole(shape):
        return pl.BlockSpec(shape, lambda at: (0, 0))

    cuts = [block(array.shape, by_rows) for array, by_rows, _ in arrays]
    own_channels, both = gates.shape
    share = gains.shape[1] // count
    rest = [(taps, own_channels), (own_channels, both // 2), (own_channels, both // 2), (1, own_channels)]
    rest += [(1, own_channels), (1, share), (1, share)]
    return pl.pallas_call(
        partial(lay_out_kernel, count, taps),
        grid=(steps,),
        in_specs=cuts + [whole(each.shape) for each in (gates, small, gains)],
        out_specs=cuts + [whole(shape) for shape in rest],
        out_shape=[jax.ShapeDtypeStruct(array.shape, kind) for array, _, kind in arrays]
        + [jax.ShapeDtypeStruct(shape, full) for shape in rest],
        compiler_params=pltpu.CompilerParams(vmem_limit_bytes=63 << 20),
    )(*[array for array, _, _ in arrays], gates, small, gains)


def on_device(
    inputs,
    cotangent,
    resets,
    real_mask,
    gain_mix,
    w_branch_gate,
    w_branch_x,
    conv_kernel,
    gate_rate,
    gate_input,
    decay_param,
    w_mix_out,
    gain_mlp,
    w_mlp_gate,
    w_mlp_up,
    w_mlp_down,
):
    seq = lax.axis_size("seq")
    rows_own, length, depth = inputs.shape
    taps = conv_kernel.shape[1]
    block = rows_own * length
    tokens = block * lax.axis_size("dp")
    own_channels, size = gate_rate.shape
    shard, part_w = w_branch_x.shape
    rows = inputs.reshape(block, depth)
    (
        marks, w_both, gains, chan, cot_low, middle, feed_own, halo, ends, d_feed, w_down,
        w_gate_all, w_x_all, mixer_in, pre_gate, branch, w_mix_out, conv_low, pre_rate, pre_inlet, rate_mat, inlet_mat,
        states, mixed,
    ) = forward(
        rows, cotangent.reshape(block, depth), resets, real_mask, gain_mix, gain_mlp, conv_kernel.T,
        decay_param[None], gate_rate, gate_input, w_branch_gate, w_branch_x, w_mix_out, w_mlp_gate, w_mlp_up,
        w_mlp_down,
    )
    w_down = w_down.reshape(-1, depth)

    d_feed_own, feed_sum, down_own, down_others, hidden = feed_forward(feed_own, w_both, w_down, d_feed)

    (
        output, d_middle, d_pre_gate, d_branch, grad_mix_out, gate_grads, small_grads, gain_share, grad_down,
        feed_gate, feed_up,
    ) = mix_back(
        taps,
        size,
        (d_feed_own, middle, cot_low, gains, marks, chan, halo, ends, w_down),
        (w_mix_out, mixed, rate_mat, inlet_mat, conv_low, down_own),
        (pre_gate, pre_rate, pre_inlet, states, branch),
        hidden,
        down_others,
        feed_sum.reshape(seq, shard, -1),
    )

    grad_inputs, grad_gate, grad_x, grad_gates, grad_small, gains = close(
        (
            rows, d_middle, gains, gain_share, mixer_in, d_pre_gate.reshape(tokens, part_w),
            d_branch.reshape(tokens, part_w), gate_grads, small_grads, w_gate_all.reshape(depth, part_w),
            w_x_all.reshape(depth, part_w),
        )
    )
    (
        output, grad_inputs, grad_gate, grad_x, feed_gate, feed_up, grad_mix_out, grad_down,
        grad_taps, grad_rate, grad_input, grad_decay, decay_log, grad_gain_mix, grad_gain_mlp,
    ) = lay_out(
        taps,
        (
            (output, True, low), (grad_inputs, True, low), (grad_gate, True, full), (grad_x, True, full),
            (feed_gate, True, full), (feed_up, True, full), (grad_mix_out, False, full), (grad_down, False, full),
        ),
        grad_gates,
        grad_small,
        gains,
    )
    return (
        output[None],
        grad_inputs[None],
        grad_gain_mix[0],
        grad_gate,
        grad_x,
        grad_taps.T,
        grad_rate,
        grad_input,
        grad_decay[0],
        grad_mix_out,
        grad_gain_mlp[0],
        feed_gate,
        feed_up,
        grad_down,
        decay_log[0],
    )


def solution(mesh):
    placed = (
        P("dp", "seq", None),
        P("dp", "seq", None),
        P("dp", "seq"),
        P("dp", "seq"),
        P("seq"),
        P("seq", "dp"),
        P("seq", "dp"),
        P(("dp", "seq"), None),
        P(("dp", "seq"), None),
        P(("dp", "seq"), None),
        P(("dp", "seq")),
        P(("dp", "seq"), None),
        P("seq"),
        P("seq", "dp"),
        P("seq", "dp"),
        P(("dp", "seq"), None),
    )
    return jax.shard_map(
        on_device,
        mesh=mesh,
        in_specs=placed,
        out_specs=(
            P("dp", "seq", None),
            P("dp", "seq", None),
            P(("dp", "seq")),
            P("seq", "dp"),
            P("seq", "dp"),
            P(("dp", "seq"), None),
            P(("dp", "seq"), None),
            P(("dp", "seq"), None),
            P(("dp", "seq")),
            P(("dp", "seq"), None),
            P(("dp", "seq")),
            P("seq", "dp"),
            P("seq", "dp"),
            P(("dp", "seq"), None),
            P(("dp", "seq")),
        ),
        check_vma=False,
    )
```

```python
from functools import partial

import jax
import jax.numpy as jnp
from jax import lax
from jax.experimental import pallas as pl
from jax.experimental.pallas import tpu as pltpu
from jax.sharding import PartitionSpec as P

epsilon = 1e-06
low = jnp.bfloat16
full = jnp.float32
CORES = 2


def ring_of(count):
    deep = 4 if count % 4 == 0 else 1
    wide = count // deep
    walk = [(z, 0) for z in range(deep)]
    for turn, z in enumerate(reversed(range(deep))):
        across = list(range(1, wide))
        walk += [(z, y) for y in (across if turn % 2 == 0 else across[::-1])]
    return [z * wide + y for z, y in walk]


NT = ((1,), (1,))
TN = ((0,), (0,))


MESH = pl.DeviceIdType.MESH


def pick_from(table, index):
    found = table[0]
    for at in range(1, len(table)):
        found = jnp.where(index == at, table[at], found)
    return found


def ring_sides(count):
    ring = ring_of(count)
    place = {index: position for position, index in enumerate(ring)}
    mine = lax.axis_index("seq")
    after = pick_from([ring[(place[index] + 1) % count] for index in range(count)], mine)
    before = pick_from([ring[(place[index] - 1) % count] for index in range(count)], mine)
    return {"seq": after}, {"seq": before}


def core_mate():
    mine = lax.axis_index("dp")
    return {"dp": mine + 1 - 2 * lax.rem(mine, 2)}


def greet(*devices):
    barrier = pltpu.get_barrier_semaphore()
    for device in devices:
        pl.semaphore_signal(barrier, inc=1, device_id=device, device_id_type=MESH)
    return lambda: pl.semaphore_wait(barrier, len(devices))


def send(source, target, sems, device):
    return pltpu.make_async_remote_copy(
        src_ref=source, dst_ref=target, send_sem=sems[0], recv_sem=sems[1], device_id=device, device_id_type=MESH
    )


def gelu_and_slope(value):
    scale = 0.7978845608028654
    square = value * value
    bent = jnp.tanh(scale * value * (1.0 + 0.044715 * square))
    half = 0.5 * (1.0 + bent)
    slope = half + 0.5 * value * (1.0 - bent * bent) * (scale * (1.0 + 3.0 * 0.044715 * square))
    return value * half, slope


def ring_index(count, offset):
    ring = ring_of(count)
    place = {index: position for position, index in enumerate(ring)}
    mine = lax.axis_index("seq")
    return pick_from([ring[(place[index] + offset) % count] for index in range(count)], mine)


def chip_mates(width, ahead=False):
    chips = width // CORES
    mine = lax.axis_index("dp")
    return [{"dp": lax.rem(mine + (k if ahead else chips - k) * CORES, width)} for k in range(1, chips)]


class RingSum:
    def __init__(self, count, refs, sems, after, before, mate):
        self.half, self.far = count // 2, count - 1
        self.stash, self.core_out, self.core_in, self.right_in, self.left_in = refs
        self.core_sems, self.right_sems, self.left_sems = sems[0:2], sems[2:4], sems[4:6]
        self.after, self.before, self.mate = after, before, mate
        self.held = self.core_out.shape[0]
        self.block = self.stash.shape[1]
        self.cut = self.block // 2

    @staticmethod
    def scratch(count, block, depth):
        half = count // 2
        dma = pltpu.SemaphoreType.DMA
        return [
            pltpu.VMEM((count, block, depth), low),
            pltpu.VMEM((4, block, depth), low),
            pltpu.VMEM((count, block, depth), low),
            pltpu.VMEM((half, block, depth), low),
            pltpu.VMEM((half, block, depth), low),
            dma((4,)), dma((count,)), dma((half, 2)), dma((half, 2)), dma((half, 2)), dma((half, 2)),
        ]

    def core_copy(self, slot):
        place = slot % self.held
        sems = (self.core_sems[0].at[place], self.core_sems[1].at[slot])
        return send(self.core_out.at[place], self.core_in.at[slot], sems, self.mate)

    def rows(self, part):
        return pl.ds(part * self.cut, self.cut)

    def side_copy(self, way, slot, step, part):
        target, sems = ((self.right_in, self.right_sems), (self.left_in, self.left_sems))[way]
        sems = (sems[0].at[step, part], sems[1].at[step, part])
        rows = self.rows(part)
        return send(self.stash.at[slot, rows], target.at[step, rows], sems, (self.after, self.before)[way])

    def offer(self, slot, part, again):
        part = part.astype(low)
        self.stash[slot] = part[: self.block]

        @pl.when(again)
        def _():
            self.core_copy(slot).wait_send()

        self.core_out[slot % self.held] = part[self.block :]
        self.core_copy(slot).start()

    def begin(self):
        self.core_copy(self.far).wait_recv()
        for way in range(2):
            rows = self.rows(way)
            total = self.stash[self.far, rows].astype(full) + self.core_in[self.far, rows].astype(full)
            self.stash[self.far, rows] = total.astype(low)
            self.side_copy(way, self.far, 0, way).start()

    def step(self, step, turn):
        for way, arrived in ((0, self.right_in), (1, self.left_in)):
            slot = 2 * (self.half - step) - way
            part = 1 - way if turn == 0 else way
            rows = self.rows(part)
            if turn == 0:
                self.core_copy(slot).wait_recv()
            total = self.stash[slot, rows].astype(full) + self.core_in[slot, rows].astype(full)
            if step > 1 or turn == 1:
                self.side_copy(way, slot, step - 1, part).wait_recv()
                total = total + arrived[step - 1, rows].astype(full)
            self.stash[slot, rows] = total.astype(low)
            self.side_copy(way, slot, step, part).start()

    def finish(self):
        self.core_copy(0).wait_recv()
        total = self.stash[0].astype(full) + self.core_in[0].astype(full)
        last = self.half - 1
        for way in range(2):
            for part in range(2):
                self.side_copy(way, 0, last, part).wait_recv()
        return total + self.right_in[last].astype(full) + self.left_in[last].astype(full)

    def drain(self):
        for slot in range(self.held):
            self.core_copy(slot).wait_send()
        for way in range(2):
            self.side_copy(way, 0, 0, way).wait_send()
            for step in range(1, self.half):
                for part in range(2):
                    self.side_copy(way, 0, step, part).wait_send()


class RingGather:
    def __init__(self, count, own, found, sems, after, before, mate, keep_sem=None):
        self.half, self.far = count // 2, count - 1
        self.own, self.found, self.sems, self.keep_sem = own, found, sems, keep_sem
        self.after, self.before, self.mate = after, before, mate
        self.cut = own.shape[0] // 2

    @staticmethod
    def scratch(count):
        dma = pltpu.SemaphoreType.DMA
        return [dma((count, 2)), dma((count, 2)), dma((count,)), dma((count,))]

    def onward(self, way, slot, to, part):
        rows = pl.ds(part * self.cut, self.cut)
        source = self.own.at[rows] if slot is None else self.found.at[slot, 0, rows]
        sems = (self.sems[0].at[to, part], self.sems[1].at[to, part])
        return send(source, self.found.at[to, 0, rows], sems, (self.after, self.before)[way])

    def to_mate(self, slot):
        sems = (self.sems[2].at[slot], self.sems[3].at[slot])
        source = self.own if isinstance(slot, int) and slot == 0 else self.found.at[slot, 0]
        return send(source, self.found.at[slot, 1], sems, self.mate)

    def start(self):
        for turn in range(2):
            for way in range(2):
                self.onward(way, None, 1 + way, way if turn == 0 else 1 - way).start()
        self.to_mate(0).start()
        if self.keep_sem is None:
            self.found[0, 0] = self.own[...]
        else:
            self.keep().start()

    def keep(self):
        return pltpu.make_async_copy(self.own, self.found.at[0, 0], self.keep_sem)

    def hop(self, h, turn, last):
        for way in range(2):
            slot = 2 * h - 1 + way
            part = way if turn == 0 else 1 - way
            self.onward(way, slot, slot, part).wait_recv()
            if not last:
                self.onward(way, slot, slot + 2, part).start()
            elif turn == 0:
                self.onward(way, slot, self.far, part).start()
            if turn == 1:
                self.to_mate(slot).start()

    def last(self):
        for way in range(2):
            self.onward(way, self.far, self.far, way).wait_recv()
        self.to_mate(self.far).start()

    def drain(self):
        for slot in range(self.far + 1):
            self.to_mate(slot).wait_send()
        for slot in range(1, self.far + 1):
            for part in range(2):
                self.onward(0, self.far, slot, part).wait_send()
        if self.keep_sem is not None:
            self.keep().wait()


class RingTurn:
    def __init__(self, count, source, target, transit, sems, after, before):
        self.count, self.half = count, count // 2
        self.source, self.target, self.transit, self.sems = source, target, transit, sems
        self.after, self.before = after, before
        self.cut = source.shape[1] // 2

    @staticmethod
    def scratch(count, rows, columns):
        half = count // 2
        dma = pltpu.SemaphoreType.DMA
        return [
            pltpu.VMEM((2, half * (half - 1) // 2, rows, columns), low),
            dma((2, half * (half + 1) // 2)),
            dma((2, half * (half + 1) // 2)),
        ]

    def copy(self, way, hop, away):
        sign = 1 - 2 * way
        number = sum(range(hop)) if hop == 0 else sum(self.half - j + 1 for j in range(1, hop)) + away - hop
        if hop == 1:
            source = self.source.at[ring_index(self.count, sign * away)]
        else:
            source = self.transit.at[way, sum(self.half - j for j in range(1, hop - 1)) + away - hop]
        if away == hop:
            target = self.target.at[ring_index(self.count, sign * (1 - hop))]
        else:
            target = self.transit.at[way, sum(self.half - j for j in range(1, hop)) + away - hop - 1]
        if away == self.half:
            rows = pl.ds(way * self.cut, self.cut)
            source, target = source.at[rows], target.at[rows]
        sems = (self.sems[0].at[way, number], self.sems[1].at[way, number])
        return send(source, target, sems, (self.after, self.before)[way])

    def start(self):
        for away in range(self.half, 0, -1):
            for way in range(2):
                self.copy(way, 1, away).start()

    def hop(self, hop):
        for away in range(self.half, hop - 1, -1):
            for way in range(2):
                self.copy(way, hop, away).wait_recv()
                if away > hop:
                    self.copy(way, hop + 1, away).start()

    def drain(self):
        for hop in range(1, self.half + 1):
            for away in range(hop, self.half + 1):
                for way in range(2):
                    self.copy(way, hop, away).wait_send()


class RingScatter:
    def __init__(self, count, items, sems, after, before):
        self.count, self.half = count, count // 2
        self.items, self.sems = items, sems
        self.after, self.before = after, before

    @staticmethod
    def scratch(count, shapes):
        half = count // 2
        dma = pltpu.SemaphoreType.DMA
        arrived = [pltpu.VMEM((2, half) + shape, kind) for shape, kind in shapes]
        leaving = [pltpu.VMEM((2, 2) + shape, kind) for shape, kind in shapes]
        return arrived + leaving + [dma((len(shapes), 2, half)), dma((len(shapes), 2, half))]

    def columns(self, item, way):
        _, arrived, _, ways = self.items[item]
        wide = arrived.shape[-1]
        return pl.ds(way * (wide // 2), wide // 2) if len(ways) == 2 else pl.ds(0, wide)

    def copy(self, item, way, step):
        _, arrived, leaving, _ = self.items[item]
        source, target = leaving.at[way, step % 2], arrived.at[way, step]
        if step == 0:
            columns = self.columns(item, way)
            source, target = source.at[:, columns], target.at[:, columns]
        sems = (self.sems[0].at[item, way, step], self.sems[1].at[item, way, step])
        return send(source, target, sems, (self.after, self.before)[way])

    def begin(self, met=None):
        index = ring_index(self.count, self.half)
        for item, (value, _, leaving, ways) in enumerate(self.items):
            far = value(index).astype(leaving.dtype)
            for way in ways:
                leaving[way, 0] = far
        if met is not None:
            met()
        for item, (_, _, _, ways) in enumerate(self.items):
            for way in ways:
                self.copy(item, way, 0).start()

    def onward(self, step):
        for item, (value, arrived, leaving, ways) in enumerate(self.items):
            for way in range(2):
                offset = self.half - step
                mine = value(ring_index(self.count, offset if way == 0 else -offset))
                if step > 1:
                    self.copy(item, way, step - 1).wait_recv()
                    mine = mine + arrived[way, step - 1].astype(full)
                if step > 2 or (step == 2 and way in ways):
                    self.copy(item, way, step - 2).wait_send()
                leaving[way, step % 2] = mine.astype(leaving.dtype)
                if step == 1 and way in ways:
                    self.copy(item, way, 0).wait_recv()
                    columns = self.columns(item, way)
                    leaving[way, 1, :, columns] = (
                        leaving[way, 1, :, columns].astype(full) + arrived[way, 0, :, columns].astype(full)
                    ).astype(leaving.dtype)
                self.copy(item, way, step).start()

    def finish(self, item):
        value, arrived, _, _ = self.items[item]
        total = value(lax.axis_index("seq"))
        for way in range(2):
            self.copy(item, way, self.half - 1).wait_recv()
            total = total + arrived[way, self.half - 1].astype(full)
        return total

    def drain(self):
        for item, (_, _, _, ways) in enumerate(self.items):
            for way in range(2):
                for step in range(self.half - 2, self.half):
                    if step > 0 or way in ways:
                        self.copy(item, way, step).wait_send()


def feed_kernel(
    count, width, own, w_both_far, w_down_far, cotangent, total, feed_sum, down_own, down_others, hidden_far,
    w_both, w_down, hidden, feed, d_both, cot_rows, down_total, feed_others, feed_in, late_sem, cot_sem, cross_out,
    cross_in, *rest
):
    gather_sems, rest = rest[:4], rest[4:]
    ring_refs, ring_sems = rest[:5], rest[5:]
    half, chips = count // 2, width // CORES
    far = count - 1
    block, depth = own.shape
    units = w_down.shape[0]
    slice_f = units // chips
    tokens = count * 2 * block
    after, before = ring_sides(count)
    mate = core_mate()
    back, ahead = chip_mates(width), chip_mates(width, True)
    met = greet(after, before, mate, *back)
    gather = RingGather(count, own, feed, gather_sems, after, before, mate)
    ring = RingSum(count, ring_refs, ring_sems, after, before, mate)
    late = [
        pltpu.make_async_copy(w_both_far, w_both, late_sem.at[0]),
        pltpu.make_async_copy(w_down_far, w_down, late_sem.at[1]),
    ]
    save_hidden = pltpu.make_async_copy(hidden, hidden_far, late_sem.at[2])

    def cross(k):
        sems = (cross_out.at[k], cross_in.at[k])
        return send(feed_others.at[k - 1], feed_in.at[k - 1], sems, ahead[k - 1])

    def fetch(slot):
        return pltpu.make_async_copy(cotangent.at[slot], cot_rows.at[slot % 2], cot_sem.at[slot % 2])

    def fetched(slot):
        fetch(slot).wait()

        @pl.when(slot < far)
        def _():
            fetch(slot + 1).start()

        return cot_rows[slot % 2].reshape(2 * block, depth)

    def work(slot):
        back_all = lax.dot_general(fetched(slot), w_down[...], (NT, ((), ())), preferred_element_type=full)
        gather.to_mate(slot).wait_recv()
        rows = feed[slot].reshape(2 * block, depth)
        before_act = jnp.dot(rows, w_both[...], preferred_element_type=full)
        forth, back_parts = [], []
        for k in range(chips):
            start = 2 * k * slice_f
            gate, up = before_act[:, start : start + slice_f], before_act[:, start + slice_f : start + 2 * slice_f]
            active, slope = gelu_and_slope(gate)
            back = back_all[:, k * slice_f : (k + 1) * slice_f]
            forth.append(active * up)
            back_parts += [back * up * slope, back * active]
        hidden[slot] = jnp.concatenate(forth, axis=1).astype(low).reshape(2, block, units)
        d_rows = jnp.concatenate(back_parts, axis=1).astype(low)
        for k in range(chips):
            d_both[k, slot] = d_rows[:, 2 * k * slice_f : 2 * (k + 1) * slice_f].reshape(2, block, 2 * slice_f)
        part = lax.dot_general(d_rows, w_both[...], (NT, ((), ())), preferred_element_type=full)
        ring.offer(slot, part, slot >= ring.held)

    for copy in late:
        copy.start()
    fetch(0).start()
    met()
    gather.start()
    gather.hop(1, 0, half == 2)
    for copy in late:
        copy.wait()
    gather.hop(1, 1, half == 2)
    work(0)

    def advance(h, last):
        gather.hop(h, 0, last)
        work(2 * h - 3)
        gather.hop(h, 1, last)
        work(2 * h - 2)

    @pl.loop(2, half - 1)
    def _(h):
        advance(h, False)

    if half > 2:
        advance(half - 1, True)
    pl.loop(far - 2, far - 1)(work)
    gather.last()
    pl.loop(far - 1, far + 1)(work)
    save_hidden.start()

    pieces = 4
    wide = depth // pieces

    def grads(first, last):
        @pl.loop(first, last)
        def _(at):
            columns = pl.ds(pl.multiple_of((at % pieces) * wide, wide), wide)
            k = chips - 1 - at // pieces
            part = lax.dot_general(
                feed[:, :, :, columns].reshape(tokens, wide),
                d_both[k].reshape(tokens, 2 * slice_f),
                (TN, ((), ())),
                preferred_element_type=full,
            ).astype(low)

            @pl.when(k == 0)
            def _():
                feed_sum[columns] = part

            @pl.when(k > 0)
            def _():
                feed_others[jnp.maximum(k - 1, 0), columns] = part

    def down(slot):
        rows = fetched(slot)
        part = lax.dot_general(
            hidden[slot].reshape(2 * block, units), rows, (TN, ((), ())), preferred_element_type=full
        )

        @pl.when(slot == 0)
        def _():
            down_total[...] = part

        @pl.when(slot > 0)
        def _():
            down_total[...] += part

    fetch(0).start()
    ring.step(1, 0)
    ring.begin()
    grads(0, (chips - 1) * pieces)
    for k in range(1, chips):
        cross(k).start()
    ring.step(1, 1)
    steps = [(step, turn) for step in range(2, half) for turn in range(2)]
    ring_step = iter(steps)

    def next_step():
        for step, turn in [next(ring_step, (0, 0))]:
            if step > 0:
                ring.step(step, turn)

    next_step()
    grads((chips - 1) * pieces, chips * pieces)
    next_step()
    pl.loop(0, count // 2)(down)
    for _ in range(len(steps)):
        next_step()
    pl.loop(count // 2, count)(down)
    down_own[...] = down_total[:slice_f].astype(low)
    for k in range(1, chips):
        down_others[k - 1] = down_total[k * slice_f : (k + 1) * slice_f].astype(low)
    total[...] = ring.finish()
    for k in range(1, chips):
        cross(k).wait_recv()
    for at in range(pieces):
        rows = slice(at * wide, (at + 1) * wide)
        part = feed_sum[rows].astype(full)
        for k in range(1, chips):
            part = part + feed_in[k - 1, rows].astype(full)
        feed_sum[rows] = part.astype(low)
    save_hidden.wait()
    gather.drain()
    ring.drain()
    for k in range(1, chips):
        cross(k).wait_send()


def feed_forward(own, w_both, w_down, cotangent):
    count, width = lax.axis_size("seq"), lax.axis_size("dp")
    chips = width // CORES
    block, depth = own.shape
    units = w_down.shape[0]
    slice_f = units // chips
    whole = pl.BlockSpec(memory_space=pltpu.VMEM)
    dma = pltpu.SemaphoreType.DMA
    shapes = [
        ((block, depth), full), ((depth, 2 * slice_f), low), ((slice_f, depth), low),
        ((chips - 1, slice_f, depth), low), ((count, 2, block, units), low),
    ]
    far = pl.BlockSpec(memory_space=pl.ANY)
    return pl.pallas_call(
        partial(feed_kernel, count, width),
        in_specs=[whole, far, far, far],
        out_specs=[whole] * 4 + [far],
        out_shape=[jax.ShapeDtypeStruct(*shape) for shape in shapes],
        scratch_shapes=[
            pltpu.VMEM(w_both.shape, low),
            pltpu.VMEM(w_down.shape, low),
            pltpu.VMEM((count, 2, block, units), low),
            pltpu.VMEM((count, 2, block, depth), low),
            pltpu.VMEM((chips, count, 2, block, 2 * slice_f), low),
            pltpu.VMEM((2, 2, block, depth), low),
            pltpu.VMEM((units, depth), full),
            pltpu.VMEM((chips - 1, depth, 2 * slice_f), low),
            pltpu.VMEM((chips - 1, depth, 2 * slice_f), low),
            dma((3,)), dma((2,)), dma((chips,)), dma((chips,)),
            *RingGather.scratch(count),
            *RingSum.scratch(count, block, depth),
        ],
        compiler_params=pltpu.CompilerParams(collective_id=1, has_side_effects=True, vmem_limit_bytes=63 << 20),
        cost_estimate=pl.CostEstimate(
            flops=2 * 2 * count * block * depth * units * 9, bytes_accessed=40 << 20, transcendentals=0
        ),
    )(own, w_both, w_down, cotangent)


def seq_peer(count, step):
    place = lax.rem(lax.axis_index("seq") + (step + count), count)
    return {"seq": place}, place


def keep_column(marks, row):
    mark = jnp.broadcast_to(marks[row, :1], marks.shape[1:])
    padding = jnp.where(mark > 1.5, 1.0, 0.0)
    keep = 1.0 - (mark - 2.0 * padding)
    return jnp.transpose(keep)[:, :1], jnp.transpose(1.0 - padding)[:, :1]


def gate_terms(pre_rate, pre_inlet, soft):
    rate, inlet = jax.nn.sigmoid(pre_rate), jax.nn.sigmoid(pre_inlet)
    twice = -16.0 * rate * soft
    decay = jnp.exp(0.5 * twice)
    near = -twice * (
        1.0 + twice * (1 / 2 + twice * (1 / 6 + twice * (1 / 24 + twice * (1 / 120 + twice * (1 / 720)))))
    )
    rest = jnp.where(twice > -0.25, near, 1.0 - decay * decay)
    return rate, inlet, decay, rest, jnp.sqrt(rest)


def scan_rows(rate, value, backward):
    length, channels = rate.shape
    groups = length // 8
    rate = rate.reshape(groups, 8, channels)
    value = value.reshape(groups, 8, channels)
    place = lax.broadcasted_iota(jnp.int32, rate.shape, 1)
    for step in (1, 2, 4):
        keep = place < 8 - step if backward else place >= step
        move = 8 - step if backward else step
        earlier_rate = jnp.where(keep, pltpu.roll(rate, move, 1), 1.0)
        earlier_value = jnp.where(keep, pltpu.roll(value, move, 1), 0.0)
        value = value + rate * earlier_value
        rate = rate * earlier_rate
    product_in = jnp.ones((1, channels), full)
    state_in = jnp.zeros((1, channels), full)
    end = 0 if backward else 7
    products, states = [None] * groups, [None] * groups
    for group in reversed(range(groups)) if backward else range(groups):
        states[group] = value[group] + rate[group] * state_in
        products[group] = rate[group] * product_in
        product_in, state_in = products[group][end : end + 1], states[group][end : end + 1]
    return jnp.concatenate(products, axis=0), jnp.concatenate(states, axis=0)


def fold_states(count, arrived, backward):
    mine = lax.axis_index("seq")
    total = jnp.zeros(arrived.shape[2:], full)
    scale = jnp.ones(arrived.shape[2:], full)
    for step in range(1, count):
        there = (mine + step < count) if backward else (mine >= step)
        total = total + jnp.where(there, scale * arrived[step, 1], 0.0)
        scale = scale * arrived[step, 0]
    return total


def stack_rows(ref):
    pieces, rows, columns = ref.shape
    if rows % 16 == 0:
        return ref[...].reshape(pieces * rows, columns)
    return jnp.concatenate([ref[piece].astype(full) for piece in range(pieces)], axis=0).astype(ref.dtype)


def tail_factor(column, taps):
    length = column.shape[0]
    place = lax.broadcasted_iota(jnp.int32, (8, 1), 0)
    factor, run = jnp.where(place == 7, 1.0, 0.0), jnp.ones((1, 1), full)
    for back in range(1, taps - 1):
        run = run * column[length - back : length - back + 1]
        factor = jnp.where(place == 7 - back, run, factor)
    return factor


def front_kernel(
    count, width, own, cot_raw, resets, real_mask, gain_mix, gain_mlp, conv_kernel, decay_param, gate_rate, gate_input,
    w_gate, w_x, w_mix, w_feed_gate, w_feed_up, w_down,
    marks_all, w_both, gains, chan, cotangent, middle, feed_own, halo, ends, cot_all, down_all,
    gate_far, x_far, normed_far, pre_gate_far, branch_far, w_mix_far, conv_far, pre_rate_far, pre_inlet_far, rate_far,
    inlet_far, states_far, mixed_far,
    gate_all, x_all, normed, pre_gate, branch, w_mix_all, conv_low, pre_rate, pre_inlet, rate_mat, inlet_mat, states,
    mixed, save_sem, own_marks, small, small_all, own_gates, gates_all, mix_all, rows_all, x_total, scale, turned, arrived,
    keep, product, state, ext, halo_out, halo_in, state_out, state_all, core_out, core_in, chip_out, chip_in,
    ring_out, ring_in, last_out, last_in, rows_out, rows_in, mate_out, mate_in, cross_out, cross_in, down_out, down_in,
    halo_sem, state_out_sem, state_in_sem, core_out_sem, core_in_sem, chip_out_sem, chip_in_sem, cot_sem, *rest
):
    gather_sems, turn_refs = rest[:4], rest[4:]
    half = count // 2
    chips = width // CORES
    block, depth = own.shape
    shard, channels = w_gate.shape
    own_channels, size = gate_rate.shape
    taps = conv_kernel.shape[0]
    slice_f = w_down.shape[0]
    mine = lax.axis_index("seq")
    after, before = ring_sides(count)
    mate = core_mate()
    back, ahead = chip_mates(width), chip_mates(width, True)
    peers = [None] + [seq_peer(count, step)[0] for step in range(1, count)]
    met = greet(mate, *back, *peers[1:])
    gather = RingGather(count, cotangent, cot_all, gather_sems, after, before, mate, cot_sem.at[0])
    turn = RingTurn(count, turned, arrived.at[0], turn_refs[0], turn_refs[1:], after, before)
    saves = [
        pltpu.make_async_copy(source, target, save_sem.at[at])
        for at, (source, target) in enumerate(
            (
                (gate_all, gate_far), (x_all, x_far), (normed, normed_far), (pre_gate, pre_gate_far),
                (branch, branch_far), (w_mix_all, w_mix_far), (conv_low, conv_far), (pre_rate, pre_rate_far),
                (pre_inlet, pre_inlet_far), (rate_mat, rate_far), (inlet_mat, inlet_far), (states, states_far),
                (mixed, mixed_far), (w_down, down_all.at[0]),
            )
        )
    ]
    moved = ((w_gate, gate_all), (small, small_all), (w_x, x_all), (own_gates, gates_all), (w_mix, mix_all))
    shared = ((0,), (0,), (1,), (1,), (0, 1))

    def rows_copy(what, k):
        source, target = ((own, rows_all), (own_marks, marks_all))[what]
        return send(source, target.at[k], (rows_out.at[what, k], rows_in.at[what, k]), back[k - 1])

    def mate_copy(what, k):
        source, target = ((own, rows_all), (own_marks, marks_all))[what]
        source = source if k == 0 else target.at[k]
        return send(source, target.at[chips + k], (mate_out.at[what, k], mate_in.at[what, k]), mate)

    def ring_copy(way, hop, item):
        source, target = moved[item]
        index = mine if hop == 1 else ring_index(count, (1 - hop) if way == 0 else (hop - 1))
        return send(
            source if hop == 1 else target.at[index],
            target.at[index],
            (ring_out.at[way, hop, item], ring_in.at[way, hop, item]),
            after if way == 0 else before,
        )

    def last_copy(way, item):
        index = ring_index(count, (1 - half) if way == 0 else (half - 1))
        ref = moved[item][1].at[index]
        if len(shared[item]) == 2:
            ref = ref.at[:, pl.ds(way * (depth // 2), depth // 2)]
        return send(ref, ref, (last_out.at[way, item], last_in.at[way, item]), after if way == 0 else before)

    def cross(slot, k):
        offset = half if slot == count - 1 else (slot + 1) // 2 * (1 - 2 * (slot % 2))
        origin = ring_index(count, offset)
        sems = (cross_out.at[k, slot], cross_in.at[k, slot])
        return send(arrived.at[0, origin], arrived.at[k, origin], sems, back[k - 1])

    def cross_down(k):
        return send(w_down, down_all.at[k], (down_out.at[k], down_in.at[k]), back[k - 1])

    def halo_copy():
        return send(halo_out, halo_in, (halo_sem.at[0], halo_sem.at[1]), peers[1])

    def state_copy(step):
        return send(state_out, state_all.at[step], (state_out_sem.at[step], state_in_sem.at[step]), peers[step])

    def core_copy(k):
        return send(core_out.at[k], core_in.at[k], (core_out_sem.at[k], core_in_sem.at[k]), mate)

    def chip_copy(k):
        return send(chip_out.at[k], chip_in.at[k], (chip_out_sem.at[k], chip_in_sem.at[k]), ahead[k - 1])

    def send_item(item):
        ring_copy(0, 1, item).start()
        ring_copy(1, 1, item).start()
        moved[item][1][mine] = moved[item][0][...]

    real = real_mask[...].astype(full)
    own_marks[...] = jnp.broadcast_to(resets[...].astype(full) + 2.0 * (1.0 - real), own_marks.shape)
    tap_rows = conv_kernel[...].astype(full)
    padding = jnp.zeros((1, shard - own_channels), full)
    pieces = [jnp.concatenate([tap_rows[tap : tap + 1], padding], axis=1) for tap in range(taps)]
    pieces.append(jnp.concatenate([decay_param[...].astype(full), padding], axis=1))
    pieces += [gain_mix[...].astype(full).reshape(1, shard), gain_mlp[...].astype(full).reshape(1, shard)]
    place = lax.broadcasted_iota(jnp.int32, (16, shard), 0)
    total = jnp.zeros((16, shard), full)
    for at, piece in enumerate(pieces):
        total = jnp.where(place == at, piece, total)
    small[...] = total.astype(low)
    own_gates[...] = jnp.concatenate([gate_rate[...].astype(full), gate_input[...].astype(full)], axis=1).astype(low)
    met()
    send_item(0)
    mate_copy(0, 0).start()
    mate_copy(1, 0).start()
    for k in range(1, chips):
        rows_copy(0, k).start()
        rows_copy(1, k).start()
    for item in range(1, len(moved)):
        send_item(item)
    rows_all[0] = own[...]
    marks_all[0] = own_marks[...]
    _, real = keep_column(marks_all, 0)
    cotangent[...] = (cot_raw[...].astype(full) * real).astype(low)
    saves[13].start()
    for k in range(1, chips):
        cross_down(k).start()
    for k in range(1, chips):
        for what in range(2):
            rows_copy(what, k).wait_recv()
            mate_copy(what, k).start()
    for k in range(chips):
        for what in range(2):
            mate_copy(what, k).wait_recv()
    for row in range(width):
        values = rows_all[row].astype(full)
        scale[row] = lax.rsqrt(jnp.mean(values * values, axis=-1, keepdims=True) + epsilon)

    def work(index, first):
        columns = pl.ds(pl.multiple_of(index * shard, shard), shard)
        gain = small_all[index].astype(full)[taps + 1 : taps + 2]
        values = rows_all[:, :, columns].astype(full)
        part = (values * scale[...] * gain).astype(low).reshape(width * block, shard)
        normed[:, columns] = part
        for weight, target in ((gate_all, pre_gate), (x_all, x_total)):
            term = jnp.dot(part, weight[index], preferred_element_type=full).reshape(width, block, channels)
            if first:
                target[...] = term
            else:
                target[...] += term

    work(mine, True)
    for at in range(count):
        columns = slice(at * slice_f, (at + 1) * slice_f)
        turned[at] = jnp.concatenate(
            [w_feed_gate[:, columns].astype(full), w_feed_up[:, columns].astype(full)], axis=1
        ).astype(low)
    arrived[0, mine] = turned[mine]
    for k in range(1, chips):
        cross(0, k).start()
    for hop in range(1, half):
        for item in range(len(moved)):
            for way in range(2):
                ring_copy(way, hop, item).wait_recv()
                if hop < half - 1:
                    ring_copy(way, hop + 1, item).start()
                elif way in shared[item]:
                    last_copy(way, item).start()
            if item == 2:
                for way in range(2):
                    work(ring_index(count, -hop if way == 0 else hop), False)
    for item in range(3):
        last_copy(shared[item][0], item).wait_recv()
    work(ring_index(count, half), False)
    branch[...] = x_total[...].astype(low)
    for item in range(3, len(moved)):
        for way in shared[item]:
            last_copy(way, item).wait_recv()

    for row in range(width):
        column, _ = keep_column(marks_all, row)
        keep[row, :8] = jnp.ones((8, 1), full)
        keep[row, 8:] = column
        halo_out[row] = branch[row, block - 16 :].astype(full)[8:] * tail_factor(column, taps)
    halo_copy().start()
    turn.start()
    gather.start()
    entries = jnp.concatenate([small_all[at].astype(full)[:8, :own_channels] for at in range(count)], axis=1)
    place = lax.broadcasted_iota(jnp.int32, entries.shape, 0)
    decay_row = entries[taps : taps + 1]
    entries = jnp.where(place == taps, jax.nn.softplus(decay_row), entries)
    chan[...] = jnp.where(place == taps + 1, jax.nn.sigmoid(decay_row), entries)
    entries = jnp.concatenate([small_all[at].astype(full)[:8] for at in range(count)], axis=1)
    gains[...] = jnp.concatenate([entries[taps + 1 : taps + 3], jnp.zeros((6, depth), full)], axis=0)
    w_mix_all[...] = stack_rows(mix_all)
    for copy in saves[:6]:
        copy.start()
    entries = stack_rows(gates_all)
    for at in range(channels // size):
        rows = slice(at * size, (at + 1) * size)
        for target, first in ((rate_mat, 0), (inlet_mat, size)):
            parts = [entries[rows].astype(full)[:, first : first + size]]
            if at > 0:
                parts.insert(0, jnp.zeros((size, at * size), full))
            if at + 1 < channels // size:
                parts.append(jnp.zeros((size, channels - (at + 1) * size), full))
            target[rows] = jnp.concatenate(parts, axis=1).astype(low)

    halo_copy().wait_recv()
    soft = chan[taps : taps + 1]
    state_out[...] = jnp.zeros_like(state_out)

    @pl.loop(0, width)
    def _(row):
        from_before = jnp.where(mine > 0, halo_in[row], 0.0)
        halo[row] = from_before
        ext[:8] = from_before
        ext[8:] = branch[row].astype(full)
        valid = jnp.ones((block, 1), full)
        total = jnp.zeros((block, channels), full)
        for tap in range(taps):
            total = total + chan[tap : tap + 1] * valid * ext[8 - tap : 8 - tap + block]
            valid = valid * keep[row, 8 - tap : 8 - tap + block]
        conv = total.astype(low)
        conv_low[row] = conv
        rate_in = lax.dot_general(conv, rate_mat[...], (NT, ((), ())), preferred_element_type=full)
        inlet_in = lax.dot_general(conv, inlet_mat[...], (NT, ((), ())), preferred_element_type=full)
        pre_rate[row] = rate_in
        pre_inlet[row] = inlet_in
        _, inlet, decay, _, root = gate_terms(rate_in, inlet_in, soft)
        kept = keep[row, 8:]
        inflow = conv.astype(full) * inlet * ((1.0 - kept) + kept * root)
        row_product, row_state = scan_rows(decay * kept, inflow, False)
        product[row] = row_product
        state[row] = row_state
        state_out[0, pl.ds(row, 1)] = row_product[block - 1 :]
        state_out[1, pl.ds(row, 1)] = row_state[block - 1 :]

    for copy in saves[6:11]:
        copy.start()

    def background(h):
        turn.hop(h)
        for slot in (2 * h - 1, 2 * h) if h < half else (count - 1,):
            for k in range(1, chips):
                cross(slot, k).start()
        if h < half:
            gather.hop(h, 0, h == half - 1)
            gather.hop(h, 1, h == half - 1)
        else:
            gather.last()

    for step in range(1, count):
        state_copy(step).start()
    background(1)
    for step in range(1, count):
        state_copy(step).wait_recv()
    ends[0] = fold_states(count, state_all, False)
    ends[1] = state_out[0]

    def close(row):
        row_states = state[row] + product[row] * ends[0, pl.ds(row, 1)]
        states[row] = row_states
        active, _ = gelu_and_slope(pre_gate[row])
        row_mixed = (row_states * active).astype(low)
        mixed[row] = row_mixed
        return jnp.dot(row_mixed, w_mix_all[...], preferred_element_type=full)

    @pl.loop(0, chips)
    def _(at):
        k = chips - 1 - at
        core_out[k] = close(chips + k).astype(low)
        core_copy(k).start()

    @pl.loop(0, chips - 1)
    def _(at):
        k = chips - 1 - at
        part = close(k)
        core_copy(k).wait_recv()
        chip_out[k] = (part + core_in[k].astype(full)).astype(low)

    for k in range(chips - 1, 0, -1):
        chip_copy(k).start()
    part = close(0)
    background(2)
    core_copy(0).wait_recv()
    total = part + core_in[0].astype(full) + own[...].astype(full)
    for k in range(1, chips):
        chip_copy(k).wait_recv()
        total = total + chip_in[k].astype(full)
    for copy in saves[11:13]:
        copy.start()
    middle[...] = total
    scaled = total * lax.rsqrt(jnp.mean(total * total, axis=-1, keepdims=True) + epsilon)
    feed_own[...] = (scaled * gains[1:2]).astype(low)
    for h in range(3, half + 1):
        background(h)
    for k in range(chips):
        if k > 0:
            cross_down(k).wait_recv()
            for slot in range(count):
                cross(slot, k).wait_recv()
        w_both[:, 2 * k * slice_f : 2 * (k + 1) * slice_f] = arrived[k].reshape(depth, 2 * slice_f)
    for slot in range(count):
        gather.to_mate(slot).wait_recv()

    for copy in saves:
        copy.wait()
    for item in range(len(moved)):
        for way in range(2):
            for hop in range(1, half):
                ring_copy(way, hop, item).wait_send()
            if way in shared[item]:
                last_copy(way, item).wait_send()
    for what in range(2):
        for k in range(chips):
            mate_copy(what, k).wait_send()
        for k in range(1, chips):
            rows_copy(what, k).wait_send()
    for k in range(1, chips):
        cross_down(k).wait_send()
        chip_copy(k).wait_send()
        for slot in range(count):
            cross(slot, k).wait_send()
    for k in range(chips):
        core_copy(k).wait_send()
    for step in range(1, count):
        state_copy(step).wait_send()
    halo_copy().wait_send()
    turn.drain()
    gather.drain()


def forward(own, cotangent, resets, real_mask, *weights):
    conv_kernel, gate_rate, w_gate, w_mix, w_down = weights[2], weights[4], weights[6], weights[8], weights[11]
    count, width = lax.axis_size("seq"), lax.axis_size("dp")
    half, chips = count // 2, width // CORES
    block, depth = own.shape
    shard, part = w_gate.shape
    own_channels, size = gate_rate.shape
    channels = count * own_channels
    slice_f = w_down.shape[0]
    whole = pl.BlockSpec(memory_space=pltpu.VMEM)
    dma = pltpu.SemaphoreType.DMA
    rows = (width, block, channels)
    shapes = [
        ((width, 8, block), full), ((depth, 2 * chips * slice_f), low), ((8, depth), full), ((8, channels), full),
        ((block, depth), low), ((block, depth), full), ((block, depth), low), ((width, 8, channels), full),
        ((2, 8, channels), full), ((count, 2, block, depth), low), ((chips,) + w_down.shape, low),
    ]
    saved = [
        ((count, shard, part), low), ((count, shard, part), low), ((width * block, depth), low), (rows, full),
        (rows, low), ((channels, depth), low), (rows, low), (rows, full), (rows, full), ((channels, channels), low),
        ((channels, channels), low), (rows, full), (rows, low),
    ]
    return pl.pallas_call(
        partial(front_kernel, count, width),
        in_specs=[whole] * (4 + len(weights)),
        out_specs=[whole] * (len(shapes) - 2) + [pl.BlockSpec(memory_space=pl.ANY)] * (len(saved) + 2),
        out_shape=[jax.ShapeDtypeStruct(*shape) for shape in shapes + saved],
        scratch_shapes=[
            *[pltpu.VMEM(*shape) for shape in saved],
            dma((len(saved) + 1,)),
            pltpu.VMEM((8, block), full),
            pltpu.VMEM((16, shard), low),
            pltpu.VMEM((count, 16, shard), low),
            pltpu.VMEM((own_channels, 2 * size), low),
            pltpu.VMEM((count, own_channels, 2 * size), low),
            pltpu.VMEM((count,) + w_mix.shape, low),
            pltpu.VMEM((width, block, depth), low),
            pltpu.VMEM(rows, full),
            pltpu.VMEM((width, block, 1), full),
            pltpu.VMEM((count, shard, 2 * slice_f), low),
            pltpu.VMEM((chips, count, shard, 2 * slice_f), low),
            pltpu.VMEM((width, 8 + block, 1), full),
            pltpu.VMEM(rows, full),
            pltpu.VMEM(rows, full),
            pltpu.VMEM((8 + block, channels), full),
            pltpu.VMEM((width, 8, channels), full),
            pltpu.VMEM((width, 8, channels), full),
            pltpu.VMEM((2, 8, channels), full),
            pltpu.VMEM((count, 2, 8, channels), full),
            *[pltpu.VMEM((chips, block, depth), low)] * 4,
            dma((2, half, 5)), dma((2, half, 5)), dma((2, 5)), dma((2, 5)),
            dma((2, chips)), dma((2, chips)), dma((2, chips)), dma((2, chips)),
            dma((chips, count)), dma((chips, count)), dma((chips,)), dma((chips,)),
            dma((2,)), dma((count,)), dma((count,)), dma((chips,)), dma((chips,)), dma((chips,)), dma((chips,)), dma((1,)),
            *RingGather.scratch(count),
            *RingTurn.scratch(count, shard, 2 * slice_f),
        ],
        compiler_params=pltpu.CompilerParams(collective_id=2, has_side_effects=True, vmem_limit_bytes=63 << 20),
        cost_estimate=pl.CostEstimate(
            flops=6 * width * block * depth * channels, bytes_accessed=60 << 20, transcendentals=0
        ),
    )(own, cotangent, resets, real_mask, *weights)


def back_kernel(
    count, width, taps, d_feed, middle, cotangent, gains, marks, chan, halo, ends, w_down,
    w_mix_far, mixed_far, rate_far, inlet_far, conv_far, down_far,
    pre_gate, pre_rate, pre_inlet, states, branch, hidden, down_others, feed_sum,
    output, d_middle, d_pre_gate, d_branch, grad_mix, gate_grads, small_grads, gain_share, down_sum, feed_gate, feed_up,
    w_mix, mixed, rate_mat, inlet_mat, conv_low, down_own, gate_rows, rate_rows, inlet_rows, state_rows, branch_rows,
    hidden_rows, keep, mix_rows, mix_grads, later, local, shift, ext, d_rate, d_inlet, sums, halo_out, halo_in,
    state_out, state_all, down_in, feed_parts, late_sem, row_sem, hidden_sem, *rest
):
    ring_refs, rest = rest[:5], rest[5:]
    ring_sems, rest = rest[:6], rest[6:]
    (arrived, leaving), mix_sems, rest = rest[:2], rest[2:4], rest[4:]
    halo_sem, state_out_sem, state_in_sem, chip_out, chip_in, mate_out, mate_in, cross_out, cross_in = rest[:9]
    turn_refs = rest[9:]
    half = count // 2
    chips = width // CORES
    far = count - 1
    block, depth = middle.shape
    channels = chan.shape[1]
    own_channels = channels // count
    size = gate_grads.shape[-1] // 2
    mine = lax.axis_index("seq")
    after, before = ring_sides(count)
    mate = core_mate()
    back, ahead = chip_mates(width), chip_mates(width, True)
    peers = [None] + [seq_peer(count, -step)[0] for step in range(1, count)]
    met = greet(mate, *back, *peers[1:])
    ring = RingSum(count, ring_refs, ring_sems, after, before, mate)
    items = [(lambda index: mix_grads[index].astype(full), arrived, leaving, (0, 1))]
    scatter = RingScatter(count, items, mix_sems, after, before)
    turn = RingTurn(count, feed_sum, feed_parts, turn_refs[0], turn_refs[1:], after, before)

    def chips_copy(k):
        return send(mix_rows.at[0], mix_rows.at[k], (chip_out.at[k], chip_in.at[k]), back[k - 1])

    def mate_copy(k):
        return send(mix_rows.at[k], mix_rows.at[chips + k], (mate_out.at[k], mate_in.at[k]), mate)

    def cross(k):
        return send(down_others.at[k - 1], down_in.at[k - 1], (cross_out.at[k], cross_in.at[k]), ahead[k - 1])

    late = [
        pltpu.make_async_copy(source, target, late_sem.at[at])
        for at, (source, target) in enumerate(
            (
                (mixed_far, mixed), (w_mix_far, w_mix), (rate_far, rate_mat), (inlet_far, inlet_mat),
                (conv_far, conv_low), (down_far, down_own), (feed_sum.at[mine], feed_parts.at[mine]),
            )
        )
    ]
    streams = (
        ((pre_gate, gate_rows), (pre_rate, rate_rows), (states, state_rows)),
        ((pre_rate, rate_rows), (pre_inlet, inlet_rows), (states, state_rows), (branch, branch_rows)),
    )

    def row_copies(which, row):
        return [
            pltpu.make_async_copy(source.at[row], target.at[row % 2], row_sem.at[at, row % 2])
            for at, (source, target) in enumerate(streams[which])
        ]

    def row_start(which, row):
        for copy in row_copies(which, row):
            copy.start()

    def row_ready(which, row):
        for copy in row_copies(which, row):
            copy.wait()

        @pl.when(row + 1 < width)
        def _():
            row_start(which, row + 1)

        return row % 2

    def halo_copy():
        return send(halo_out, halo_in, (halo_sem.at[0], halo_sem.at[1]), peers[1])

    def state_copy(step):
        return send(state_out, state_all.at[step], (state_out_sem.at[step], state_in_sem.at[step]), peers[step])

    def fetch(at):
        return pltpu.make_async_copy(hidden.at[far - at], hidden_rows.at[at % 2], hidden_sem.at[at % 2])

    fetch(0).start()
    for copy in late:
        copy.start()
    row_start(0, 0)

    values, arriving = middle[...], d_feed[...]
    scale = lax.rsqrt(jnp.mean(values * values, axis=-1, keepdims=True) + epsilon)
    normed = values * scale
    scaled = arriving * gains[1:2]
    gain_share[...] = jnp.sum(arriving * normed, axis=0, keepdims=True)
    total = cotangent[...].astype(full) + scale * (
        scaled - normed * jnp.mean(scaled * normed, axis=-1, keepdims=True)
    )
    d_middle[...] = total
    mix_rows[0] = total.astype(low)
    met()
    for k in range(1, chips):
        chips_copy(k).start()
    mate_copy(0).start()
    turn.start()

    def offer(at):
        slot = far - at
        fetch(at).wait()

        @pl.when(at < far)
        def _():
            fetch(at + 1).start()

        rows = hidden_rows[at % 2].reshape(2 * block, hidden.shape[-1])
        ring.offer(slot, jnp.dot(rows, w_down[...], preferred_element_type=full), at >= ring.held)

    pl.loop(0, 3)(offer)
    ring.begin()
    ring.step(1, 0)
    pl.loop(3, count)(offer)
    for k in range(1, chips):
        chips_copy(k).wait_recv()
        mate_copy(k).start()
    for k in range(1, chips):
        cross(k).start()
    ring.step(1, 1)
    turn.hop(1)
    for copy in late[:2]:
        copy.wait()
    for k in range(chips):
        mate_copy(k).wait_recv()
    tokens = width * block
    rows = mixed[...].reshape(tokens, channels)
    wide = depth // 4
    for at in range(4):
        part = lax.dot_general(
            rows,
            mix_rows[:, :, at * wide : (at + 1) * wide].reshape(tokens, wide),
            (TN, ((), ())),
            preferred_element_type=full,
        )
        for piece in range(count):
            mix_grads[piece, :, at * wide : (at + 1) * wide] = part[
                piece * own_channels : (piece + 1) * own_channels
            ].astype(low)
    scatter.begin()

    soft, soft_slope = chan[taps : taps + 1], chan[taps + 1 : taps + 2]
    state_out[0] = ends[1]
    state_out[1] = jnp.zeros_like(ends[1])
    sums[...] = jnp.zeros_like(sums)

    def adjoint_row(row):
        at = row_ready(0, row)
        column, real = keep_column(marks, row)
        keep[row, :8] = jnp.ones((8, 1), full)
        keep[row, 8:] = column
        sums[taps + 2 : taps + 3] += jnp.sum(real)
        d_mixed = lax.dot_general(mix_rows[row], w_mix[...], (NT, ((), ())), preferred_element_type=full)
        active, slope = gelu_and_slope(gate_rows[at])
        d_pre_gate[row] = (d_mixed * state_rows[at] * slope).astype(low)
        decay = jnp.exp(-8.0 * jax.nn.sigmoid(rate_rows[at]) * soft)
        sums[taps + 1 : taps + 2] += jnp.sum(decay * real, axis=0, keepdims=True)
        shift[:block] = decay * column
        shift[block:] = jnp.ones((8, channels), full)
        row_later, row_local = scan_rows(shift[1 : block + 1], d_mixed * active, True)
        later[row] = row_later
        local[row] = row_local
        state_out[1, pl.ds(row, 1)] = shift[:1] * row_local[:1]

    if half > 2:
        ring.step(2, 0)
    pl.loop(0, width // 2)(adjoint_row)
    if half > 2:
        ring.step(2, 1)
    pl.loop(width // 2, width)(adjoint_row)
    row_start(1, 0)
    for step in range(1, count):
        state_copy(step).start()
    scatter.onward(1)
    turn.hop(2)
    for copy in late[2:]:
        copy.wait()
    for step in range(1, count):
        state_copy(step).wait_recv()
    sums[8:16] = fold_states(count, state_all, True)

    def gate_row(row):
        at = row_ready(1, row)
        column = keep[row, 8:]
        rate, inlet, decay, _, root = gate_terms(rate_rows[at], inlet_rows[at], soft)
        conv = conv_low[row].astype(full)
        adjoint = local[row] + later[row] * sums[pl.ds(8 + row, 1)]
        shift[:8] = jnp.broadcast_to(ends[0, pl.ds(row, 1)], (8, channels))
        shift[8:] = state_rows[at]
        previous = shift[7 : 7 + block]
        mult = (1.0 - column) + column * root
        d_log = adjoint * column * (decay * previous - conv * inlet * decay * decay / root)
        rate_part = (d_log * (-8.0 * soft) * rate * (1.0 - rate)).astype(low)
        inlet_part = (adjoint * conv * mult * inlet * (1.0 - inlet)).astype(low)
        d_rate[row] = rate_part
        d_inlet[row] = inlet_part
        sums[taps : taps + 1] += jnp.sum(d_log * (-8.0 * rate), axis=0, keepdims=True) * soft_slope
        through = (
            adjoint * inlet * mult
            + jnp.dot(rate_part, rate_mat[...], preferred_element_type=full)
            + jnp.dot(inlet_part, inlet_mat[...], preferred_element_type=full)
        )
        ext[:8] = halo[row]
        ext[8:] = branch_rows[at].astype(full)
        place = lax.broadcasted_iota(jnp.int32, (8, 1), 0)
        valid = jnp.ones((block, 1), full)
        branch_part = jnp.zeros((block, channels), full)
        tail = jnp.zeros((8, channels), full)
        for tap in range(taps):
            moved = valid * through
            sums[tap : tap + 1] += jnp.sum(moved * ext[8 - tap : 8 - tap + block], axis=0, keepdims=True)
            moved = moved * chan[tap : tap + 1]
            if tap == 0:
                branch_part = moved
            else:
                shift[:block] = moved
                shift[block:] = jnp.zeros((8, channels), full)
                branch_part = branch_part + shift[tap : tap + block]
                for j in range(1, tap + 1):
                    tail = tail + jnp.where(place == 8 - j, moved[tap - j : tap - j + 1], 0.0)
            valid = valid * keep[row, 8 - tap : 8 - tap + block]
        local[row] = branch_part
        halo_out[row] = tail

    pl.loop(0, width // 2)(gate_row)
    if half > 2:
        scatter.onward(2)
    for step in range(3, half):
        ring.step(step, 0)
        ring.step(step, 1)
    if half > 2:
        turn.hop(3)
    pl.loop(width // 2, width)(gate_row)
    halo_copy().start()
    rows = conv_low[...].reshape(tokens, channels)
    both = [
        lax.dot_general(part[...].reshape(tokens, channels), rows, (TN, ((), ())), preferred_element_type=full)
        for part in (d_rate, d_inlet)
    ]
    for piece in range(count):
        first = piece * own_channels
        at = first // size * size
        gate_grads[piece] = jnp.concatenate(
            [part[first : first + own_channels, at : at + size] for part in both], axis=1
        ).astype(low)
    for step in range(3, half):
        scatter.onward(step)
        turn.hop(step + 1)
    halo_copy().wait_recv()

    @pl.loop(0, width)
    def _(row):
        column = keep[row, 8:]
        arriving = jnp.where(mine < count - 1, halo_in[row] * tail_factor(column, taps), 0.0)
        local[row, block - 8 :] += arriving
        d_branch[row] = local[row].astype(low)

    for piece in range(count):
        entries = sums[:8, piece * own_channels : (piece + 1) * own_channels]
        small_grads[piece] = jnp.concatenate([entries, jnp.zeros((8, 128 - own_channels), full)], axis=1)
    total = down_own[...].astype(full)
    for k in range(1, chips):
        cross(k).wait_recv()
        total = total + down_in[k - 1].astype(full)
    down_sum[...] = total.astype(low)
    _, real = keep_column(marks, 0)
    output[...] = ((middle[...] + ring.finish()) * real).astype(low)

    wide = feed_parts.shape[-1] // 2
    for target, columns in ((feed_gate, slice(0, wide)), (feed_up, slice(wide, 2 * wide))):
        parts = [feed_parts[at].astype(full)[:, columns] for at in range(count)]
        target[...] = jnp.concatenate(parts, axis=1).astype(low)
    grad_mix[...] = scatter.finish(0).astype(low)
    ring.drain()
    scatter.drain()
    turn.drain()
    halo_copy().wait_send()
    for step in range(1, count):
        state_copy(step).wait_send()
    for k in range(chips):
        mate_copy(k).wait_send()
    for k in range(1, chips):
        chips_copy(k).wait_send()
        cross(k).wait_send()


def mix_back(taps, size, near, late, rows, hidden, down_others, feed_sum):
    (d_feed, middle, _, _, _, chan, *_) = near
    count, width = lax.axis_size("seq"), lax.axis_size("dp")
    chips = width // CORES
    block, depth = middle.shape
    channels = chan.shape[1]
    own_channels = channels // count
    whole = pl.BlockSpec(memory_space=pltpu.VMEM)
    far = pl.BlockSpec(memory_space=pl.ANY)
    dma = pltpu.SemaphoreType.DMA
    all_rows = (width, block, channels)
    shapes = [
        ((block, depth), low), ((block, depth), full), (all_rows, low), (all_rows, low),
        ((own_channels, depth), low), ((count, own_channels, 2 * size), low), ((count, 8, 128), full),
        ((1, depth), full), (late[-1].shape, low),
        *[((feed_sum.shape[1], feed_sum.shape[2] // 2 * count), low)] * 2,
    ]
    operands = (*near, *late, *rows, hidden, down_others, feed_sum)
    return pl.pallas_call(
        partial(back_kernel, count, width, taps),
        in_specs=[whole] * len(near) + [far] * (len(operands) - len(near)),
        out_specs=[whole] * len(shapes),
        out_shape=[jax.ShapeDtypeStruct(*shape) for shape in shapes],
        scratch_shapes=[
            *[pltpu.VMEM(each.shape, each.dtype) for each in (late[0], late[1], *late[2:])],
            *[pltpu.VMEM((2,) + each.shape[1:], each.dtype) for each in (*rows, hidden)],
            pltpu.VMEM((width, 8 + block, 1), full),
            pltpu.VMEM((width, block, depth), low),
            pltpu.VMEM((count, own_channels, depth), low),
            pltpu.VMEM(all_rows, full),
            pltpu.VMEM(all_rows, full),
            pltpu.VMEM((block + 8, channels), full),
            pltpu.VMEM((block + 8, channels), full),
            pltpu.VMEM(all_rows, low),
            pltpu.VMEM(all_rows, low),
            pltpu.VMEM((16, channels), full),
            pltpu.VMEM((width, 8, channels), full),
            pltpu.VMEM((width, 8, channels), full),
            pltpu.VMEM((2, 8, channels), full),
            pltpu.VMEM((count, 2, 8, channels), full),
            pltpu.VMEM(down_others.shape, low),
            pltpu.VMEM(feed_sum.shape, low),
            dma((len(late) + 1,)), dma((4, 2)), dma((2,)),
            *RingSum.scratch(count, block, depth),
            *RingScatter.scratch(count, [((own_channels, depth), low)]),
            dma((2,)), dma((count,)), dma((count,)), dma((chips,)), dma((chips,)), dma((chips,)), dma((chips,)),
            dma((chips,)), dma((chips,)),
            *RingTurn.scratch(count, *feed_sum.shape[1:]),
        ],
        compiler_params=pltpu.CompilerParams(collective_id=4, has_side_effects=True, vmem_limit_bytes=63 << 20),
        cost_estimate=pl.CostEstimate(
            flops=4 * width * block * channels * (depth + 2 * channels), bytes_accessed=60 << 20, transcendentals=0
        ),
    )(*operands)


def close_kernel(
    count, width, own, d_middle, gains, gain_share, normed, d_pre_gate, d_branch, gate_grads, small_grads,
    w_gate_far, w_x_far, d_inputs, out_gate, out_x, out_gates, out_small, out_gains, w_gate, w_x, late_sem, *rest
):
    travel, rest = rest[:10], rest[10:]
    core_out, core_in, chip_out, chip_in, gain_out, gain_width, gain_total, gain_seq = rest[:8]
    core_out_sem, core_in_sem, chip_out_sem, chip_in_sem, width_out, width_in, seq_out, seq_in = rest[8:16]
    half = count // 2
    chips = width // CORES
    block, depth = own.shape
    shard = out_gate.shape[0]
    share = depth // width
    my_width = lax.axis_index("dp")
    after, before = ring_sides(count)
    mate = core_mate()
    ahead = chip_mates(width, True)
    peers = [None] + [seq_peer(count, step) for step in range(1, count)]
    others = [None] + [lax.rem(my_width + step, width) for step in range(1, width)]
    met = greet(*[peer for peer, _ in peers[1:]], *[{"dp": place} for place in others[1:]])

    def product(grads):
        def at(index):
            columns = pl.ds(pl.multiple_of(index * shard, shard), shard)
            return lax.dot_general(normed[:, columns], grads[...], (TN, ((), ())), preferred_element_type=full)

        return at

    def stored(grads):
        return lambda index: grads[index].astype(full)

    values = (product(d_pre_gate), product(d_branch), stored(gate_grads), stored(small_grads))
    results = (out_gate, out_x, out_gates, out_small)
    items = list(zip(values, travel[:4], travel[4:8], ((0,), (1,), (1,), (0,))))
    scatter = RingScatter(count, items, travel[8:], after, before)

    late = [
        pltpu.make_async_copy(source, target, late_sem.at[at])
        for at, (source, target) in enumerate(((w_gate_far, w_gate), (w_x_far, w_x)))
    ]

    def core_copy(k):
        return send(core_out.at[k], core_in.at[k], (core_out_sem.at[k], core_in_sem.at[k]), mate)

    def chip_copy(k):
        return send(chip_out.at[k], chip_in.at[k], (chip_out_sem.at[k], chip_in_sem.at[k]), ahead[k - 1])

    def width_copy(step):
        columns = pl.ds(pl.multiple_of(others[step] * share, share), share)
        sems = (width_out.at[step], width_in.at[step])
        return send(gain_out.at[:, columns], gain_width.at[step], sems, {"dp": others[step]})

    def seq_copy(step):
        return send(gain_total, gain_seq.at[step], (seq_out.at[step], seq_in.at[step]), peers[step][0])

    def through(row):
        return lax.dot_general(
            d_pre_gate[pl.ds(pl.multiple_of(row * block, block), block)],
            w_gate[...],
            (NT, ((), ())),
            preferred_element_type=full,
        ) + lax.dot_general(
            d_branch[pl.ds(pl.multiple_of(row * block, block), block)],
            w_x[...],
            (NT, ((), ())),
            preferred_element_type=full,
        )

    for copy in late:
        copy.start()
    scatter.begin(met)
    for copy in late:
        copy.wait()

    @pl.loop(0, chips)
    def _(at):
        k = chips - 1 - at
        core_out[k] = through(chips + k).astype(low)
        core_copy(k).start()

    scatter.onward(1)

    @pl.loop(0, chips - 1)
    def _(at):
        k = chips - 1 - at
        part = through(k)
        core_copy(k).wait_recv()
        chip_out[k] = (part + core_in[k].astype(full)).astype(low)

    for k in range(chips - 1, 0, -1):
        chip_copy(k).start()
    part = through(0)
    core_copy(0).wait_recv()
    total = part + core_in[0].astype(full)
    for k in range(1, chips):
        chip_copy(k).wait_recv()
        total = total + chip_in[k].astype(full)
    rows = own[...].astype(full)
    scale = lax.rsqrt(jnp.mean(rows * rows, axis=-1, keepdims=True) + epsilon)
    rows = rows * scale
    scaled = total * gains[:1]
    d_inputs[...] = (
        d_middle[...] + scale * (scaled - rows * jnp.mean(scaled * rows, axis=-1, keepdims=True))
    ).astype(low)
    gain_out[...] = jnp.zeros_like(gain_out)
    gain_out[:1] = jnp.sum(total * rows, axis=0, keepdims=True)
    gain_out[1:2] = gain_share[...]
    for step in range(1, width):
        width_copy(step).start()
    if half > 2:
        scatter.onward(2)
    columns = pl.ds(pl.multiple_of(my_width * share, share), share)
    gain_sum = gain_out[:, columns]
    for step in range(1, width):
        width_copy(step).wait_recv()
        gain_sum = gain_sum + gain_width[step]
    gain_total[...] = gain_sum
    for step in range(1, count):
        seq_copy(step).start()
    for step in range(3, half):
        scatter.onward(step)
    for step in range(1, count):
        seq_copy(step).wait_recv()
        gain_sum = gain_sum + gain_seq[step]
    out_gains[...] = gain_sum
    for item, result in enumerate(results):
        result[...] = scatter.finish(item).astype(result.dtype)
    scatter.drain()
    for step in range(1, count):
        seq_copy(step).wait_send()
    for step in range(1, width):
        width_copy(step).wait_send()
    for k in range(chips):
        core_copy(k).wait_send()
    for k in range(1, chips):
        chip_copy(k).wait_send()


def close(operands):
    own, _, _, _, normed, d_pre_gate, _, gate_grads, small_grads, w_gate, w_x = operands
    count, width = lax.axis_size("seq"), lax.axis_size("dp")
    chips = width // CORES
    block, depth = own.shape
    channels = d_pre_gate.shape[1]
    shard, share = depth // count, depth // width
    whole = pl.BlockSpec(memory_space=pltpu.VMEM)
    dma = pltpu.SemaphoreType.DMA
    items = [
        ((shard, channels), low), ((shard, channels), low), (gate_grads.shape[1:], low), (small_grads.shape[1:], full),
    ]
    shapes = [
        ((block, depth), low), *[(shape, low if at < 2 else full) for at, (shape, _) in enumerate(items)],
        ((8, share), full),
    ]
    return pl.pallas_call(
        partial(close_kernel, count, width),
        in_specs=[whole] * (len(operands) - 2) + [pl.BlockSpec(memory_space=pl.ANY)] * 2,
        out_specs=[whole] * len(shapes),
        out_shape=[jax.ShapeDtypeStruct(*shape) for shape in shapes],
        scratch_shapes=[
            *[pltpu.VMEM(each.shape, low) for each in (w_gate, w_x)],
            dma((2,)),
            *RingScatter.scratch(count, items),
            *[pltpu.VMEM((chips, block, depth), low)] * 4,
            pltpu.VMEM((8, depth), full),
            pltpu.VMEM((width, 8, share), full),
            pltpu.VMEM((8, share), full),
            pltpu.VMEM((count, 8, share), full),
            dma((chips,)), dma((chips,)), dma((chips,)), dma((chips,)),
            dma((width,)), dma((width,)), dma((count,)), dma((count,)),
        ],
        compiler_params=pltpu.CompilerParams(collective_id=5, has_side_effects=True, vmem_limit_bytes=63 << 20),
        cost_estimate=pl.CostEstimate(
            flops=8 * normed.shape[0] * depth * channels, bytes_accessed=40 << 20, transcendentals=0
        ),
    )(*operands)


def lay_out_kernel(count, taps, *refs):
    for source, target in zip(refs[:8], refs[11:19]):
        target[...] = source[...].astype(target.dtype)
    gates, small, gains = refs[8:11]
    taps_out, rate_out, input_out, decay_out, log_out, mix_out, mlp_out = refs[19:]
    size = rate_out.shape[1]
    channels, share = decay_out.shape[1], mix_out.shape[1]
    rate_out[...] = gates[:, :size]
    input_out[...] = gates[:, size:]
    taps_out[...] = small[:taps, :channels]
    decay_out[...] = small[taps : taps + 1, :channels]
    log_out[...] = small[taps + 1 : taps + 2, :channels] / small[taps + 2 : taps + 3, :channels]
    mine = lax.axis_index("seq")
    total = jnp.zeros((8, share), full)
    for at in range(count):
        total = jnp.where(mine == at, gains[:, at * share : (at + 1) * share], total)
    mix_out[...] = total[:1]
    mlp_out[...] = total[1:2]


def lay_out(taps, arrays, gates, small, gains):
    count = lax.axis_size("seq")
    steps = 2

    def block(shape, by_rows):
        if by_rows:
            return pl.BlockSpec((shape[0] // steps, shape[1]), lambda at: (at, 0))
        return pl.BlockSpec((shape[0], shape[1] // steps), lambda at: (0, at))

    def whole(shape):
        return pl.BlockSpec(shape, lambda at: (0, 0))

    cuts = [block(array.shape, by_rows) for array, by_rows, _ in arrays]
    own_channels, both = gates.shape
    share = gains.shape[1] // count
    rest = [(taps, own_channels), (own_channels, both // 2), (own_channels, both // 2), (1, own_channels)]
    rest += [(1, own_channels), (1, share), (1, share)]
    return pl.pallas_call(
        partial(lay_out_kernel, count, taps),
        grid=(steps,),
        in_specs=cuts + [whole(each.shape) for each in (gates, small, gains)],
        out_specs=cuts + [whole(shape) for shape in rest],
        out_shape=[jax.ShapeDtypeStruct(array.shape, kind) for array, _, kind in arrays]
        + [jax.ShapeDtypeStruct(shape, full) for shape in rest],
        compiler_params=pltpu.CompilerParams(vmem_limit_bytes=63 << 20),
    )(*[array for array, _, _ in arrays], gates, small, gains)


def on_device(
    inputs,
    cotangent,
    resets,
    real_mask,
    gain_mix,
    w_branch_gate,
    w_branch_x,
    conv_kernel,
    gate_rate,
    gate_input,
    decay_param,
    w_mix_out,
    gain_mlp,
    w_mlp_gate,
    w_mlp_up,
    w_mlp_down,
):
    seq = lax.axis_size("seq")
    rows_own, length, depth = inputs.shape
    taps = conv_kernel.shape[1]
    block = rows_own * length
    tokens = block * lax.axis_size("dp")
    own_channels, size = gate_rate.shape
    shard, part_w = w_branch_x.shape
    rows = inputs.reshape(block, depth)
    (
        marks, w_both, gains, chan, cot_low, middle, feed_own, halo, ends, d_feed, w_down,
        w_gate_all, w_x_all, mixer_in, pre_gate, branch, w_mix_out, conv_low, pre_rate, pre_inlet, rate_mat, inlet_mat,
        states, mixed,
    ) = forward(
        rows, cotangent.reshape(block, depth), resets, real_mask, gain_mix, gain_mlp, conv_kernel.T,
        decay_param[None], gate_rate, gate_input, w_branch_gate, w_branch_x, w_mix_out, w_mlp_gate, w_mlp_up,
        w_mlp_down,
    )
    w_down = w_down.reshape(-1, depth)

    d_feed_own, feed_sum, down_own, down_others, hidden = feed_forward(feed_own, w_both, w_down, d_feed)

    (
        output, d_middle, d_pre_gate, d_branch, grad_mix_out, gate_grads, small_grads, gain_share, grad_down,
        feed_gate, feed_up,
    ) = mix_back(
        taps,
        size,
        (d_feed_own, middle, cot_low, gains, marks, chan, halo, ends, w_down),
        (w_mix_out, mixed, rate_mat, inlet_mat, conv_low, down_own),
        (pre_gate, pre_rate, pre_inlet, states, branch),
        hidden,
        down_others,
        feed_sum.reshape(seq, shard, -1),
    )

    grad_inputs, grad_gate, grad_x, grad_gates, grad_small, gains = close(
        (
            rows, d_middle, gains, gain_share, mixer_in, d_pre_gate.reshape(tokens, part_w),
            d_branch.reshape(tokens, part_w), gate_grads, small_grads, w_gate_all.reshape(depth, part_w),
            w_x_all.reshape(depth, part_w),
        )
    )
    (
        output, grad_inputs, grad_gate, grad_x, feed_gate, feed_up, grad_mix_out, grad_down,
        grad_taps, grad_rate, grad_input, grad_decay, decay_log, grad_gain_mix, grad_gain_mlp,
    ) = lay_out(
        taps,
        (
            (output, True, low), (grad_inputs, True, low), (grad_gate, True, full), (grad_x, True, full),
            (feed_gate, True, full), (feed_up, True, full), (grad_mix_out, False, full), (grad_down, False, full),
        ),
        grad_gates,
        grad_small,
        gains,
    )
    return (
        output[None],
        grad_inputs[None],
        grad_gain_mix[0],
        grad_gate,
        grad_x,
        grad_taps.T,
        grad_rate,
        grad_input,
        grad_decay[0],
        grad_mix_out,
        grad_gain_mlp[0],
        feed_gate,
        feed_up,
        grad_down,
        decay_log[0],
    )


def solution(mesh):
    placed = (
        P("dp", "seq", None),
        P("dp", "seq", None),
        P("dp", "seq"),
        P("dp", "seq"),
        P("seq"),
        P("seq", "dp"),
        P("seq", "dp"),
        P(("dp", "seq"), None),
        P(("dp", "seq"), None),
        P(("dp", "seq"), None),
        P(("dp", "seq")),
        P(("dp", "seq"), None),
        P("seq"),
        P("seq", "dp"),
        P("seq", "dp"),
        P(("dp", "seq"), None),
    )
    return jax.shard_map(
        on_device,
        mesh=mesh,
        in_specs=placed,
        out_specs=(
            P("dp", "seq", None),
            P("dp", "seq", None),
            P(("dp", "seq")),
            P("seq", "dp"),
            P("seq", "dp"),
            P(("dp", "seq"), None),
            P(("dp", "seq"), None),
            P(("dp", "seq"), None),
            P(("dp", "seq")),
            P(("dp", "seq"), None),
            P(("dp", "seq")),
            P("seq", "dp"),
            P("seq", "dp"),
            P(("dp", "seq"), None),
            P(("dp", "seq")),
        ),
        check_vma=False,
    )
```

```python
from functools import partial

import jax
import jax.numpy as jnp
from jax import lax
from jax.experimental import pallas as pl
from jax.experimental.pallas import tpu as pltpu
from jax.sharding import PartitionSpec as P

epsilon = 1e-06
low = jnp.bfloat16
full = jnp.float32
CORES = 2


def ring_of(count):
    deep = 4 if count % 4 == 0 else 1
    wide = count // deep
    walk = [(z, 0) for z in range(deep)]
    for turn, z in enumerate(reversed(range(deep))):
        across = list(range(1, wide))
        walk += [(z, y) for y in (across if turn % 2 == 0 else across[::-1])]
    return [z * wide + y for z, y in walk]


NT = ((1,), (1,))
TN = ((0,), (0,))


MESH = pl.DeviceIdType.MESH


def pick_from(table, index):
    found = table[0]
    for at in range(1, len(table)):
        found = jnp.where(index == at, table[at], found)
    return found


def ring_sides(count):
    ring = ring_of(count)
    place = {index: position for position, index in enumerate(ring)}
    mine = lax.axis_index("seq")
    after = pick_from([ring[(place[index] + 1) % count] for index in range(count)], mine)
    before = pick_from([ring[(place[index] - 1) % count] for index in range(count)], mine)
    return {"seq": after}, {"seq": before}


def core_mate():
    mine = lax.axis_index("dp")
    return {"dp": mine + 1 - 2 * lax.rem(mine, 2)}


def greet(*devices):
    barrier = pltpu.get_barrier_semaphore()
    for device in devices:
        pl.semaphore_signal(barrier, inc=1, device_id=device, device_id_type=MESH)
    return lambda: pl.semaphore_wait(barrier, len(devices))


def send(source, target, sems, device):
    return pltpu.make_async_remote_copy(
        src_ref=source, dst_ref=target, send_sem=sems[0], recv_sem=sems[1], device_id=device, device_id_type=MESH
    )


def gelu_and_slope(value):
    scale = 0.7978845608028654
    square = value * value
    bent = jnp.tanh(scale * value * (1.0 + 0.044715 * square))
    half = 0.5 * (1.0 + bent)
    slope = half + 0.5 * value * (1.0 - bent * bent) * (scale * (1.0 + 3.0 * 0.044715 * square))
    return value * half, slope


def ring_index(count, offset):
    ring = ring_of(count)
    place = {index: position for position, index in enumerate(ring)}
    mine = lax.axis_index("seq")
    return pick_from([ring[(place[index] + offset) % count] for index in range(count)], mine)


def chip_mates(width, ahead=False):
    chips = width // CORES
    mine = lax.axis_index("dp")
    return [{"dp": lax.rem(mine + (k if ahead else chips - k) * CORES, width)} for k in range(1, chips)]


class RingSum:
    def __init__(self, count, refs, sems, after, before, mate):
        self.half, self.far = count // 2, count - 1
        self.stash, self.core_out, self.core_in, self.right_in, self.left_in = refs
        self.core_sems, self.right_sems, self.left_sems = sems[0:2], sems[2:4], sems[4:6]
        self.after, self.before, self.mate = after, before, mate
        self.held = self.core_out.shape[0]
        self.block = self.stash.shape[1]
        self.cut = self.block // 2

    @staticmethod
    def scratch(count, block, depth):
        half = count // 2
        dma = pltpu.SemaphoreType.DMA
        return [
            pltpu.VMEM((count, block, depth), low),
            pltpu.VMEM((4, block, depth), low),
            pltpu.VMEM((count, block, depth), low),
            pltpu.VMEM((half, block, depth), low),
            pltpu.VMEM((half, block, depth), low),
            dma((4,)), dma((count,)), dma((half, 2)), dma((half, 2)), dma((half, 2)), dma((half, 2)),
        ]

    def core_copy(self, slot):
        place = slot % self.held
        sems = (self.core_sems[0].at[place], self.core_sems[1].at[slot])
        return send(self.core_out.at[place], self.core_in.at[slot], sems, self.mate)

    def rows(self, part):
        return pl.ds(part * self.cut, self.cut)

    def side_copy(self, way, slot, step, part):
        target, sems = ((self.right_in, self.right_sems), (self.left_in, self.left_sems))[way]
        sems = (sems[0].at[step, part], sems[1].at[step, part])
        rows = self.rows(part)
        return send(self.stash.at[slot, rows], target.at[step, rows], sems, (self.after, self.before)[way])

    def offer(self, slot, part, again):
        part = part.astype(low)
        self.stash[slot] = part[: self.block]

        @pl.when(again)
        def _():
            self.core_copy(slot).wait_send()

        self.core_out[slot % self.held] = part[self.block :]
        self.core_copy(slot).start()

    def begin(self):
        self.core_copy(self.far).wait_recv()
        for way in range(2):
            rows = self.rows(way)
            total = self.stash[self.far, rows].astype(full) + self.core_in[self.far, rows].astype(full)
            self.stash[self.far, rows] = total.astype(low)
            self.side_copy(way, self.far, 0, way).start()

    def step(self, step, turn):
        for way, arrived in ((0, self.right_in), (1, self.left_in)):
            slot = 2 * (self.half - step) - way
            part = 1 - way if turn == 0 else way
            rows = self.rows(part)
            if turn == 0:
                self.core_copy(slot).wait_recv()
            total = self.stash[slot, rows].astype(full) + self.core_in[slot, rows].astype(full)
            if step > 1 or turn == 1:
                self.side_copy(way, slot, step - 1, part).wait_recv()
                total = total + arrived[step - 1, rows].astype(full)
            self.stash[slot, rows] = total.astype(low)
            self.side_copy(way, slot, step, part).start()

    def finish(self):
        self.core_copy(0).wait_recv()
        total = self.stash[0].astype(full) + self.core_in[0].astype(full)
        last = self.half - 1
        for way in range(2):
            for part in range(2):
                self.side_copy(way, 0, last, part).wait_recv()
        return total + self.right_in[last].astype(full) + self.left_in[last].astype(full)

    def drain(self):
        for slot in range(self.held):
            self.core_copy(slot).wait_send()
        for way in range(2):
            self.side_copy(way, 0, 0, way).wait_send()
            for step in range(1, self.half):
                for part in range(2):
                    self.side_copy(way, 0, step, part).wait_send()


class RingGather:
    def __init__(self, count, own, found, sems, after, before, mate, keep_sem=None):
        self.half, self.far = count // 2, count - 1
        self.own, self.found, self.sems, self.keep_sem = own, found, sems, keep_sem
        self.after, self.before, self.mate = after, before, mate
        self.cut = own.shape[0] // 2

    @staticmethod
    def scratch(count):
        dma = pltpu.SemaphoreType.DMA
        return [dma((count, 2)), dma((count, 2)), dma((count,)), dma((count,))]

    def onward(self, way, slot, to, part):
        rows = pl.ds(part * self.cut, self.cut)
        source = self.own.at[rows] if slot is None else self.found.at[slot, 0, rows]
        sems = (self.sems[0].at[to, part], self.sems[1].at[to, part])
        return send(source, self.found.at[to, 0, rows], sems, (self.after, self.before)[way])

    def to_mate(self, slot):
        sems = (self.sems[2].at[slot], self.sems[3].at[slot])
        source = self.own if isinstance(slot, int) and slot == 0 else self.found.at[slot, 0]
        return send(source, self.found.at[slot, 1], sems, self.mate)

    def start(self):
        for turn in range(2):
            for way in range(2):
                self.onward(way, None, 1 + way, way if turn == 0 else 1 - way).start()
        self.to_mate(0).start()
        if self.keep_sem is None:
            self.found[0, 0] = self.own[...]
        else:
            self.keep().start()

    def keep(self):
        return pltpu.make_async_copy(self.own, self.found.at[0, 0], self.keep_sem)

    def hop(self, h, turn, last):
        for way in range(2):
            slot = 2 * h - 1 + way
            part = way if turn == 0 else 1 - way
            self.onward(way, slot, slot, part).wait_recv()
            if not last:
                self.onward(way, slot, slot + 2, part).start()
            elif turn == 0:
                self.onward(way, slot, self.far, part).start()
            if turn == 1:
                self.to_mate(slot).start()

    def last(self):
        for way in range(2):
            self.onward(way, self.far, self.far, way).wait_recv()
        self.to_mate(self.far).start()

    def drain(self):
        for slot in range(self.far + 1):
            self.to_mate(slot).wait_send()
        for slot in range(1, self.far + 1):
            for part in range(2):
                self.onward(0, self.far, slot, part).wait_send()
        if self.keep_sem is not None:
            self.keep().wait()


class RingTurn:
    def __init__(self, count, source, target, transit, sems, after, before):
        self.count, self.half = count, count // 2
        self.source, self.target, self.transit, self.sems = source, target, transit, sems
        self.after, self.before = after, before
        self.cut = source.shape[1] // 2

    @staticmethod
    def scratch(count, rows, columns):
        half = count // 2
        dma = pltpu.SemaphoreType.DMA
        return [
            pltpu.VMEM((2, half * (half - 1) // 2, rows, columns), low),
            dma((2, half * (half + 1) // 2)),
            dma((2, half * (half + 1) // 2)),
        ]

    def copy(self, way, hop, away):
        sign = 1 - 2 * way
        number = sum(range(hop)) if hop == 0 else sum(self.half - j + 1 for j in range(1, hop)) + away - hop
        if hop == 1:
            source = self.source.at[ring_index(self.count, sign * away)]
        else:
            source = self.transit.at[way, sum(self.half - j for j in range(1, hop - 1)) + away - hop]
        if away == hop:
            target = self.target.at[ring_index(self.count, sign * (1 - hop))]
        else:
            target = self.transit.at[way, sum(self.half - j for j in range(1, hop)) + away - hop - 1]
        if away == self.half:
            rows = pl.ds(way * self.cut, self.cut)
            source, target = source.at[rows], target.at[rows]
        sems = (self.sems[0].at[way, number], self.sems[1].at[way, number])
        return send(source, target, sems, (self.after, self.before)[way])

    def start(self):
        for away in range(self.half, 0, -1):
            for way in range(2):
                self.copy(way, 1, away).start()

    def hop(self, hop):
        for away in range(self.half, hop - 1, -1):
            for way in range(2):
                self.copy(way, hop, away).wait_recv()
                if away > hop:
                    self.copy(way, hop + 1, away).start()

    def drain(self):
        for hop in range(1, self.half + 1):
            for away in range(hop, self.half + 1):
                for way in range(2):
                    self.copy(way, hop, away).wait_send()


class RingScatter:
    def __init__(self, count, items, sems, after, before):
        self.count, self.half = count, count // 2
        self.items, self.sems = items, sems
        self.after, self.before = after, before

    @staticmethod
    def scratch(count, shapes):
        half = count // 2
        dma = pltpu.SemaphoreType.DMA
        arrived = [pltpu.VMEM((2, half) + shape, kind) for shape, kind in shapes]
        leaving = [pltpu.VMEM((2, 2) + shape, kind) for shape, kind in shapes]
        return arrived + leaving + [dma((len(shapes), 2, half)), dma((len(shapes), 2, half))]

    def columns(self, item, way):
        _, arrived, _, ways = self.items[item]
        wide = arrived.shape[-1]
        return pl.ds(way * (wide // 2), wide // 2) if len(ways) == 2 else pl.ds(0, wide)

    def copy(self, item, way, step):
        _, arrived, leaving, _ = self.items[item]
        source, target = leaving.at[way, step % 2], arrived.at[way, step]
        if step == 0:
            columns = self.columns(item, way)
            source, target = source.at[:, columns], target.at[:, columns]
        sems = (self.sems[0].at[item, way, step], self.sems[1].at[item, way, step])
        return send(source, target, sems, (self.after, self.before)[way])

    def begin(self, met=None):
        index = ring_index(self.count, self.half)
        for item, (value, _, leaving, ways) in enumerate(self.items):
            far = value(index).astype(leaving.dtype)
            for way in ways:
                leaving[way, 0] = far
        if met is not None:
            met()
        for item, (_, _, _, ways) in enumerate(self.items):
            for way in ways:
                self.copy(item, way, 0).start()

    def onward(self, step):
        for item, (value, arrived, leaving, ways) in enumerate(self.items):
            for way in range(2):
                offset = self.half - step
                mine = value(ring_index(self.count, offset if way == 0 else -offset))
                if step > 1:
                    self.copy(item, way, step - 1).wait_recv()
                    mine = mine + arrived[way, step - 1].astype(full)
                if step > 2 or (step == 2 and way in ways):
                    self.copy(item, way, step - 2).wait_send()
                leaving[way, step % 2] = mine.astype(leaving.dtype)
                if step == 1 and way in ways:
                    self.copy(item, way, 0).wait_recv()
                    columns = self.columns(item, way)
                    leaving[way, 1, :, columns] = (
                        leaving[way, 1, :, columns].astype(full) + arrived[way, 0, :, columns].astype(full)
                    ).astype(leaving.dtype)
                self.copy(item, way, step).start()

    def finish(self, item):
        value, arrived, _, _ = self.items[item]
        total = value(lax.axis_index("seq"))
        for way in range(2):
            self.copy(item, way, self.half - 1).wait_recv()
            total = total + arrived[way, self.half - 1].astype(full)
        return total

    def drain(self):
        for item, (_, _, _, ways) in enumerate(self.items):
            for way in range(2):
                for step in range(self.half - 2, self.half):
                    if step > 0 or way in ways:
                        self.copy(item, way, step).wait_send()


def feed_kernel(
    count, width, own, w_both_far, w_down_far, cotangent, total, feed_sum, down_own, down_others, hidden_far,
    w_both, w_down, hidden, feed, d_both, cot_rows, down_total, feed_others, feed_in, late_sem, cot_sem, cross_out,
    cross_in, *rest
):
    gather_sems, rest = rest[:4], rest[4:]
    ring_refs, ring_sems = rest[:5], rest[5:]
    half, chips = count // 2, width // CORES
    far = count - 1
    block, depth = own.shape
    units = w_down.shape[0]
    slice_f = units // chips
    tokens = count * 2 * block
    after, before = ring_sides(count)
    mate = core_mate()
    back, ahead = chip_mates(width), chip_mates(width, True)
    met = greet(after, before, mate, *back)
    gather = RingGather(count, own, feed, gather_sems, after, before, mate)
    ring = RingSum(count, ring_refs, ring_sems, after, before, mate)
    late = [
        pltpu.make_async_copy(w_both_far, w_both, late_sem.at[0]),
        pltpu.make_async_copy(w_down_far, w_down, late_sem.at[1]),
    ]
    save_hidden = pltpu.make_async_copy(hidden, hidden_far, late_sem.at[2])

    def cross(k):
        sems = (cross_out.at[k], cross_in.at[k])
        return send(feed_others.at[k - 1], feed_in.at[k - 1], sems, ahead[k - 1])

    def fetch(slot):
        return pltpu.make_async_copy(cotangent.at[slot], cot_rows.at[slot % 2], cot_sem.at[slot % 2])

    def fetched(slot):
        fetch(slot).wait()

        @pl.when(slot < far)
        def _():
            fetch(slot + 1).start()

        return cot_rows[slot % 2].reshape(2 * block, depth)

    def work(slot):
        back_all = lax.dot_general(fetched(slot), w_down[...], (NT, ((), ())), preferred_element_type=full)
        gather.to_mate(slot).wait_recv()
        rows = feed[slot].reshape(2 * block, depth)
        before_act = jnp.dot(rows, w_both[...], preferred_element_type=full)
        forth, back_parts = [], []
        for k in range(chips):
            start = 2 * k * slice_f
            gate, up = before_act[:, start : start + slice_f], before_act[:, start + slice_f : start + 2 * slice_f]
            active, slope = gelu_and_slope(gate)
            back = back_all[:, k * slice_f : (k + 1) * slice_f]
            forth.append(active * up)
            back_parts += [back * up * slope, back * active]
        hidden[slot] = jnp.concatenate(forth, axis=1).astype(low).reshape(2, block, units)
        d_rows = jnp.concatenate(back_parts, axis=1).astype(low)
        for k in range(chips):
            d_both[k, slot] = d_rows[:, 2 * k * slice_f : 2 * (k + 1) * slice_f].reshape(2, block, 2 * slice_f)
        part = lax.dot_general(d_rows, w_both[...], (NT, ((), ())), preferred_element_type=full)
        ring.offer(slot, part, slot >= ring.held)

    for copy in late:
        copy.start()
    fetch(0).start()
    met()
    gather.start()
    gather.hop(1, 0, half == 2)
    for copy in late:
        copy.wait()
    gather.hop(1, 1, half == 2)
    work(0)

    def advance(h, last):
        gather.hop(h, 0, last)
        work(2 * h - 3)
        gather.hop(h, 1, last)
        work(2 * h - 2)

    @pl.loop(2, half - 1)
    def _(h):
        advance(h, False)

    if half > 2:
        advance(half - 1, True)
    pl.loop(far - 2, far - 1)(work)
    gather.last()
    pl.loop(far - 1, far + 1)(work)
    save_hidden.start()

    pieces = 4
    wide = depth // pieces

    def grads(first, last):
        @pl.loop(first, last)
        def _(at):
            columns = pl.ds(pl.multiple_of((at % pieces) * wide, wide), wide)
            k = chips - 1 - at // pieces
            part = lax.dot_general(
                feed[:, :, :, columns].reshape(tokens, wide),
                d_both[k].reshape(tokens, 2 * slice_f),
                (TN, ((), ())),
                preferred_element_type=full,
            ).astype(low)

            @pl.when(k == 0)
            def _():
                feed_sum[columns] = part

            @pl.when(k > 0)
            def _():
                feed_others[jnp.maximum(k - 1, 0), columns] = part

    def down(slot):
        rows = fetched(slot)
        part = lax.dot_general(
            hidden[slot].reshape(2 * block, units), rows, (TN, ((), ())), preferred_element_type=full
        )

        @pl.when(slot == 0)
        def _():
            down_total[...] = part

        @pl.when(slot > 0)
        def _():
            down_total[...] += part

    fetch(0).start()
    ring.step(1, 0)
    ring.begin()
    grads(0, (chips - 1) * pieces)
    for k in range(1, chips):
        cross(k).start()
    ring.step(1, 1)
    steps = [(step, turn) for step in range(2, half) for turn in range(2)]
    ring_step = iter(steps)

    def next_step():
        for step, turn in [next(ring_step, (0, 0))]:
            if step > 0:
                ring.step(step, turn)

    next_step()
    grads((chips - 1) * pieces, chips * pieces)
    next_step()
    pl.loop(0, count // 2)(down)
    for _ in range(len(steps)):
        next_step()
    pl.loop(count // 2, count)(down)
    down_own[...] = down_total[:slice_f].astype(low)
    for k in range(1, chips):
        down_others[k - 1] = down_total[k * slice_f : (k + 1) * slice_f].astype(low)
    total[...] = ring.finish()
    for k in range(1, chips):
        cross(k).wait_recv()
    for at in range(pieces):
        rows = slice(at * wide, (at + 1) * wide)
        part = feed_sum[rows].astype(full)
        for k in range(1, chips):
            part = part + feed_in[k - 1, rows].astype(full)
        feed_sum[rows] = part.astype(low)
    save_hidden.wait()
    gather.drain()
    ring.drain()
    for k in range(1, chips):
        cross(k).wait_send()


def feed_forward(own, w_both, w_down, cotangent):
    count, width = lax.axis_size("seq"), lax.axis_size("dp")
    chips = width // CORES
    block, depth = own.shape
    units = w_down.shape[0]
    slice_f = units // chips
    whole = pl.BlockSpec(memory_space=pltpu.VMEM)
    dma = pltpu.SemaphoreType.DMA
    shapes = [
        ((block, depth), full), ((depth, 2 * slice_f), low), ((slice_f, depth), low),
        ((chips - 1, slice_f, depth), low), ((count, 2, block, units), low),
    ]
    far = pl.BlockSpec(memory_space=pl.ANY)
    return pl.pallas_call(
        partial(feed_kernel, count, width),
        in_specs=[whole, far, far, far],
        out_specs=[whole] * 4 + [far],
        out_shape=[jax.ShapeDtypeStruct(*shape) for shape in shapes],
        scratch_shapes=[
            pltpu.VMEM(w_both.shape, low),
            pltpu.VMEM(w_down.shape, low),
            pltpu.VMEM((count, 2, block, units), low),
            pltpu.VMEM((count, 2, block, depth), low),
            pltpu.VMEM((chips, count, 2, block, 2 * slice_f), low),
            pltpu.VMEM((2, 2, block, depth), low),
            pltpu.VMEM((units, depth), full),
            pltpu.VMEM((chips - 1, depth, 2 * slice_f), low),
            pltpu.VMEM((chips - 1, depth, 2 * slice_f), low),
            dma((3,)), dma((2,)), dma((chips,)), dma((chips,)),
            *RingGather.scratch(count),
            *RingSum.scratch(count, block, depth),
        ],
        compiler_params=pltpu.CompilerParams(collective_id=1, has_side_effects=True, vmem_limit_bytes=63 << 20),
        cost_estimate=pl.CostEstimate(
            flops=2 * 2 * count * block * depth * units * 9, bytes_accessed=40 << 20, transcendentals=0
        ),
    )(own, w_both, w_down, cotangent)


def seq_peer(count, step):
    place = lax.rem(lax.axis_index("seq") + (step + count), count)
    return {"seq": place}, place


def keep_column(marks, row):
    mark = jnp.broadcast_to(marks[row, :1], marks.shape[1:])
    padding = jnp.where(mark > 1.5, 1.0, 0.0)
    keep = 1.0 - (mark - 2.0 * padding)
    return jnp.transpose(keep)[:, :1], jnp.transpose(1.0 - padding)[:, :1]


def gate_terms(pre_rate, pre_inlet, soft):
    rate, inlet = jax.nn.sigmoid(pre_rate), jax.nn.sigmoid(pre_inlet)
    twice = -16.0 * rate * soft
    decay = jnp.exp(0.5 * twice)
    near = -twice * (
        1.0 + twice * (1 / 2 + twice * (1 / 6 + twice * (1 / 24 + twice * (1 / 120 + twice * (1 / 720)))))
    )
    rest = jnp.where(twice > -0.25, near, 1.0 - decay * decay)
    return rate, inlet, decay, rest, jnp.sqrt(rest)


def scan_rows(rate, value, backward):
    length, channels = rate.shape
    groups = length // 8
    rate = rate.reshape(groups, 8, channels)
    value = value.reshape(groups, 8, channels)
    place = lax.broadcasted_iota(jnp.int32, rate.shape, 1)
    for step in (1, 2, 4):
        keep = place < 8 - step if backward else place >= step
        move = 8 - step if backward else step
        earlier_rate = jnp.where(keep, pltpu.roll(rate, move, 1), 1.0)
        earlier_value = jnp.where(keep, pltpu.roll(value, move, 1), 0.0)
        value = value + rate * earlier_value
        rate = rate * earlier_rate
    product_in = jnp.ones((1, channels), full)
    state_in = jnp.zeros((1, channels), full)
    end = 0 if backward else 7
    products, states = [None] * groups, [None] * groups
    for group in reversed(range(groups)) if backward else range(groups):
        states[group] = value[group] + rate[group] * state_in
        products[group] = rate[group] * product_in
        product_in, state_in = products[group][end : end + 1], states[group][end : end + 1]
    return jnp.concatenate(products, axis=0), jnp.concatenate(states, axis=0)


def fold_states(count, arrived, backward):
    mine = lax.axis_index("seq")
    total = jnp.zeros(arrived.shape[2:], full)
    scale = jnp.ones(arrived.shape[2:], full)
    for step in range(1, count):
        there = (mine + step < count) if backward else (mine >= step)
        total = total + jnp.where(there, scale * arrived[step, 1], 0.0)
        scale = scale * arrived[step, 0]
    return total


def stack_rows(ref):
    pieces, rows, columns = ref.shape
    if rows % 16 == 0:
        return ref[...].reshape(pieces * rows, columns)
    return jnp.concatenate([ref[piece].astype(full) for piece in range(pieces)], axis=0).astype(ref.dtype)


def tail_factor(column, taps):
    length = column.shape[0]
    place = lax.broadcasted_iota(jnp.int32, (8, 1), 0)
    factor, run = jnp.where(place == 7, 1.0, 0.0), jnp.ones((1, 1), full)
    for back in range(1, taps - 1):
        run = run * column[length - back : length - back + 1]
        factor = jnp.where(place == 7 - back, run, factor)
    return factor


def front_kernel(
    count, width, own, cot_raw, resets, real_mask, gain_mix, gain_mlp, conv_kernel, decay_param, gate_rate, gate_input,
    w_gate, w_x, w_mix, w_feed_gate_far, w_feed_up_far, w_down,
    marks_all, w_both, gains, chan, cotangent, middle, feed_own, halo, ends, cot_all, down_all,
    gate_far, x_far, normed_far, pre_gate_far, branch_far, w_mix_far, conv_far, pre_rate_far, pre_inlet_far, rate_far,
    inlet_far, states_far, mixed_far,
    gate_all, x_all, normed, pre_gate, branch, w_mix_all, conv_low, pre_rate, pre_inlet, rate_mat, inlet_mat, states,
    mixed, w_feed_gate, w_feed_up, save_sem, own_marks, small, small_all, own_gates, gates_all, mix_all, rows_all, x_total, scale, turned, arrived,
    keep, product, state, ext, halo_out, halo_in, state_out, state_all, core_out, core_in, chip_out, chip_in,
    ring_out, ring_in, last_out, last_in, rows_out, rows_in, mate_out, mate_in, cross_out, cross_in, down_out, down_in,
    halo_sem, state_out_sem, state_in_sem, core_out_sem, core_in_sem, chip_out_sem, chip_in_sem, cot_sem, *rest
):
    gather_sems, turn_refs = rest[:4], rest[4:]
    half = count // 2
    chips = width // CORES
    block, depth = own.shape
    shard, channels = w_gate.shape
    own_channels, size = gate_rate.shape
    taps = conv_kernel.shape[0]
    slice_f = w_down.shape[0]
    mine = lax.axis_index("seq")
    after, before = ring_sides(count)
    mate = core_mate()
    back, ahead = chip_mates(width), chip_mates(width, True)
    peers = [None] + [seq_peer(count, step)[0] for step in range(1, count)]
    met = greet(mate, *back, *peers[1:])
    loads = [
        pltpu.make_async_copy(w_feed_gate_far, w_feed_gate, save_sem.at[14]),
        pltpu.make_async_copy(w_feed_up_far, w_feed_up, save_sem.at[15]),
    ]
    for copy in loads:
        copy.start()
    gather = RingGather(count, cotangent, cot_all, gather_sems, after, before, mate, cot_sem.at[0])
    turn = RingTurn(count, turned, arrived.at[0], turn_refs[0], turn_refs[1:], after, before)
    saves = [
        pltpu.make_async_copy(source, target, save_sem.at[at])
        for at, (source, target) in enumerate(
            (
                (gate_all, gate_far), (x_all, x_far), (normed, normed_far), (pre_gate, pre_gate_far),
                (branch, branch_far), (w_mix_all, w_mix_far), (conv_low, conv_far), (pre_rate, pre_rate_far),
                (pre_inlet, pre_inlet_far), (rate_mat, rate_far), (inlet_mat, inlet_far), (states, states_far),
                (mixed, mixed_far), (w_down, down_all.at[0]),
            )
        )
    ]
    moved = ((w_gate, gate_all), (small, small_all), (w_x, x_all), (own_gates, gates_all), (w_mix, mix_all))
    shared = ((0,), (0,), (1,), (1,), (0, 1))

    def rows_copy(what, k):
        source, target = ((own, rows_all), (own_marks, marks_all))[what]
        return send(source, target.at[k], (rows_out.at[what, k], rows_in.at[what, k]), back[k - 1])

    def mate_copy(what, k):
        source, target = ((own, rows_all), (own_marks, marks_all))[what]
        source = source if k == 0 else target.at[k]
        return send(source, target.at[chips + k], (mate_out.at[what, k], mate_in.at[what, k]), mate)

    def ring_copy(way, hop, item):
        source, target = moved[item]
        index = mine if hop == 1 else ring_index(count, (1 - hop) if way == 0 else (hop - 1))
        return send(
            source if hop == 1 else target.at[index],
            target.at[index],
            (ring_out.at[way, hop, item], ring_in.at[way, hop, item]),
            after if way == 0 else before,
        )

    def last_copy(way, item):
        index = ring_index(count, (1 - half) if way == 0 else (half - 1))
        ref = moved[item][1].at[index]
        if len(shared[item]) == 2:
            ref = ref.at[:, pl.ds(way * (depth // 2), depth // 2)]
        return send(ref, ref, (last_out.at[way, item], last_in.at[way, item]), after if way == 0 else before)

    def cross(slot, k):
        offset = half if slot == count - 1 else (slot + 1) // 2 * (1 - 2 * (slot % 2))
        origin = ring_index(count, offset)
        sems = (cross_out.at[k, slot], cross_in.at[k, slot])
        return send(arrived.at[0, origin], arrived.at[k, origin], sems, back[k - 1])

    def cross_down(k):
        return send(w_down, down_all.at[k], (down_out.at[k], down_in.at[k]), back[k - 1])

    def halo_copy():
        return send(halo_out, halo_in, (halo_sem.at[0], halo_sem.at[1]), peers[1])

    def state_copy(step):
        return send(state_out, state_all.at[step], (state_out_sem.at[step], state_in_sem.at[step]), peers[step])

    def core_copy(k):
        return send(core_out.at[k], core_in.at[k], (core_out_sem.at[k], core_in_sem.at[k]), mate)

    def chip_copy(k):
        return send(chip_out.at[k], chip_in.at[k], (chip_out_sem.at[k], chip_in_sem.at[k]), ahead[k - 1])

    def send_item(item):
        ring_copy(0, 1, item).start()
        ring_copy(1, 1, item).start()
        moved[item][1][mine] = moved[item][0][...]

    real = real_mask[...].astype(full)
    own_marks[...] = jnp.broadcast_to(resets[...].astype(full) + 2.0 * (1.0 - real), own_marks.shape)
    tap_rows = conv_kernel[...].astype(full)
    padding = jnp.zeros((1, shard - own_channels), full)
    pieces = [jnp.concatenate([tap_rows[tap : tap + 1], padding], axis=1) for tap in range(taps)]
    pieces.append(jnp.concatenate([decay_param[...].astype(full), padding], axis=1))
    pieces += [gain_mix[...].astype(full).reshape(1, shard), gain_mlp[...].astype(full).reshape(1, shard)]
    place = lax.broadcasted_iota(jnp.int32, (16, shard), 0)
    total = jnp.zeros((16, shard), full)
    for at, piece in enumerate(pieces):
        total = jnp.where(place == at, piece, total)
    small[...] = total.astype(low)
    own_gates[...] = jnp.concatenate([gate_rate[...].astype(full), gate_input[...].astype(full)], axis=1).astype(low)
    met()
    send_item(0)
    mate_copy(0, 0).start()
    mate_copy(1, 0).start()
    for k in range(1, chips):
        rows_copy(0, k).start()
        rows_copy(1, k).start()
    for item in range(1, len(moved)):
        send_item(item)
    rows_all[0] = own[...]
    marks_all[0] = own_marks[...]
    _, real = keep_column(marks_all, 0)
    cotangent[...] = (cot_raw[...].astype(full) * real).astype(low)
    saves[13].start()
    for k in range(1, chips):
        cross_down(k).start()
    for k in range(1, chips):
        for what in range(2):
            rows_copy(what, k).wait_recv()
            mate_copy(what, k).start()
    for k in range(chips):
        for what in range(2):
            mate_copy(what, k).wait_recv()
    for row in range(width):
        values = rows_all[row].astype(full)
        scale[row] = lax.rsqrt(jnp.mean(values * values, axis=-1, keepdims=True) + epsilon)

    def work(index, first):
        columns = pl.ds(pl.multiple_of(index * shard, shard), shard)
        gain = small_all[index].astype(full)[taps + 1 : taps + 2]
        values = rows_all[:, :, columns].astype(full)
        part = (values * scale[...] * gain).astype(low).reshape(width * block, shard)
        normed[:, columns] = part
        for weight, target in ((gate_all, pre_gate), (x_all, x_total)):
            term = jnp.dot(part, weight[index], preferred_element_type=full).reshape(width, block, channels)
            if first:
                target[...] = term
            else:
                target[...] += term

    work(mine, True)
    for copy in loads:
        copy.wait()
    for at in range(count):
        columns = slice(at * slice_f, (at + 1) * slice_f)
        turned[at] = jnp.concatenate(
            [w_feed_gate[:, columns].astype(full), w_feed_up[:, columns].astype(full)], axis=1
        ).astype(low)
    arrived[0, mine] = turned[mine]
    for k in range(1, chips):
        cross(0, k).start()
    for hop in range(1, half):
        for item in range(len(moved)):
            for way in range(2):
                ring_copy(way, hop, item).wait_recv()
                if hop < half - 1:
                    ring_copy(way, hop + 1, item).start()
                elif way in shared[item]:
                    last_copy(way, item).start()
            if item == 2:
                for way in range(2):
                    work(ring_index(count, -hop if way == 0 else hop), False)
    for item in range(3):
        last_copy(shared[item][0], item).wait_recv()
    work(ring_index(count, half), False)
    branch[...] = x_total[...].astype(low)
    for item in range(3, len(moved)):
        for way in shared[item]:
            last_copy(way, item).wait_recv()

    for row in range(width):
        column, _ = keep_column(marks_all, row)
        keep[row, :8] = jnp.ones((8, 1), full)
        keep[row, 8:] = column
        halo_out[row] = branch[row, block - 16 :].astype(full)[8:] * tail_factor(column, taps)
    halo_copy().start()
    turn.start()
    gather.start()
    entries = jnp.concatenate([small_all[at].astype(full)[:8, :own_channels] for at in range(count)], axis=1)
    place = lax.broadcasted_iota(jnp.int32, entries.shape, 0)
    decay_row = entries[taps : taps + 1]
    entries = jnp.where(place == taps, jax.nn.softplus(decay_row), entries)
    chan[...] = jnp.where(place == taps + 1, jax.nn.sigmoid(decay_row), entries)
    entries = jnp.concatenate([small_all[at].astype(full)[:8] for at in range(count)], axis=1)
    gains[...] = jnp.concatenate([entries[taps + 1 : taps + 3], jnp.zeros((6, depth), full)], axis=0)
    w_mix_all[...] = stack_rows(mix_all)
    for copy in saves[:6]:
        copy.start()
    entries = stack_rows(gates_all)
    for at in range(channels // size):
        rows = slice(at * size, (at + 1) * size)
        for target, first in ((rate_mat, 0), (inlet_mat, size)):
            parts = [entries[rows].astype(full)[:, first : first + size]]
            if at > 0:
                parts.insert(0, jnp.zeros((size, at * size), full))
            if at + 1 < channels // size:
                parts.append(jnp.zeros((size, channels - (at + 1) * size), full))
            target[rows] = jnp.concatenate(parts, axis=1).astype(low)

    halo_copy().wait_recv()
    soft = chan[taps : taps + 1]
    state_out[...] = jnp.zeros_like(state_out)

    @pl.loop(0, width)
    def _(row):
        from_before = jnp.where(mine > 0, halo_in[row], 0.0)
        halo[row] = from_before
        ext[:8] = from_before
        ext[8:] = branch[row].astype(full)
        valid = jnp.ones((block, 1), full)
        total = jnp.zeros((block, channels), full)
        for tap in range(taps):
            total = total + chan[tap : tap + 1] * valid * ext[8 - tap : 8 - tap + block]
            valid = valid * keep[row, 8 - tap : 8 - tap + block]
        conv = total.astype(low)
        conv_low[row] = conv
        rate_in = lax.dot_general(conv, rate_mat[...], (NT, ((), ())), preferred_element_type=full)
        inlet_in = lax.dot_general(conv, inlet_mat[...], (NT, ((), ())), preferred_element_type=full)
        pre_rate[row] = rate_in
        pre_inlet[row] = inlet_in
        _, inlet, decay, _, root = gate_terms(rate_in, inlet_in, soft)
        kept = keep[row, 8:]
        inflow = conv.astype(full) * inlet * ((1.0 - kept) + kept * root)
        row_product, row_state = scan_rows(decay * kept, inflow, False)
        product[row] = row_product
        state[row] = row_state
        state_out[0, pl.ds(row, 1)] = row_product[block - 1 :]
        state_out[1, pl.ds(row, 1)] = row_state[block - 1 :]

    for copy in saves[6:11]:
        copy.start()

    def background(h):
        turn.hop(h)
        for slot in (2 * h - 1, 2 * h) if h < half else (count - 1,):
            for k in range(1, chips):
                cross(slot, k).start()
        if h < half:
            gather.hop(h, 0, h == half - 1)
            gather.hop(h, 1, h == half - 1)
        else:
            gather.last()

    for step in range(1, count):
        state_copy(step).start()
    background(1)
    for step in range(1, count):
        state_copy(step).wait_recv()
    ends[0] = fold_states(count, state_all, False)
    ends[1] = state_out[0]

    def close(row):
        row_states = state[row] + product[row] * ends[0, pl.ds(row, 1)]
        states[row] = row_states
        active, _ = gelu_and_slope(pre_gate[row])
        row_mixed = (row_states * active).astype(low)
        mixed[row] = row_mixed
        return jnp.dot(row_mixed, w_mix_all[...], preferred_element_type=full)

    @pl.loop(0, chips)
    def _(at):
        k = chips - 1 - at
        core_out[k] = close(chips + k).astype(low)
        core_copy(k).start()

    @pl.loop(0, chips - 1)
    def _(at):
        k = chips - 1 - at
        part = close(k)
        core_copy(k).wait_recv()
        chip_out[k] = (part + core_in[k].astype(full)).astype(low)

    for k in range(chips - 1, 0, -1):
        chip_copy(k).start()
    part = close(0)
    background(2)
    core_copy(0).wait_recv()
    total = part + core_in[0].astype(full) + own[...].astype(full)
    for k in range(1, chips):
        chip_copy(k).wait_recv()
        total = total + chip_in[k].astype(full)
    for copy in saves[11:13]:
        copy.start()
    middle[...] = total
    scaled = total * lax.rsqrt(jnp.mean(total * total, axis=-1, keepdims=True) + epsilon)
    feed_own[...] = (scaled * gains[1:2]).astype(low)
    for h in range(3, half + 1):
        background(h)
    for k in range(chips):
        if k > 0:
            cross_down(k).wait_recv()
            for slot in range(count):
                cross(slot, k).wait_recv()
        w_both[:, 2 * k * slice_f : 2 * (k + 1) * slice_f] = arrived[k].reshape(depth, 2 * slice_f)
    for slot in range(count):
        gather.to_mate(slot).wait_recv()

    for copy in saves:
        copy.wait()
    for item in range(len(moved)):
        for way in range(2):
            for hop in range(1, half):
                ring_copy(way, hop, item).wait_send()
            if way in shared[item]:
                last_copy(way, item).wait_send()
    for what in range(2):
        for k in range(chips):
            mate_copy(what, k).wait_send()
        for k in range(1, chips):
            rows_copy(what, k).wait_send()
    for k in range(1, chips):
        cross_down(k).wait_send()
        chip_copy(k).wait_send()
        for slot in range(count):
            cross(slot, k).wait_send()
    for k in range(chips):
        core_copy(k).wait_send()
    for step in range(1, count):
        state_copy(step).wait_send()
    halo_copy().wait_send()
    turn.drain()
    gather.drain()


def forward(own, cotangent, resets, real_mask, *weights):
    conv_kernel, gate_rate, w_gate, w_mix, w_down = weights[2], weights[4], weights[6], weights[8], weights[11]
    count, width = lax.axis_size("seq"), lax.axis_size("dp")
    half, chips = count // 2, width // CORES
    block, depth = own.shape
    shard, part = w_gate.shape
    own_channels, size = gate_rate.shape
    channels = count * own_channels
    slice_f = w_down.shape[0]
    whole = pl.BlockSpec(memory_space=pltpu.VMEM)
    dma = pltpu.SemaphoreType.DMA
    rows = (width, block, channels)
    shapes = [
        ((width, 8, block), full), ((depth, 2 * chips * slice_f), low), ((8, depth), full), ((8, channels), full),
        ((block, depth), low), ((block, depth), full), ((block, depth), low), ((width, 8, channels), full),
        ((2, 8, channels), full), ((count, 2, block, depth), low), ((chips,) + w_down.shape, low),
    ]
    saved = [
        ((count, shard, part), low), ((count, shard, part), low), ((width * block, depth), low), (rows, full),
        (rows, low), ((channels, depth), low), (rows, low), (rows, full), (rows, full), ((channels, channels), low),
        ((channels, channels), low), (rows, full), (rows, low),
    ]
    return pl.pallas_call(
        partial(front_kernel, count, width),
        in_specs=[whole] * (4 + len(weights) - 3) + [pl.BlockSpec(memory_space=pl.ANY)] * 3,
        out_specs=[whole] * (len(shapes) - 2) + [pl.BlockSpec(memory_space=pl.ANY)] * (len(saved) + 2),
        out_shape=[jax.ShapeDtypeStruct(*shape) for shape in shapes + saved],
        scratch_shapes=[
            *[pltpu.VMEM(*shape) for shape in saved],
            pltpu.VMEM(weights[9].shape, low),
            pltpu.VMEM(weights[10].shape, low),
            dma((len(saved) + 3,)),
            pltpu.VMEM((8, block), full),
            pltpu.VMEM((16, shard), low),
            pltpu.VMEM((count, 16, shard), low),
            pltpu.VMEM((own_channels, 2 * size), low),
            pltpu.VMEM((count, own_channels, 2 * size), low),
            pltpu.VMEM((count,) + w_mix.shape, low),
            pltpu.VMEM((width, block, depth), low),
            pltpu.VMEM(rows, full),
            pltpu.VMEM((width, block, 1), full),
            pltpu.VMEM((count, shard, 2 * slice_f), low),
            pltpu.VMEM((chips, count, shard, 2 * slice_f), low),
            pltpu.VMEM((width, 8 + block, 1), full),
            pltpu.VMEM(rows, full),
            pltpu.VMEM(rows, full),
            pltpu.VMEM((8 + block, channels), full),
            pltpu.VMEM((width, 8, channels), full),
            pltpu.VMEM((width, 8, channels), full),
            pltpu.VMEM((2, 8, channels), full),
            pltpu.VMEM((count, 2, 8, channels), full),
            *[pltpu.VMEM((chips, block, depth), low)] * 4,
            dma((2, half, 5)), dma((2, half, 5)), dma((2, 5)), dma((2, 5)),
            dma((2, chips)), dma((2, chips)), dma((2, chips)), dma((2, chips)),
            dma((chips, count)), dma((chips, count)), dma((chips,)), dma((chips,)),
            dma((2,)), dma((count,)), dma((count,)), dma((chips,)), dma((chips,)), dma((chips,)), dma((chips,)), dma((1,)),
            *RingGather.scratch(count),
            *RingTurn.scratch(count, shard, 2 * slice_f),
        ],
        compiler_params=pltpu.CompilerParams(collective_id=2, has_side_effects=True, vmem_limit_bytes=63 << 20),
        cost_estimate=pl.CostEstimate(
            flops=6 * width * block * depth * channels, bytes_accessed=60 << 20, transcendentals=0
        ),
    )(own, cotangent, resets, real_mask, *weights)


def back_kernel(
    count, width, taps, gains, marks, chan, halo, ends, d_feed_far, middle_far, cotangent_far, w_down_far, w_mix_far,
    mixed_far, rate_far, inlet_far, conv_far, down_far,
    pre_gate, pre_rate, pre_inlet, states, branch, hidden, down_others, feed_sum,
    output, d_middle, d_pre_gate, d_branch, grad_mix, gate_grads, small_grads, gain_share, down_sum, feed_gate, feed_up,
    d_feed, middle, cotangent, w_down, w_mix, mixed, rate_mat, inlet_mat, conv_low, down_own,
    gate_rows, rate_rows, inlet_rows, state_rows, branch_rows,
    hidden_rows, keep, mix_rows, mix_grads, later, local, shift, ext, d_rate, d_inlet, sums, halo_out, halo_in,
    state_out, state_all, down_in, feed_parts, late_sem, row_sem, hidden_sem, *rest
):
    ring_refs, rest = rest[:5], rest[5:]
    ring_sems, rest = rest[:6], rest[6:]
    (arrived, leaving), mix_sems, rest = rest[:2], rest[2:4], rest[4:]
    halo_sem, state_out_sem, state_in_sem, chip_out, chip_in, mate_out, mate_in, cross_out, cross_in = rest[:9]
    turn_refs = rest[9:]
    half = count // 2
    chips = width // CORES
    far = count - 1
    block, depth = middle.shape
    channels = chan.shape[1]
    own_channels = channels // count
    size = gate_grads.shape[-1] // 2
    mine = lax.axis_index("seq")
    after, before = ring_sides(count)
    mate = core_mate()
    back, ahead = chip_mates(width), chip_mates(width, True)
    peers = [None] + [seq_peer(count, -step)[0] for step in range(1, count)]
    met = greet(mate, *back, *peers[1:])
    ring = RingSum(count, ring_refs, ring_sems, after, before, mate)
    items = [(lambda index: mix_grads[index].astype(full), arrived, leaving, (0, 1))]
    scatter = RingScatter(count, items, mix_sems, after, before)
    turn = RingTurn(count, feed_sum, feed_parts, turn_refs[0], turn_refs[1:], after, before)

    def chips_copy(k):
        return send(mix_rows.at[0], mix_rows.at[k], (chip_out.at[k], chip_in.at[k]), back[k - 1])

    def mate_copy(k):
        return send(mix_rows.at[k], mix_rows.at[chips + k], (mate_out.at[k], mate_in.at[k]), mate)

    def cross(k):
        return send(down_others.at[k - 1], down_in.at[k - 1], (cross_out.at[k], cross_in.at[k]), ahead[k - 1])

    late = [
        pltpu.make_async_copy(source, target, late_sem.at[at])
        for at, (source, target) in enumerate(
            (
                (d_feed_far, d_feed), (middle_far, middle), (cotangent_far, cotangent), (w_down_far, w_down),
                (mixed_far, mixed), (w_mix_far, w_mix), (rate_far, rate_mat), (inlet_far, inlet_mat),
                (conv_far, conv_low), (down_far, down_own), (feed_sum.at[mine], feed_parts.at[mine]),
            )
        )
    ]
    streams = (
        ((pre_gate, gate_rows), (pre_rate, rate_rows), (states, state_rows)),
        ((pre_rate, rate_rows), (pre_inlet, inlet_rows), (states, state_rows), (branch, branch_rows)),
    )

    def row_copies(which, row):
        return [
            pltpu.make_async_copy(source.at[row], target.at[row % 2], row_sem.at[at, row % 2])
            for at, (source, target) in enumerate(streams[which])
        ]

    def row_start(which, row):
        for copy in row_copies(which, row):
            copy.start()

    def row_ready(which, row):
        for copy in row_copies(which, row):
            copy.wait()

        @pl.when(row + 1 < width)
        def _():
            row_start(which, row + 1)

        return row % 2

    def halo_copy():
        return send(halo_out, halo_in, (halo_sem.at[0], halo_sem.at[1]), peers[1])

    def state_copy(step):
        return send(state_out, state_all.at[step], (state_out_sem.at[step], state_in_sem.at[step]), peers[step])

    def fetch(at):
        return pltpu.make_async_copy(hidden.at[far - at], hidden_rows.at[at % 2], hidden_sem.at[at % 2])

    for copy in late[:4]:
        copy.start()
    fetch(0).start()
    for copy in late[4:]:
        copy.start()
    row_start(0, 0)
    for copy in late[:3]:
        copy.wait()

    values, arriving = middle[...], d_feed[...]
    scale = lax.rsqrt(jnp.mean(values * values, axis=-1, keepdims=True) + epsilon)
    normed = values * scale
    scaled = arriving * gains[1:2]
    gain_share[...] = jnp.sum(arriving * normed, axis=0, keepdims=True)
    total = cotangent[...].astype(full) + scale * (
        scaled - normed * jnp.mean(scaled * normed, axis=-1, keepdims=True)
    )
    d_middle[...] = total
    mix_rows[0] = total.astype(low)
    met()
    for k in range(1, chips):
        chips_copy(k).start()
    mate_copy(0).start()
    turn.start()

    def offer(at):
        slot = far - at
        fetch(at).wait()

        @pl.when(at < far)
        def _():
            fetch(at + 1).start()

        rows = hidden_rows[at % 2].reshape(2 * block, hidden.shape[-1])
        ring.offer(slot, jnp.dot(rows, w_down[...], preferred_element_type=full), at >= ring.held)

    late[3].wait()
    pl.loop(0, 3)(offer)
    ring.begin()
    ring.step(1, 0)
    pl.loop(3, count)(offer)
    for k in range(1, chips):
        chips_copy(k).wait_recv()
        mate_copy(k).start()
    for k in range(1, chips):
        cross(k).start()
    ring.step(1, 1)
    turn.hop(1)
    for copy in late[4:6]:
        copy.wait()
    for k in range(chips):
        mate_copy(k).wait_recv()
    tokens = width * block
    rows = mixed[...].reshape(tokens, channels)
    wide = depth // 4
    for at in range(4):
        part = lax.dot_general(
            rows,
            mix_rows[:, :, at * wide : (at + 1) * wide].reshape(tokens, wide),
            (TN, ((), ())),
            preferred_element_type=full,
        )
        for piece in range(count):
            mix_grads[piece, :, at * wide : (at + 1) * wide] = part[
                piece * own_channels : (piece + 1) * own_channels
            ].astype(low)
    scatter.begin()

    soft, soft_slope = chan[taps : taps + 1], chan[taps + 1 : taps + 2]
    state_out[0] = ends[1]
    state_out[1] = jnp.zeros_like(ends[1])
    sums[...] = jnp.zeros_like(sums)

    def adjoint_row(row):
        at = row_ready(0, row)
        column, real = keep_column(marks, row)
        keep[row, :8] = jnp.ones((8, 1), full)
        keep[row, 8:] = column
        sums[taps + 2 : taps + 3] += jnp.sum(real)
        d_mixed = lax.dot_general(mix_rows[row], w_mix[...], (NT, ((), ())), preferred_element_type=full)
        active, slope = gelu_and_slope(gate_rows[at])
        d_pre_gate[row] = (d_mixed * state_rows[at] * slope).astype(low)
        decay = jnp.exp(-8.0 * jax.nn.sigmoid(rate_rows[at]) * soft)
        sums[taps + 1 : taps + 2] += jnp.sum(decay * real, axis=0, keepdims=True)
        shift[:block] = decay * column
        shift[block:] = jnp.ones((8, channels), full)
        row_later, row_local = scan_rows(shift[1 : block + 1], d_mixed * active, True)
        later[row] = row_later
        local[row] = row_local
        state_out[1, pl.ds(row, 1)] = shift[:1] * row_local[:1]

    if half > 2:
        ring.step(2, 0)
    pl.loop(0, width // 2)(adjoint_row)
    if half > 2:
        ring.step(2, 1)
    pl.loop(width // 2, width)(adjoint_row)
    row_start(1, 0)
    for step in range(1, count):
        state_copy(step).start()
    scatter.onward(1)
    turn.hop(2)
    for copy in late[6:]:
        copy.wait()
    for step in range(1, count):
        state_copy(step).wait_recv()
    sums[8:16] = fold_states(count, state_all, True)

    def gate_row(row):
        at = row_ready(1, row)
        column = keep[row, 8:]
        rate, inlet, decay, _, root = gate_terms(rate_rows[at], inlet_rows[at], soft)
        conv = conv_low[row].astype(full)
        adjoint = local[row] + later[row] * sums[pl.ds(8 + row, 1)]
        shift[:8] = jnp.broadcast_to(ends[0, pl.ds(row, 1)], (8, channels))
        shift[8:] = state_rows[at]
        previous = shift[7 : 7 + block]
        mult = (1.0 - column) + column * root
        d_log = adjoint * column * (decay * previous - conv * inlet * decay * decay / root)
        rate_part = (d_log * (-8.0 * soft) * rate * (1.0 - rate)).astype(low)
        inlet_part = (adjoint * conv * mult * inlet * (1.0 - inlet)).astype(low)
        d_rate[row] = rate_part
        d_inlet[row] = inlet_part
        sums[taps : taps + 1] += jnp.sum(d_log * (-8.0 * rate), axis=0, keepdims=True) * soft_slope
        through = (
            adjoint * inlet * mult
            + jnp.dot(rate_part, rate_mat[...], preferred_element_type=full)
            + jnp.dot(inlet_part, inlet_mat[...], preferred_element_type=full)
        )
        ext[:8] = halo[row]
        ext[8:] = branch_rows[at].astype(full)
        place = lax.broadcasted_iota(jnp.int32, (8, 1), 0)
        valid = jnp.ones((block, 1), full)
        branch_part = jnp.zeros((block, channels), full)
        tail = jnp.zeros((8, channels), full)
        for tap in range(taps):
            moved = valid * through
            sums[tap : tap + 1] += jnp.sum(moved * ext[8 - tap : 8 - tap + block], axis=0, keepdims=True)
            moved = moved * chan[tap : tap + 1]
            if tap == 0:
                branch_part = moved
            else:
                shift[:block] = moved
                shift[block:] = jnp.zeros((8, channels), full)
                branch_part = branch_part + shift[tap : tap + block]
                for j in range(1, tap + 1):
                    tail = tail + jnp.where(place == 8 - j, moved[tap - j : tap - j + 1], 0.0)
            valid = valid * keep[row, 8 - tap : 8 - tap + block]
        local[row] = branch_part
        halo_out[row] = tail

    pl.loop(0, width // 2)(gate_row)
    if half > 2:
        scatter.onward(2)
    for step in range(3, half):
        ring.step(step, 0)
        ring.step(step, 1)
    if half > 2:
        turn.hop(3)
    pl.loop(width // 2, width)(gate_row)
    halo_copy().start()
    rows = conv_low[...].reshape(tokens, channels)
    both = [
        lax.dot_general(part[...].reshape(tokens, channels), rows, (TN, ((), ())), preferred_element_type=full)
        for part in (d_rate, d_inlet)
    ]
    for piece in range(count):
        first = piece * own_channels
        at = first // size * size
        gate_grads[piece] = jnp.concatenate(
            [part[first : first + own_channels, at : at + size] for part in both], axis=1
        ).astype(low)
    for step in range(3, half):
        scatter.onward(step)
        turn.hop(step + 1)
    halo_copy().wait_recv()

    @pl.loop(0, width)
    def _(row):
        column = keep[row, 8:]
        arriving = jnp.where(mine < count - 1, halo_in[row] * tail_factor(column, taps), 0.0)
        local[row, block - 8 :] += arriving
        d_branch[row] = local[row].astype(low)

    for piece in range(count):
        entries = sums[:8, piece * own_channels : (piece + 1) * own_channels]
        small_grads[piece] = jnp.concatenate([entries, jnp.zeros((8, 128 - own_channels), full)], axis=1)
    total = down_own[...].astype(full)
    for k in range(1, chips):
        cross(k).wait_recv()
        total = total + down_in[k - 1].astype(full)
    down_sum[...] = total.astype(low)
    _, real = keep_column(marks, 0)
    output[...] = ((middle[...] + ring.finish()) * real).astype(low)

    wide = feed_parts.shape[-1] // 2
    for target, columns in ((feed_gate, slice(0, wide)), (feed_up, slice(wide, 2 * wide))):
        parts = [feed_parts[at].astype(full)[:, columns] for at in range(count)]
        target[...] = jnp.concatenate(parts, axis=1).astype(low)
    grad_mix[...] = scatter.finish(0).astype(low)
    ring.drain()
    scatter.drain()
    turn.drain()
    halo_copy().wait_send()
    for step in range(1, count):
        state_copy(step).wait_send()
    for k in range(chips):
        mate_copy(k).wait_send()
    for k in range(1, chips):
        chips_copy(k).wait_send()
        cross(k).wait_send()


def mix_back(taps, size, near, late, rows, hidden, down_others, feed_sum):
    chan, middle = near[2], late[1]
    count, width = lax.axis_size("seq"), lax.axis_size("dp")
    chips = width // CORES
    block, depth = middle.shape
    channels = chan.shape[1]
    own_channels = channels // count
    whole = pl.BlockSpec(memory_space=pltpu.VMEM)
    far = pl.BlockSpec(memory_space=pl.ANY)
    dma = pltpu.SemaphoreType.DMA
    all_rows = (width, block, channels)
    shapes = [
        ((block, depth), low), ((block, depth), full), (all_rows, low), (all_rows, low),
        ((own_channels, depth), low), ((count, own_channels, 2 * size), low), ((count, 8, 128), full),
        ((1, depth), full), (late[-1].shape, low),
        *[((feed_sum.shape[1], feed_sum.shape[2] // 2 * count), low)] * 2,
    ]
    operands = (*near, *late, *rows, hidden, down_others, feed_sum)
    return pl.pallas_call(
        partial(back_kernel, count, width, taps),
        in_specs=[whole] * len(near) + [far] * (len(operands) - len(near)),
        out_specs=[whole] * len(shapes),
        out_shape=[jax.ShapeDtypeStruct(*shape) for shape in shapes],
        scratch_shapes=[
            *[pltpu.VMEM(each.shape, each.dtype) for each in late],
            *[pltpu.VMEM((2,) + each.shape[1:], each.dtype) for each in (*rows, hidden)],
            pltpu.VMEM((width, 8 + block, 1), full),
            pltpu.VMEM((width, block, depth), low),
            pltpu.VMEM((count, own_channels, depth), low),
            pltpu.VMEM(all_rows, full),
            pltpu.VMEM(all_rows, full),
            pltpu.VMEM((block + 8, channels), full),
            pltpu.VMEM((block + 8, channels), full),
            pltpu.VMEM(all_rows, low),
            pltpu.VMEM(all_rows, low),
            pltpu.VMEM((16, channels), full),
            pltpu.VMEM((width, 8, channels), full),
            pltpu.VMEM((width, 8, channels), full),
            pltpu.VMEM((2, 8, channels), full),
            pltpu.VMEM((count, 2, 8, channels), full),
            pltpu.VMEM(down_others.shape, low),
            pltpu.VMEM(feed_sum.shape, low),
            dma((len(late) + 1,)), dma((4, 2)), dma((2,)),
            *RingSum.scratch(count, block, depth),
            *RingScatter.scratch(count, [((own_channels, depth), low)]),
            dma((2,)), dma((count,)), dma((count,)), dma((chips,)), dma((chips,)), dma((chips,)), dma((chips,)),
            dma((chips,)), dma((chips,)),
            *RingTurn.scratch(count, *feed_sum.shape[1:]),
        ],
        compiler_params=pltpu.CompilerParams(collective_id=4, has_side_effects=True, vmem_limit_bytes=63 << 20),
        cost_estimate=pl.CostEstimate(
            flops=4 * width * block * channels * (depth + 2 * channels), bytes_accessed=60 << 20, transcendentals=0
        ),
    )(*operands)


def close_kernel(
    count, width, own, d_middle, gains, gain_share, gate_grads, small_grads, normed_far, d_pre_gate_far, d_branch_far,
    w_gate_far, w_x_far, d_inputs, out_gate, out_x, out_gates, out_small, out_gains,
    normed, d_pre_gate, d_branch, w_gate, w_x, late_sem, *rest
):
    travel, rest = rest[:10], rest[10:]
    core_out, core_in, chip_out, chip_in, gain_out, gain_width, gain_total, gain_seq = rest[:8]
    core_out_sem, core_in_sem, chip_out_sem, chip_in_sem, width_out, width_in, seq_out, seq_in = rest[8:16]
    half = count // 2
    chips = width // CORES
    block, depth = own.shape
    shard = out_gate.shape[0]
    share = depth // width
    my_width = lax.axis_index("dp")
    after, before = ring_sides(count)
    mate = core_mate()
    ahead = chip_mates(width, True)
    peers = [None] + [seq_peer(count, step) for step in range(1, count)]
    others = [None] + [lax.rem(my_width + step, width) for step in range(1, width)]
    met = greet(*[peer for peer, _ in peers[1:]], *[{"dp": place} for place in others[1:]])

    def product(grads):
        def at(index):
            columns = pl.ds(pl.multiple_of(index * shard, shard), shard)
            return lax.dot_general(normed[:, columns], grads[...], (TN, ((), ())), preferred_element_type=full)

        return at

    def stored(grads):
        return lambda index: grads[index].astype(full)

    values = (product(d_pre_gate), product(d_branch), stored(gate_grads), stored(small_grads))
    results = (out_gate, out_x, out_gates, out_small)
    items = list(zip(values, travel[:4], travel[4:8], ((0,), (1,), (1,), (0,))))
    scatter = RingScatter(count, items, travel[8:], after, before)

    late = [
        pltpu.make_async_copy(source, target, late_sem.at[at])
        for at, (source, target) in enumerate(
            (
                (normed_far, normed), (d_pre_gate_far, d_pre_gate), (d_branch_far, d_branch), (w_gate_far, w_gate),
                (w_x_far, w_x),
            )
        )
    ]

    def core_copy(k):
        return send(core_out.at[k], core_in.at[k], (core_out_sem.at[k], core_in_sem.at[k]), mate)

    def chip_copy(k):
        return send(chip_out.at[k], chip_in.at[k], (chip_out_sem.at[k], chip_in_sem.at[k]), ahead[k - 1])

    def width_copy(step):
        columns = pl.ds(pl.multiple_of(others[step] * share, share), share)
        sems = (width_out.at[step], width_in.at[step])
        return send(gain_out.at[:, columns], gain_width.at[step], sems, {"dp": others[step]})

    def seq_copy(step):
        return send(gain_total, gain_seq.at[step], (seq_out.at[step], seq_in.at[step]), peers[step][0])

    def through(row):
        return lax.dot_general(
            d_pre_gate[pl.ds(pl.multiple_of(row * block, block), block)],
            w_gate[...],
            (NT, ((), ())),
            preferred_element_type=full,
        ) + lax.dot_general(
            d_branch[pl.ds(pl.multiple_of(row * block, block), block)],
            w_x[...],
            (NT, ((), ())),
            preferred_element_type=full,
        )

    for copy in late:
        copy.start()
    for copy in late[:3]:
        copy.wait()
    scatter.begin(met)
    for copy in late[3:]:
        copy.wait()

    @pl.loop(0, chips)
    def _(at):
        k = chips - 1 - at
        core_out[k] = through(chips + k).astype(low)
        core_copy(k).start()

    scatter.onward(1)

    @pl.loop(0, chips - 1)
    def _(at):
        k = chips - 1 - at
        part = through(k)
        core_copy(k).wait_recv()
        chip_out[k] = (part + core_in[k].astype(full)).astype(low)

    for k in range(chips - 1, 0, -1):
        chip_copy(k).start()
    part = through(0)
    core_copy(0).wait_recv()
    total = part + core_in[0].astype(full)
    for k in range(1, chips):
        chip_copy(k).wait_recv()
        total = total + chip_in[k].astype(full)
    rows = own[...].astype(full)
    scale = lax.rsqrt(jnp.mean(rows * rows, axis=-1, keepdims=True) + epsilon)
    rows = rows * scale
    scaled = total * gains[:1]
    d_inputs[...] = (
        d_middle[...] + scale * (scaled - rows * jnp.mean(scaled * rows, axis=-1, keepdims=True))
    ).astype(low)
    gain_out[...] = jnp.zeros_like(gain_out)
    gain_out[:1] = jnp.sum(total * rows, axis=0, keepdims=True)
    gain_out[1:2] = gain_share[...]
    for step in range(1, width):
        width_copy(step).start()
    if half > 2:
        scatter.onward(2)
    columns = pl.ds(pl.multiple_of(my_width * share, share), share)
    gain_sum = gain_out[:, columns]
    for step in range(1, width):
        width_copy(step).wait_recv()
        gain_sum = gain_sum + gain_width[step]
    gain_total[...] = gain_sum
    for step in range(1, count):
        seq_copy(step).start()
    for step in range(3, half):
        scatter.onward(step)
    for step in range(1, count):
        seq_copy(step).wait_recv()
        gain_sum = gain_sum + gain_seq[step]
    out_gains[...] = gain_sum
    for item, result in enumerate(results):
        result[...] = scatter.finish(item).astype(result.dtype)
    scatter.drain()
    for step in range(1, count):
        seq_copy(step).wait_send()
    for step in range(1, width):
        width_copy(step).wait_send()
    for k in range(chips):
        core_copy(k).wait_send()
    for k in range(1, chips):
        chip_copy(k).wait_send()


def close(operands):
    own, _, _, _, gate_grads, small_grads, normed, d_pre_gate, d_branch, w_gate, w_x = operands
    count, width = lax.axis_size("seq"), lax.axis_size("dp")
    chips = width // CORES
    block, depth = own.shape
    channels = d_pre_gate.shape[1]
    shard, share = depth // count, depth // width
    whole = pl.BlockSpec(memory_space=pltpu.VMEM)
    dma = pltpu.SemaphoreType.DMA
    items = [
        ((shard, channels), low), ((shard, channels), low), (gate_grads.shape[1:], low), (small_grads.shape[1:], full),
    ]
    shapes = [
        ((block, depth), low), *[(shape, low if at < 2 else full) for at, (shape, _) in enumerate(items)],
        ((8, share), full),
    ]
    return pl.pallas_call(
        partial(close_kernel, count, width),
        in_specs=[whole] * (len(operands) - 5) + [pl.BlockSpec(memory_space=pl.ANY)] * 5,
        out_specs=[whole] * len(shapes),
        out_shape=[jax.ShapeDtypeStruct(*shape) for shape in shapes],
        scratch_shapes=[
            *[pltpu.VMEM(each.shape, low) for each in (normed, d_pre_gate, d_branch, w_gate, w_x)],
            dma((5,)),
            *RingScatter.scratch(count, items),
            *[pltpu.VMEM((chips, block, depth), low)] * 4,
            pltpu.VMEM((8, depth), full),
            pltpu.VMEM((width, 8, share), full),
            pltpu.VMEM((8, share), full),
            pltpu.VMEM((count, 8, share), full),
            dma((chips,)), dma((chips,)), dma((chips,)), dma((chips,)),
            dma((width,)), dma((width,)), dma((count,)), dma((count,)),
        ],
        compiler_params=pltpu.CompilerParams(collective_id=5, has_side_effects=True, vmem_limit_bytes=63 << 20),
        cost_estimate=pl.CostEstimate(
            flops=8 * normed.shape[0] * depth * channels, bytes_accessed=40 << 20, transcendentals=0
        ),
    )(*operands)


def lay_out_kernel(count, taps, *refs):
    for source, target in zip(refs[:8], refs[11:19]):
        target[...] = source[...].astype(target.dtype)
    gates, small, gains = refs[8:11]
    taps_out, rate_out, input_out, decay_out, log_out, mix_out, mlp_out = refs[19:]
    size = rate_out.shape[1]
    channels, share = decay_out.shape[1], mix_out.shape[1]
    rate_out[...] = gates[:, :size]
    input_out[...] = gates[:, size:]
    taps_out[...] = small[:taps, :channels]
    decay_out[...] = small[taps : taps + 1, :channels]
    log_out[...] = small[taps + 1 : taps + 2, :channels] / small[taps + 2 : taps + 3, :channels]
    mine = lax.axis_index("seq")
    total = jnp.zeros((8, share), full)
    for at in range(count):
        total = jnp.where(mine == at, gains[:, at * share : (at + 1) * share], total)
    mix_out[...] = total[:1]
    mlp_out[...] = total[1:2]


def lay_out(taps, arrays, gates, small, gains):
    count = lax.axis_size("seq")
    steps = 2

    def block(shape, by_rows):
        if by_rows:
            return pl.BlockSpec((shape[0] // steps, shape[1]), lambda at: (at, 0))
        return pl.BlockSpec((shape[0], shape[1] // steps), lambda at: (0, at))

    def whole(shape):
        return pl.BlockSpec(shape, lambda at: (0, 0))

    cuts = [block(array.shape, by_rows) for array, by_rows, _ in arrays]
    own_channels, both = gates.shape
    share = gains.shape[1] // count
    rest = [(taps, own_channels), (own_channels, both // 2), (own_channels, both // 2), (1, own_channels)]
    rest += [(1, own_channels), (1, share), (1, share)]
    return pl.pallas_call(
        partial(lay_out_kernel, count, taps),
        grid=(steps,),
        in_specs=cuts + [whole(each.shape) for each in (gates, small, gains)],
        out_specs=cuts + [whole(shape) for shape in rest],
        out_shape=[jax.ShapeDtypeStruct(array.shape, kind) for array, _, kind in arrays]
        + [jax.ShapeDtypeStruct(shape, full) for shape in rest],
        compiler_params=pltpu.CompilerParams(vmem_limit_bytes=63 << 20),
    )(*[array for array, _, _ in arrays], gates, small, gains)


def on_device(
    inputs,
    cotangent,
    resets,
    real_mask,
    gain_mix,
    w_branch_gate,
    w_branch_x,
    conv_kernel,
    gate_rate,
    gate_input,
    decay_param,
    w_mix_out,
    gain_mlp,
    w_mlp_gate,
    w_mlp_up,
    w_mlp_down,
):
    seq = lax.axis_size("seq")
    rows_own, length, depth = inputs.shape
    taps = conv_kernel.shape[1]
    block = rows_own * length
    tokens = block * lax.axis_size("dp")
    own_channels, size = gate_rate.shape
    shard, part_w = w_branch_x.shape
    rows = inputs.reshape(block, depth)
    (
        marks, w_both, gains, chan, cot_low, middle, feed_own, halo, ends, d_feed, w_down,
        w_gate_all, w_x_all, mixer_in, pre_gate, branch, w_mix_out, conv_low, pre_rate, pre_inlet, rate_mat, inlet_mat,
        states, mixed,
    ) = forward(
        rows, cotangent.reshape(block, depth), resets, real_mask, gain_mix, gain_mlp, conv_kernel.T,
        decay_param[None], gate_rate, gate_input, w_branch_gate, w_branch_x, w_mix_out, w_mlp_gate, w_mlp_up,
        w_mlp_down,
    )
    w_down = w_down.reshape(-1, depth)

    d_feed_own, feed_sum, down_own, down_others, hidden = feed_forward(feed_own, w_both, w_down, d_feed)

    (
        output, d_middle, d_pre_gate, d_branch, grad_mix_out, gate_grads, small_grads, gain_share, grad_down,
        feed_gate, feed_up,
    ) = mix_back(
        taps,
        size,
        (gains, marks, chan, halo, ends),
        (d_feed_own, middle, cot_low, w_down, w_mix_out, mixed, rate_mat, inlet_mat, conv_low, down_own),
        (pre_gate, pre_rate, pre_inlet, states, branch),
        hidden,
        down_others,
        feed_sum.reshape(seq, shard, -1),
    )

    grad_inputs, grad_gate, grad_x, grad_gates, grad_small, gains = close(
        (
            rows, d_middle, gains, gain_share, gate_grads, small_grads, mixer_in, d_pre_gate.reshape(tokens, part_w),
            d_branch.reshape(tokens, part_w), w_gate_all.reshape(depth, part_w), w_x_all.reshape(depth, part_w),
        )
    )
    (
        output, grad_inputs, grad_gate, grad_x, feed_gate, feed_up, grad_mix_out, grad_down,
        grad_taps, grad_rate, grad_input, grad_decay, decay_log, grad_gain_mix, grad_gain_mlp,
    ) = lay_out(
        taps,
        (
            (output, True, low), (grad_inputs, True, low), (grad_gate, True, full), (grad_x, True, full),
            (feed_gate, True, full), (feed_up, True, full), (grad_mix_out, False, full), (grad_down, False, full),
        ),
        grad_gates,
        grad_small,
        gains,
    )
    return (
        output[None],
        grad_inputs[None],
        grad_gain_mix[0],
        grad_gate,
        grad_x,
        grad_taps.T,
        grad_rate,
        grad_input,
        grad_decay[0],
        grad_mix_out,
        grad_gain_mlp[0],
        feed_gate,
        feed_up,
        grad_down,
        decay_log[0],
    )


def solution(mesh):
    placed = (
        P("dp", "seq", None),
        P("dp", "seq", None),
        P("dp", "seq"),
        P("dp", "seq"),
        P("seq"),
        P("seq", "dp"),
        P("seq", "dp"),
        P(("dp", "seq"), None),
        P(("dp", "seq"), None),
        P(("dp", "seq"), None),
        P(("dp", "seq")),
        P(("dp", "seq"), None),
        P("seq"),
        P("seq", "dp"),
        P("seq", "dp"),
        P(("dp", "seq"), None),
    )
    return jax.shard_map(
        on_device,
        mesh=mesh,
        in_specs=placed,
        out_specs=(
            P("dp", "seq", None),
            P("dp", "seq", None),
            P(("dp", "seq")),
            P("seq", "dp"),
            P("seq", "dp"),
            P(("dp", "seq"), None),
            P(("dp", "seq"), None),
            P(("dp", "seq"), None),
            P(("dp", "seq")),
            P(("dp", "seq"), None),
            P(("dp", "seq")),
            P("seq", "dp"),
            P("seq", "dp"),
            P(("dp", "seq"), None),
            P(("dp", "seq")),
        ),
        check_vma=False,
    )
```

```python
from functools import partial

import jax
import jax.numpy as jnp
from jax import lax
from jax.experimental import pallas as pl
from jax.experimental.pallas import tpu as pltpu
from jax.sharding import PartitionSpec as P

epsilon = 1e-06
low = jnp.bfloat16
full = jnp.float32
CORES = 2


def ring_of(count):
    deep = 4 if count % 4 == 0 else 1
    wide = count // deep
    walk = [(z, 0) for z in range(deep)]
    for turn, z in enumerate(reversed(range(deep))):
        across = list(range(1, wide))
        walk += [(z, y) for y in (across if turn % 2 == 0 else across[::-1])]
    return [z * wide + y for z, y in walk]


NT = ((1,), (1,))
TN = ((0,), (0,))


MESH = pl.DeviceIdType.MESH


def pick_from(table, index):
    found = table[0]
    for at in range(1, len(table)):
        found = jnp.where(index == at, table[at], found)
    return found


def ring_sides(count):
    ring = ring_of(count)
    place = {index: position for position, index in enumerate(ring)}
    mine = lax.axis_index("seq")
    after = pick_from([ring[(place[index] + 1) % count] for index in range(count)], mine)
    before = pick_from([ring[(place[index] - 1) % count] for index in range(count)], mine)
    return {"seq": after}, {"seq": before}


def core_mate():
    mine = lax.axis_index("dp")
    return {"dp": mine + 1 - 2 * lax.rem(mine, 2)}


def greet(*devices):
    barrier = pltpu.get_barrier_semaphore()
    for device in devices:
        pl.semaphore_signal(barrier, inc=1, device_id=device, device_id_type=MESH)
    return lambda: pl.semaphore_wait(barrier, len(devices))


def send(source, target, sems, device):
    return pltpu.make_async_remote_copy(
        src_ref=source, dst_ref=target, send_sem=sems[0], recv_sem=sems[1], device_id=device, device_id_type=MESH
    )


def gelu_and_slope(value):
    scale = 0.7978845608028654
    square = value * value
    bent = jnp.tanh(scale * value * (1.0 + 0.044715 * square))
    half = 0.5 * (1.0 + bent)
    slope = half + 0.5 * value * (1.0 - bent * bent) * (scale * (1.0 + 3.0 * 0.044715 * square))
    return value * half, slope


def ring_index(count, offset):
    ring = ring_of(count)
    place = {index: position for position, index in enumerate(ring)}
    mine = lax.axis_index("seq")
    return pick_from([ring[(place[index] + offset) % count] for index in range(count)], mine)


def chip_mates(width, ahead=False):
    chips = width // CORES
    mine = lax.axis_index("dp")
    return [{"dp": lax.rem(mine + (k if ahead else chips - k) * CORES, width)} for k in range(1, chips)]


class RingSum:
    def __init__(self, count, refs, sems, after, before, mate):
        self.half, self.far = count // 2, count - 1
        self.stash, self.core_out, self.core_in, self.right_in, self.left_in = refs
        self.core_sems, self.right_sems, self.left_sems = sems[0:2], sems[2:4], sems[4:6]
        self.after, self.before, self.mate = after, before, mate
        self.held = self.core_out.shape[0]
        self.block = self.stash.shape[1]
        self.cut = self.block // 2

    @staticmethod
    def scratch(count, block, depth):
        half = count // 2
        dma = pltpu.SemaphoreType.DMA
        return [
            pltpu.VMEM((count, block, depth), low),
            pltpu.VMEM((4, block, depth), low),
            pltpu.VMEM((count, block, depth), low),
            pltpu.VMEM((half, block, depth), low),
            pltpu.VMEM((half, block, depth), low),
            dma((4,)), dma((count,)), dma((half, 2)), dma((half, 2)), dma((half, 2)), dma((half, 2)),
        ]

    def core_copy(self, slot):
        place = slot % self.held
        sems = (self.core_sems[0].at[place], self.core_sems[1].at[slot])
        return send(self.core_out.at[place], self.core_in.at[slot], sems, self.mate)

    def rows(self, part):
        return pl.ds(part * self.cut, self.cut)

    def side_copy(self, way, slot, step, part):
        target, sems = ((self.right_in, self.right_sems), (self.left_in, self.left_sems))[way]
        sems = (sems[0].at[step, part], sems[1].at[step, part])
        rows = self.rows(part)
        return send(self.stash.at[slot, rows], target.at[step, rows], sems, (self.after, self.before)[way])

    def offer(self, slot, part, again):
        part = part.astype(low)
        self.stash[slot] = part[: self.block]

        @pl.when(again)
        def _():
            self.core_copy(slot).wait_send()

        self.core_out[slot % self.held] = part[self.block :]
        self.core_copy(slot).start()

    def begin(self):
        self.core_copy(self.far).wait_recv()
        for way in range(2):
            rows = self.rows(way)
            total = self.stash[self.far, rows].astype(full) + self.core_in[self.far, rows].astype(full)
            self.stash[self.far, rows] = total.astype(low)
            self.side_copy(way, self.far, 0, way).start()

    def step(self, step, turn):
        for way, arrived in ((0, self.right_in), (1, self.left_in)):
            slot = 2 * (self.half - step) - way
            part = 1 - way if turn == 0 else way
            rows = self.rows(part)
            if turn == 0:
                self.core_copy(slot).wait_recv()
            total = self.stash[slot, rows].astype(full) + self.core_in[slot, rows].astype(full)
            if step > 1 or turn == 1:
                self.side_copy(way, slot, step - 1, part).wait_recv()
                total = total + arrived[step - 1, rows].astype(full)
            self.stash[slot, rows] = total.astype(low)
            self.side_copy(way, slot, step, part).start()

    def finish(self):
        self.core_copy(0).wait_recv()
        total = self.stash[0].astype(full) + self.core_in[0].astype(full)
        last = self.half - 1
        for way in range(2):
            for part in range(2):
                self.side_copy(way, 0, last, part).wait_recv()
        return total + self.right_in[last].astype(full) + self.left_in[last].astype(full)

    def drain(self):
        for slot in range(self.held):
            self.core_copy(slot).wait_send()
        for way in range(2):
            self.side_copy(way, 0, 0, way).wait_send()
            for step in range(1, self.half):
                for part in range(2):
                    self.side_copy(way, 0, step, part).wait_send()


class RingGather:
    def __init__(self, count, own, found, sems, after, before, mate, keep_sem=None):
        self.half, self.far = count // 2, count - 1
        self.own, self.found, self.sems, self.keep_sem = own, found, sems, keep_sem
        self.after, self.before, self.mate = after, before, mate
        self.cut = own.shape[0] // 2

    @staticmethod
    def scratch(count):
        dma = pltpu.SemaphoreType.DMA
        return [dma((count, 2)), dma((count, 2)), dma((count,)), dma((count,))]

    def onward(self, way, slot, to, part):
        rows = pl.ds(part * self.cut, self.cut)
        source = self.own.at[rows] if slot is None else self.found.at[slot, 0, rows]
        sems = (self.sems[0].at[to, part], self.sems[1].at[to, part])
        return send(source, self.found.at[to, 0, rows], sems, (self.after, self.before)[way])

    def to_mate(self, slot):
        sems = (self.sems[2].at[slot], self.sems[3].at[slot])
        source = self.own if isinstance(slot, int) and slot == 0 else self.found.at[slot, 0]
        return send(source, self.found.at[slot, 1], sems, self.mate)

    def start(self):
        for turn in range(2):
            for way in range(2):
                self.onward(way, None, 1 + way, way if turn == 0 else 1 - way).start()
        self.to_mate(0).start()
        if self.keep_sem is None:
            self.found[0, 0] = self.own[...]
        else:
            self.keep().start()

    def keep(self):
        return pltpu.make_async_copy(self.own, self.found.at[0, 0], self.keep_sem)

    def hop(self, h, turn, last):
        for way in range(2):
            slot = 2 * h - 1 + way
            part = way if turn == 0 else 1 - way
            self.onward(way, slot, slot, part).wait_recv()
            if not last:
                self.onward(way, slot, slot + 2, part).start()
            elif turn == 0:
                self.onward(way, slot, self.far, part).start()
            if turn == 1:
                self.to_mate(slot).start()

    def last(self):
        for way in range(2):
            self.onward(way, self.far, self.far, way).wait_recv()
        self.to_mate(self.far).start()

    def drain(self):
        for slot in range(self.far + 1):
            self.to_mate(slot).wait_send()
        for slot in range(1, self.far + 1):
            for part in range(2):
                self.onward(0, self.far, slot, part).wait_send()
        if self.keep_sem is not None:
            self.keep().wait()


class RingTurn:
    def __init__(self, count, source, target, transit, sems, after, before):
        self.count, self.half = count, count // 2
        self.source, self.target, self.transit, self.sems = source, target, transit, sems
        self.after, self.before = after, before
        self.cut = source.shape[1] // 2

    @staticmethod
    def scratch(count, rows, columns):
        half = count // 2
        dma = pltpu.SemaphoreType.DMA
        return [
            pltpu.VMEM((2, half * (half - 1) // 2, rows, columns), low),
            dma((2, half * (half + 1) // 2)),
            dma((2, half * (half + 1) // 2)),
        ]

    def copy(self, way, hop, away):
        sign = 1 - 2 * way
        number = sum(range(hop)) if hop == 0 else sum(self.half - j + 1 for j in range(1, hop)) + away - hop
        if hop == 1:
            source = self.source.at[ring_index(self.count, sign * away)]
        else:
            source = self.transit.at[way, sum(self.half - j for j in range(1, hop - 1)) + away - hop]
        if away == hop:
            target = self.target.at[ring_index(self.count, sign * (1 - hop))]
        else:
            target = self.transit.at[way, sum(self.half - j for j in range(1, hop)) + away - hop - 1]
        if away == self.half:
            rows = pl.ds(way * self.cut, self.cut)
            source, target = source.at[rows], target.at[rows]
        sems = (self.sems[0].at[way, number], self.sems[1].at[way, number])
        return send(source, target, sems, (self.after, self.before)[way])

    def start(self):
        for away in range(self.half, 0, -1):
            for way in range(2):
                self.copy(way, 1, away).start()

    def hop(self, hop):
        for away in range(self.half, hop - 1, -1):
            for way in range(2):
                self.copy(way, hop, away).wait_recv()
                if away > hop:
                    self.copy(way, hop + 1, away).start()

    def drain(self):
        for hop in range(1, self.half + 1):
            for away in range(hop, self.half + 1):
                for way in range(2):
                    self.copy(way, hop, away).wait_send()


class RingScatter:
    def __init__(self, count, items, sems, after, before):
        self.count, self.half = count, count // 2
        self.items, self.sems = items, sems
        self.after, self.before = after, before

    @staticmethod
    def scratch(count, shapes):
        half = count // 2
        dma = pltpu.SemaphoreType.DMA
        arrived = [pltpu.VMEM((2, half) + shape, kind) for shape, kind in shapes]
        leaving = [pltpu.VMEM((2, 2) + shape, kind) for shape, kind in shapes]
        return arrived + leaving + [dma((len(shapes), 2, half)), dma((len(shapes), 2, half))]

    def columns(self, item, way):
        _, arrived, _, ways = self.items[item]
        wide = arrived.shape[-1]
        return pl.ds(way * (wide // 2), wide // 2) if len(ways) == 2 else pl.ds(0, wide)

    def copy(self, item, way, step):
        _, arrived, leaving, _ = self.items[item]
        source, target = leaving.at[way, step % 2], arrived.at[way, step]
        if step == 0:
            columns = self.columns(item, way)
            source, target = source.at[:, columns], target.at[:, columns]
        sems = (self.sems[0].at[item, way, step], self.sems[1].at[item, way, step])
        return send(source, target, sems, (self.after, self.before)[way])

    def begin(self, met=None):
        index = ring_index(self.count, self.half)
        for item, (value, _, leaving, ways) in enumerate(self.items):
            far = value(index).astype(leaving.dtype)
            for way in ways:
                leaving[way, 0] = far
        if met is not None:
            met()
        for item, (_, _, _, ways) in enumerate(self.items):
            for way in ways:
                self.copy(item, way, 0).start()

    def onward(self, step):
        for item, (value, arrived, leaving, ways) in enumerate(self.items):
            for way in range(2):
                offset = self.half - step
                mine = value(ring_index(self.count, offset if way == 0 else -offset))
                if step > 1:
                    self.copy(item, way, step - 1).wait_recv()
                    mine = mine + arrived[way, step - 1].astype(full)
                if step > 2 or (step == 2 and way in ways):
                    self.copy(item, way, step - 2).wait_send()
                leaving[way, step % 2] = mine.astype(leaving.dtype)
                if step == 1 and way in ways:
                    self.copy(item, way, 0).wait_recv()
                    columns = self.columns(item, way)
                    leaving[way, 1, :, columns] = (
                        leaving[way, 1, :, columns].astype(full) + arrived[way, 0, :, columns].astype(full)
                    ).astype(leaving.dtype)
                self.copy(item, way, step).start()

    def finish(self, item):
        value, arrived, _, _ = self.items[item]
        total = value(lax.axis_index("seq"))
        for way in range(2):
            self.copy(item, way, self.half - 1).wait_recv()
            total = total + arrived[way, self.half - 1].astype(full)
        return total

    def drain(self):
        for item, (_, _, _, ways) in enumerate(self.items):
            for way in range(2):
                for step in range(self.half - 2, self.half):
                    if step > 0 or way in ways:
                        self.copy(item, way, step).wait_send()


def feed_kernel(
    count, width, own, w_both_far, w_down_far, cotangent, total, feed_sum, down_own, down_others, hidden_far,
    w_both, w_down, hidden, feed, d_both, cot_rows, down_total, feed_others, feed_in, late_sem, cot_sem, cross_out,
    cross_in, *rest
):
    gather_sems, rest = rest[:4], rest[4:]
    ring_refs, ring_sems = rest[:5], rest[5:]
    half, chips = count // 2, width // CORES
    far = count - 1
    block, depth = own.shape
    units = w_down.shape[0]
    slice_f = units // chips
    tokens = count * 2 * block
    after, before = ring_sides(count)
    mate = core_mate()
    back, ahead = chip_mates(width), chip_mates(width, True)
    met = greet(after, before, mate, *back)
    gather = RingGather(count, own, feed, gather_sems, after, before, mate)
    ring = RingSum(count, ring_refs, ring_sems, after, before, mate)
    late = [
        pltpu.make_async_copy(w_both_far, w_both, late_sem.at[0]),
        pltpu.make_async_copy(w_down_far, w_down, late_sem.at[1]),
    ]
    save_hidden = pltpu.make_async_copy(hidden, hidden_far, late_sem.at[2])

    def cross(k):
        sems = (cross_out.at[k], cross_in.at[k])
        return send(feed_others.at[k - 1], feed_in.at[k - 1], sems, ahead[k - 1])

    def fetch(slot):
        return pltpu.make_async_copy(cotangent.at[slot], cot_rows.at[slot % 2], cot_sem.at[slot % 2])

    def fetched(slot):
        fetch(slot).wait()

        @pl.when(slot < far)
        def _():
            fetch(slot + 1).start()

        return cot_rows[slot % 2].reshape(2 * block, depth)

    def work(slot):
        back_all = lax.dot_general(fetched(slot), w_down[...], (NT, ((), ())), preferred_element_type=full)
        gather.to_mate(slot).wait_recv()
        rows = feed[slot].reshape(2 * block, depth)
        before_act = jnp.dot(rows, w_both[...], preferred_element_type=full)
        forth, back_parts = [], []
        for k in range(chips):
            start = 2 * k * slice_f
            gate, up = before_act[:, start : start + slice_f], before_act[:, start + slice_f : start + 2 * slice_f]
            active, slope = gelu_and_slope(gate)
            back = back_all[:, k * slice_f : (k + 1) * slice_f]
            forth.append(active * up)
            back_parts += [back * up * slope, back * active]
        hidden[slot] = jnp.concatenate(forth, axis=1).astype(low).reshape(2, block, units)
        d_rows = jnp.concatenate(back_parts, axis=1).astype(low)
        for k in range(chips):
            d_both[k, slot] = d_rows[:, 2 * k * slice_f : 2 * (k + 1) * slice_f].reshape(2, block, 2 * slice_f)
        part = lax.dot_general(d_rows, w_both[...], (NT, ((), ())), preferred_element_type=full)
        ring.offer(slot, part, slot >= ring.held)

    for copy in late:
        copy.start()
    fetch(0).start()
    met()
    gather.start()
    gather.hop(1, 0, half == 2)
    for copy in late:
        copy.wait()
    gather.hop(1, 1, half == 2)
    work(0)

    def advance(h, last):
        gather.hop(h, 0, last)
        work(2 * h - 3)
        gather.hop(h, 1, last)
        work(2 * h - 2)

    @pl.loop(2, half - 1)
    def _(h):
        advance(h, False)

    if half > 2:
        advance(half - 1, True)
    pl.loop(far - 2, far - 1)(work)
    gather.last()
    pl.loop(far - 1, far + 1)(work)
    save_hidden.start()

    pieces = 4
    wide = depth // pieces

    def grads(first, last):
        @pl.loop(first, last)
        def _(at):
            columns = pl.ds(pl.multiple_of((at % pieces) * wide, wide), wide)
            k = chips - 1 - at // pieces
            part = lax.dot_general(
                feed[:, :, :, columns].reshape(tokens, wide),
                d_both[k].reshape(tokens, 2 * slice_f),
                (TN, ((), ())),
                preferred_element_type=full,
            ).astype(low)

            @pl.when(k == 0)
            def _():
                feed_sum[columns] = part

            @pl.when(k > 0)
            def _():
                feed_others[jnp.maximum(k - 1, 0), columns] = part

    def down(slot):
        rows = fetched(slot)
        part = lax.dot_general(
            hidden[slot].reshape(2 * block, units), rows, (TN, ((), ())), preferred_element_type=full
        )

        @pl.when(slot == 0)
        def _():
            down_total[...] = part

        @pl.when(slot > 0)
        def _():
            down_total[...] += part

    fetch(0).start()
    ring.step(1, 0)
    ring.begin()
    grads(0, (chips - 1) * pieces)
    for k in range(1, chips):
        cross(k).start()
    ring.step(1, 1)
    steps = [(step, turn) for step in range(2, half) for turn in range(2)]
    ring_step = iter(steps)

    def next_step():
        for step, turn in [next(ring_step, (0, 0))]:
            if step > 0:
                ring.step(step, turn)

    next_step()
    grads((chips - 1) * pieces, chips * pieces)
    next_step()
    pl.loop(0, count // 2)(down)
    for _ in range(len(steps)):
        next_step()
    pl.loop(count // 2, count)(down)
    down_own[...] = down_total[:slice_f].astype(low)
    for k in range(1, chips):
        down_others[k - 1] = down_total[k * slice_f : (k + 1) * slice_f].astype(low)
    total[...] = ring.finish()
    for k in range(1, chips):
        cross(k).wait_recv()
    for at in range(pieces):
        rows = slice(at * wide, (at + 1) * wide)
        part = feed_sum[rows].astype(full)
        for k in range(1, chips):
            part = part + feed_in[k - 1, rows].astype(full)
        feed_sum[rows] = part.astype(low)
    save_hidden.wait()
    gather.drain()
    ring.drain()
    for k in range(1, chips):
        cross(k).wait_send()


def feed_forward(own, w_both, w_down, cotangent):
    count, width = lax.axis_size("seq"), lax.axis_size("dp")
    chips = width // CORES
    block, depth = own.shape
    units = w_down.shape[0]
    slice_f = units // chips
    whole = pl.BlockSpec(memory_space=pltpu.VMEM)
    dma = pltpu.SemaphoreType.DMA
    shapes = [
        ((block, depth), full), ((depth, 2 * slice_f), low), ((slice_f, depth), low),
        ((chips - 1, slice_f, depth), low), ((count, 2, block, units), low),
    ]
    far = pl.BlockSpec(memory_space=pl.ANY)
    return pl.pallas_call(
        partial(feed_kernel, count, width),
        in_specs=[whole, far, far, far],
        out_specs=[whole] * 4 + [far],
        out_shape=[jax.ShapeDtypeStruct(*shape) for shape in shapes],
        scratch_shapes=[
            pltpu.VMEM(w_both.shape, low),
            pltpu.VMEM(w_down.shape, low),
            pltpu.VMEM((count, 2, block, units), low),
            pltpu.VMEM((count, 2, block, depth), low),
            pltpu.VMEM((chips, count, 2, block, 2 * slice_f), low),
            pltpu.VMEM((2, 2, block, depth), low),
            pltpu.VMEM((units, depth), full),
            pltpu.VMEM((chips - 1, depth, 2 * slice_f), low),
            pltpu.VMEM((chips - 1, depth, 2 * slice_f), low),
            dma((3,)), dma((2,)), dma((chips,)), dma((chips,)),
            *RingGather.scratch(count),
            *RingSum.scratch(count, block, depth),
        ],
        compiler_params=pltpu.CompilerParams(collective_id=1, has_side_effects=True, vmem_limit_bytes=63 << 20),
        cost_estimate=pl.CostEstimate(
            flops=2 * 2 * count * block * depth * units * 9, bytes_accessed=40 << 20, transcendentals=0
        ),
    )(own, w_both, w_down, cotangent)


def seq_peer(count, step):
    place = lax.rem(lax.axis_index("seq") + (step + count), count)
    return {"seq": place}, place


def keep_column(marks, row):
    mark = jnp.broadcast_to(marks[row, :1], marks.shape[1:])
    padding = jnp.where(mark > 1.5, 1.0, 0.0)
    keep = 1.0 - (mark - 2.0 * padding)
    return jnp.transpose(keep)[:, :1], jnp.transpose(1.0 - padding)[:, :1]


def gate_terms(pre_rate, pre_inlet, soft):
    rate, inlet = jax.nn.sigmoid(pre_rate), jax.nn.sigmoid(pre_inlet)
    twice = -16.0 * rate * soft
    decay = jnp.exp(0.5 * twice)
    near = -twice * (
        1.0 + twice * (1 / 2 + twice * (1 / 6 + twice * (1 / 24 + twice * (1 / 120 + twice * (1 / 720)))))
    )
    rest = jnp.where(twice > -0.25, near, 1.0 - decay * decay)
    return rate, inlet, decay, rest, jnp.sqrt(rest)


def scan_rows(rate, value, backward):
    length, channels = rate.shape
    groups = length // 8
    rate = rate.reshape(groups, 8, channels)
    value = value.reshape(groups, 8, channels)
    place = lax.broadcasted_iota(jnp.int32, rate.shape, 1)
    for step in (1, 2, 4):
        keep = place < 8 - step if backward else place >= step
        move = 8 - step if backward else step
        earlier_rate = jnp.where(keep, pltpu.roll(rate, move, 1), 1.0)
        earlier_value = jnp.where(keep, pltpu.roll(value, move, 1), 0.0)
        value = value + rate * earlier_value
        rate = rate * earlier_rate
    product_in = jnp.ones((1, channels), full)
    state_in = jnp.zeros((1, channels), full)
    end = 0 if backward else 7
    products, states = [None] * groups, [None] * groups
    for group in reversed(range(groups)) if backward else range(groups):
        states[group] = value[group] + rate[group] * state_in
        products[group] = rate[group] * product_in
        product_in, state_in = products[group][end : end + 1], states[group][end : end + 1]
    return jnp.concatenate(products, axis=0), jnp.concatenate(states, axis=0)


def fold_states(count, arrived, backward):
    mine = lax.axis_index("seq")
    total = jnp.zeros(arrived.shape[2:], full)
    scale = jnp.ones(arrived.shape[2:], full)
    for step in range(1, count):
        there = (mine + step < count) if backward else (mine >= step)
        total = total + jnp.where(there, scale * arrived[step, 1], 0.0)
        scale = scale * arrived[step, 0]
    return total


def stack_rows(ref):
    pieces, rows, columns = ref.shape
    if rows % 16 == 0:
        return ref[...].reshape(pieces * rows, columns)
    return jnp.concatenate([ref[piece].astype(full) for piece in range(pieces)], axis=0).astype(ref.dtype)


def tail_factor(column, taps):
    length = column.shape[0]
    place = lax.broadcasted_iota(jnp.int32, (8, 1), 0)
    factor, run = jnp.where(place == 7, 1.0, 0.0), jnp.ones((1, 1), full)
    for back in range(1, taps - 1):
        run = run * column[length - back : length - back + 1]
        factor = jnp.where(place == 7 - back, run, factor)
    return factor


def front_kernel(
    count, width, own, cot_raw, resets, real_mask, gain_mix, gain_mlp, conv_kernel, decay_param, gate_rate, gate_input,
    w_gate, w_x, w_mix, w_feed_gate_far, w_feed_up_far, w_down,
    marks_all, w_both, gains, chan, cotangent, middle, feed_own, halo, ends, cot_all, down_all,
    gate_far, x_far, normed_far, pre_gate_far, branch_far, w_mix_far, conv_far, pre_rate_far, pre_inlet_far, rate_far,
    inlet_far, states_far, mixed_far,
    gate_all, x_all, normed, pre_gate, branch, w_mix_all, conv_low, pre_rate, pre_inlet, rate_mat, inlet_mat, states,
    mixed, w_feed_gate, w_feed_up, save_sem, own_marks, small, small_all, own_gates, gates_all, mix_all, rows_all, x_total, scale, turned, arrived,
    keep, product, state, ext, halo_out, halo_in, state_out, state_all, core_out, core_in, chip_out, chip_in,
    ring_out, ring_in, last_out, last_in, rows_out, rows_in, mate_out, mate_in, cross_out, cross_in, down_out, down_in,
    halo_sem, state_out_sem, state_in_sem, core_out_sem, core_in_sem, chip_out_sem, chip_in_sem, cot_sem, *rest
):
    gather_sems, turn_refs = rest[:4], rest[4:]
    half = count // 2
    chips = width // CORES
    block, depth = own.shape
    shard, channels = w_gate.shape
    own_channels, size = gate_rate.shape
    taps = conv_kernel.shape[0]
    slice_f = w_down.shape[0]
    mine = lax.axis_index("seq")
    after, before = ring_sides(count)
    mate = core_mate()
    back, ahead = chip_mates(width), chip_mates(width, True)
    peers = [None] + [seq_peer(count, step)[0] for step in range(1, count)]
    met = greet(mate, *back, *peers[1:])
    loads = [
        pltpu.make_async_copy(w_feed_gate_far, w_feed_gate, save_sem.at[14]),
        pltpu.make_async_copy(w_feed_up_far, w_feed_up, save_sem.at[15]),
    ]
    for copy in loads:
        copy.start()
    gather = RingGather(count, cotangent, cot_all, gather_sems, after, before, mate, cot_sem.at[0])
    turn = RingTurn(count, turned, arrived.at[0], turn_refs[0], turn_refs[1:], after, before)
    saves = [
        pltpu.make_async_copy(source, target, save_sem.at[at])
        for at, (source, target) in enumerate(
            (
                (gate_all, gate_far), (x_all, x_far), (normed, normed_far), (pre_gate, pre_gate_far),
                (branch, branch_far), (w_mix_all, w_mix_far), (conv_low, conv_far), (pre_rate, pre_rate_far),
                (pre_inlet, pre_inlet_far), (rate_mat, rate_far), (inlet_mat, inlet_far), (states, states_far),
                (mixed, mixed_far), (w_down, down_all.at[0]),
            )
        )
    ]
    moved = ((w_gate, gate_all), (small, small_all), (w_x, x_all), (own_gates, gates_all), (w_mix, mix_all))
    shared = ((0,), (0,), (1,), (1,), (0, 1))

    def rows_copy(what, k):
        source, target = ((own, rows_all), (own_marks, marks_all))[what]
        return send(source, target.at[k], (rows_out.at[what, k], rows_in.at[what, k]), back[k - 1])

    def mate_copy(what, k):
        source, target = ((own, rows_all), (own_marks, marks_all))[what]
        source = source if k == 0 else target.at[k]
        return send(source, target.at[chips + k], (mate_out.at[what, k], mate_in.at[what, k]), mate)

    def ring_copy(way, hop, item):
        source, target = moved[item]
        index = mine if hop == 1 else ring_index(count, (1 - hop) if way == 0 else (hop - 1))
        return send(
            source if hop == 1 else target.at[index],
            target.at[index],
            (ring_out.at[way, hop, item], ring_in.at[way, hop, item]),
            after if way == 0 else before,
        )

    def last_copy(way, item):
        index = ring_index(count, (1 - half) if way == 0 else (half - 1))
        ref = moved[item][1].at[index]
        if len(shared[item]) == 2:
            ref = ref.at[:, pl.ds(way * (depth // 2), depth // 2)]
        return send(ref, ref, (last_out.at[way, item], last_in.at[way, item]), after if way == 0 else before)

    def cross(slot, k):
        offset = half if slot == count - 1 else (slot + 1) // 2 * (1 - 2 * (slot % 2))
        origin = ring_index(count, offset)
        sems = (cross_out.at[k, slot], cross_in.at[k, slot])
        return send(arrived.at[0, origin], arrived.at[k, origin], sems, back[k - 1])

    def cross_down(k):
        return send(w_down, down_all.at[k], (down_out.at[k], down_in.at[k]), back[k - 1])

    def halo_copy():
        return send(halo_out, halo_in, (halo_sem.at[0], halo_sem.at[1]), peers[1])

    def state_copy(step):
        return send(state_out, state_all.at[step], (state_out_sem.at[step], state_in_sem.at[step]), peers[step])

    def core_copy(k):
        return send(core_out.at[k], core_in.at[k], (core_out_sem.at[k], core_in_sem.at[k]), mate)

    def chip_copy(k):
        return send(chip_out.at[k], chip_in.at[k], (chip_out_sem.at[k], chip_in_sem.at[k]), ahead[k - 1])

    def send_item(item):
        ring_copy(0, 1, item).start()
        ring_copy(1, 1, item).start()
        moved[item][1][mine] = moved[item][0][...]

    real = real_mask[...].astype(full)
    own_marks[...] = jnp.broadcast_to(resets[...].astype(full) + 2.0 * (1.0 - real), own_marks.shape)
    tap_rows = conv_kernel[...].astype(full)
    padding = jnp.zeros((1, shard - own_channels), full)
    pieces = [jnp.concatenate([tap_rows[tap : tap + 1], padding], axis=1) for tap in range(taps)]
    pieces.append(jnp.concatenate([decay_param[...].astype(full), padding], axis=1))
    pieces += [gain_mix[...].astype(full).reshape(1, shard), gain_mlp[...].astype(full).reshape(1, shard)]
    place = lax.broadcasted_iota(jnp.int32, (16, shard), 0)
    total = jnp.zeros((16, shard), full)
    for at, piece in enumerate(pieces):
        total = jnp.where(place == at, piece, total)
    small[...] = total.astype(low)
    own_gates[...] = jnp.concatenate([gate_rate[...].astype(full), gate_input[...].astype(full)], axis=1).astype(low)
    met()
    send_item(0)
    mate_copy(0, 0).start()
    mate_copy(1, 0).start()
    for k in range(1, chips):
        rows_copy(0, k).start()
        rows_copy(1, k).start()
    for item in range(1, len(moved)):
        send_item(item)
    rows_all[0] = own[...]
    marks_all[0] = own_marks[...]
    _, real = keep_column(marks_all, 0)
    cotangent[...] = (cot_raw[...].astype(full) * real).astype(low)
    saves[13].start()
    for k in range(1, chips):
        cross_down(k).start()
    for k in range(1, chips):
        for what in range(2):
            rows_copy(what, k).wait_recv()
            mate_copy(what, k).start()
    for k in range(chips):
        for what in range(2):
            mate_copy(what, k).wait_recv()
    for row in range(width):
        values = rows_all[row].astype(full)
        scale[row] = lax.rsqrt(jnp.mean(values * values, axis=-1, keepdims=True) + epsilon)

    def work(index, first):
        columns = pl.ds(pl.multiple_of(index * shard, shard), shard)
        gain = small_all[index].astype(full)[taps + 1 : taps + 2]
        values = rows_all[:, :, columns].astype(full)
        part = (values * scale[...] * gain).astype(low).reshape(width * block, shard)
        normed[:, columns] = part
        for weight, target in ((gate_all, pre_gate), (x_all, x_total)):
            term = jnp.dot(part, weight[index], preferred_element_type=full).reshape(width, block, channels)
            if first:
                target[...] = term
            else:
                target[...] += term

    work(mine, True)
    for copy in loads:
        copy.wait()
    for at in range(count):
        columns = slice(at * slice_f, (at + 1) * slice_f)
        turned[at] = jnp.concatenate(
            [w_feed_gate[:, columns].astype(full), w_feed_up[:, columns].astype(full)], axis=1
        ).astype(low)
    arrived[0, mine] = turned[mine]
    for k in range(1, chips):
        cross(0, k).start()
    for hop in range(1, half):
        for item in range(len(moved)):
            for way in range(2):
                ring_copy(way, hop, item).wait_recv()
                if hop < half - 1:
                    ring_copy(way, hop + 1, item).start()
                elif way in shared[item]:
                    last_copy(way, item).start()
            if item == 2:
                for way in range(2):
                    work(ring_index(count, -hop if way == 0 else hop), False)
    for item in range(3):
        last_copy(shared[item][0], item).wait_recv()
    work(ring_index(count, half), False)
    branch[...] = x_total[...].astype(low)

    for row in range(width):
        column, _ = keep_column(marks_all, row)
        keep[row, :8] = jnp.ones((8, 1), full)
        keep[row, 8:] = column
        halo_out[row] = branch[row, block - 16 :].astype(full)[8:] * tail_factor(column, taps)
    halo_copy().start()
    turn.start()
    gather.start()
    for item in range(3, len(moved)):
        for way in shared[item]:
            last_copy(way, item).wait_recv()
    entries = jnp.concatenate([small_all[at].astype(full)[:8, :own_channels] for at in range(count)], axis=1)
    place = lax.broadcasted_iota(jnp.int32, entries.shape, 0)
    decay_row = entries[taps : taps + 1]
    entries = jnp.where(place == taps, jax.nn.softplus(decay_row), entries)
    chan[...] = jnp.where(place == taps + 1, jax.nn.sigmoid(decay_row), entries)
    entries = jnp.concatenate([small_all[at].astype(full)[:8] for at in range(count)], axis=1)
    gains[...] = jnp.concatenate([entries[taps + 1 : taps + 3], jnp.zeros((6, depth), full)], axis=0)
    w_mix_all[...] = stack_rows(mix_all)
    for copy in saves[:6]:
        copy.start()
    entries = stack_rows(gates_all)
    for at in range(channels // size):
        rows = slice(at * size, (at + 1) * size)
        for target, first in ((rate_mat, 0), (inlet_mat, size)):
            parts = [entries[rows].astype(full)[:, first : first + size]]
            if at > 0:
                parts.insert(0, jnp.zeros((size, at * size), full))
            if at + 1 < channels // size:
                parts.append(jnp.zeros((size, channels - (at + 1) * size), full))
            target[rows] = jnp.concatenate(parts, axis=1).astype(low)

    halo_copy().wait_recv()
    soft = chan[taps : taps + 1]
    state_out[...] = jnp.zeros_like(state_out)

    @pl.loop(0, width)
    def _(row):
        from_before = jnp.where(mine > 0, halo_in[row], 0.0)
        halo[row] = from_before
        ext[:8] = from_before
        ext[8:] = branch[row].astype(full)
        valid = jnp.ones((block, 1), full)
        total = jnp.zeros((block, channels), full)
        for tap in range(taps):
            total = total + chan[tap : tap + 1] * valid * ext[8 - tap : 8 - tap + block]
            valid = valid * keep[row, 8 - tap : 8 - tap + block]
        conv = total.astype(low)
        conv_low[row] = conv
        rate_in = lax.dot_general(conv, rate_mat[...], (NT, ((), ())), preferred_element_type=full)
        inlet_in = lax.dot_general(conv, inlet_mat[...], (NT, ((), ())), preferred_element_type=full)
        pre_rate[row] = rate_in
        pre_inlet[row] = inlet_in
        _, inlet, decay, _, root = gate_terms(rate_in, inlet_in, soft)
        kept = keep[row, 8:]
        inflow = conv.astype(full) * inlet * ((1.0 - kept) + kept * root)
        row_product, row_state = scan_rows(decay * kept, inflow, False)
        product[row] = row_product
        state[row] = row_state
        state_out[0, pl.ds(row, 1)] = row_product[block - 1 :]
        state_out[1, pl.ds(row, 1)] = row_state[block - 1 :]

    for copy in saves[6:11]:
        copy.start()

    def background(h):
        turn.hop(h)
        for slot in (2 * h - 1, 2 * h) if h < half else (count - 1,):
            for k in range(1, chips):
                cross(slot, k).start()
        if h < half:
            gather.hop(h, 0, h == half - 1)
            gather.hop(h, 1, h == half - 1)
        else:
            gather.last()

    for step in range(1, count):
        state_copy(step).start()
    background(1)
    for step in range(1, count):
        state_copy(step).wait_recv()
    ends[0] = fold_states(count, state_all, False)
    ends[1] = state_out[0]

    def close(row):
        row_states = state[row] + product[row] * ends[0, pl.ds(row, 1)]
        states[row] = row_states
        active, _ = gelu_and_slope(pre_gate[row])
        row_mixed = (row_states * active).astype(low)
        mixed[row] = row_mixed
        return jnp.dot(row_mixed, w_mix_all[...], preferred_element_type=full)

    @pl.loop(0, chips)
    def _(at):
        k = chips - 1 - at
        core_out[k] = close(chips + k).astype(low)
        core_copy(k).start()

    @pl.loop(0, chips - 1)
    def _(at):
        k = chips - 1 - at
        part = close(k)
        core_copy(k).wait_recv()
        chip_out[k] = (part + core_in[k].astype(full)).astype(low)

    for k in range(chips - 1, 0, -1):
        chip_copy(k).start()
    part = close(0)
    background(2)
    core_copy(0).wait_recv()
    total = part + core_in[0].astype(full) + own[...].astype(full)
    for k in range(1, chips):
        chip_copy(k).wait_recv()
        total = total + chip_in[k].astype(full)
    for copy in saves[11:13]:
        copy.start()
    middle[...] = total
    scaled = total * lax.rsqrt(jnp.mean(total * total, axis=-1, keepdims=True) + epsilon)
    feed_own[...] = (scaled * gains[1:2]).astype(low)
    for h in range(3, half + 1):
        background(h)
    for k in range(chips):
        if k > 0:
            cross_down(k).wait_recv()
            for slot in range(count):
                cross(slot, k).wait_recv()
        w_both[:, 2 * k * slice_f : 2 * (k + 1) * slice_f] = arrived[k].reshape(depth, 2 * slice_f)
    for slot in range(count):
        gather.to_mate(slot).wait_recv()

    for copy in saves:
        copy.wait()
    for item in range(len(moved)):
        for way in range(2):
            for hop in range(1, half):
                ring_copy(way, hop, item).wait_send()
            if way in shared[item]:
                last_copy(way, item).wait_send()
    for what in range(2):
        for k in range(chips):
            mate_copy(what, k).wait_send()
        for k in range(1, chips):
            rows_copy(what, k).wait_send()
    for k in range(1, chips):
        cross_down(k).wait_send()
        chip_copy(k).wait_send()
        for slot in range(count):
            cross(slot, k).wait_send()
    for k in range(chips):
        core_copy(k).wait_send()
    for step in range(1, count):
        state_copy(step).wait_send()
    halo_copy().wait_send()
    turn.drain()
    gather.drain()


def forward(own, cotangent, resets, real_mask, *weights):
    conv_kernel, gate_rate, w_gate, w_mix, w_down = weights[2], weights[4], weights[6], weights[8], weights[11]
    count, width = lax.axis_size("seq"), lax.axis_size("dp")
    half, chips = count // 2, width // CORES
    block, depth = own.shape
    shard, part = w_gate.shape
    own_channels, size = gate_rate.shape
    channels = count * own_channels
    slice_f = w_down.shape[0]
    whole = pl.BlockSpec(memory_space=pltpu.VMEM)
    dma = pltpu.SemaphoreType.DMA
    rows = (width, block, channels)
    shapes = [
        ((width, 8, block), full), ((depth, 2 * chips * slice_f), low), ((8, depth), full), ((8, channels), full),
        ((block, depth), low), ((block, depth), full), ((block, depth), low), ((width, 8, channels), full),
        ((2, 8, channels), full), ((count, 2, block, depth), low), ((chips,) + w_down.shape, low),
    ]
    saved = [
        ((count, shard, part), low), ((count, shard, part), low), ((width * block, depth), low), (rows, full),
        (rows, low), ((channels, depth), low), (rows, low), (rows, full), (rows, full), ((channels, channels), low),
        ((channels, channels), low), (rows, full), (rows, low),
    ]
    return pl.pallas_call(
        partial(front_kernel, count, width),
        in_specs=[whole] * (4 + len(weights) - 3) + [pl.BlockSpec(memory_space=pl.ANY)] * 3,
        out_specs=[whole] * (len(shapes) - 2) + [pl.BlockSpec(memory_space=pl.ANY)] * (len(saved) + 2),
        out_shape=[jax.ShapeDtypeStruct(*shape) for shape in shapes + saved],
        scratch_shapes=[
            *[pltpu.VMEM(*shape) for shape in saved],
            pltpu.VMEM(weights[9].shape, low),
            pltpu.VMEM(weights[10].shape, low),
            dma((len(saved) + 3,)),
            pltpu.VMEM((8, block), full),
            pltpu.VMEM((16, shard), low),
            pltpu.VMEM((count, 16, shard), low),
            pltpu.VMEM((own_channels, 2 * size), low),
            pltpu.VMEM((count, own_channels, 2 * size), low),
            pltpu.VMEM((count,) + w_mix.shape, low),
            pltpu.VMEM((width, block, depth), low),
            pltpu.VMEM(rows, full),
            pltpu.VMEM((width, block, 1), full),
            pltpu.VMEM((count, shard, 2 * slice_f), low),
            pltpu.VMEM((chips, count, shard, 2 * slice_f), low),
            pltpu.VMEM((width, 8 + block, 1), full),
            pltpu.VMEM(rows, full),
            pltpu.VMEM(rows, full),
            pltpu.VMEM((8 + block, channels), full),
            pltpu.VMEM((width, 8, channels), full),
            pltpu.VMEM((width, 8, channels), full),
            pltpu.VMEM((2, 8, channels), full),
            pltpu.VMEM((count, 2, 8, channels), full),
            *[pltpu.VMEM((chips, block, depth), low)] * 4,
            dma((2, half, 5)), dma((2, half, 5)), dma((2, 5)), dma((2, 5)),
            dma((2, chips)), dma((2, chips)), dma((2, chips)), dma((2, chips)),
            dma((chips, count)), dma((chips, count)), dma((chips,)), dma((chips,)),
            dma((2,)), dma((count,)), dma((count,)), dma((chips,)), dma((chips,)), dma((chips,)), dma((chips,)), dma((1,)),
            *RingGather.scratch(count),
            *RingTurn.scratch(count, shard, 2 * slice_f),
        ],
        compiler_params=pltpu.CompilerParams(collective_id=2, has_side_effects=True, vmem_limit_bytes=63 << 20),
        cost_estimate=pl.CostEstimate(
            flops=6 * width * block * depth * channels, bytes_accessed=60 << 20, transcendentals=0
        ),
    )(own, cotangent, resets, real_mask, *weights)


def back_kernel(
    count, width, taps, gains, marks, chan, halo, ends, d_feed_far, middle_far, cotangent_far, w_down_far, w_mix_far,
    mixed_far, rate_far, inlet_far, conv_far, down_far,
    pre_gate, pre_rate, pre_inlet, states, branch, hidden, down_others, feed_sum,
    output, d_middle, d_pre_gate, d_branch, grad_mix, gate_grads, small_grads, gain_share, down_sum, feed_gate, feed_up,
    d_feed, middle, cotangent, w_down, w_mix, mixed, rate_mat, inlet_mat, conv_low, down_own,
    gate_rows, rate_rows, inlet_rows, state_rows, branch_rows,
    hidden_rows, keep, mix_rows, mix_grads, later, local, shift, ext, d_rate, d_inlet, sums, halo_out, halo_in,
    state_out, state_all, down_in, feed_parts, late_sem, row_sem, hidden_sem, *rest
):
    ring_refs, rest = rest[:5], rest[5:]
    ring_sems, rest = rest[:6], rest[6:]
    (arrived, leaving), mix_sems, rest = rest[:2], rest[2:4], rest[4:]
    halo_sem, state_out_sem, state_in_sem, chip_out, chip_in, mate_out, mate_in, cross_out, cross_in = rest[:9]
    turn_refs = rest[9:]
    half = count // 2
    chips = width // CORES
    far = count - 1
    block, depth = middle.shape
    channels = chan.shape[1]
    own_channels = channels // count
    size = gate_grads.shape[-1] // 2
    mine = lax.axis_index("seq")
    after, before = ring_sides(count)
    mate = core_mate()
    back, ahead = chip_mates(width), chip_mates(width, True)
    peers = [None] + [seq_peer(count, -step)[0] for step in range(1, count)]
    met = greet(mate, *back, *peers[1:])
    ring = RingSum(count, ring_refs, ring_sems, after, before, mate)
    items = [(lambda index: mix_grads[index].astype(full), arrived, leaving, (0, 1))]
    scatter = RingScatter(count, items, mix_sems, after, before)
    turn = RingTurn(count, feed_sum, feed_parts, turn_refs[0], turn_refs[1:], after, before)

    def chips_copy(k):
        return send(mix_rows.at[0], mix_rows.at[k], (chip_out.at[k], chip_in.at[k]), back[k - 1])

    def mate_copy(k):
        return send(mix_rows.at[k], mix_rows.at[chips + k], (mate_out.at[k], mate_in.at[k]), mate)

    def cross(k):
        return send(down_others.at[k - 1], down_in.at[k - 1], (cross_out.at[k], cross_in.at[k]), ahead[k - 1])

    late = [
        pltpu.make_async_copy(source, target, late_sem.at[at])
        for at, (source, target) in enumerate(
            (
                (d_feed_far, d_feed), (middle_far, middle), (cotangent_far, cotangent), (w_down_far, w_down),
                (mixed_far, mixed), (w_mix_far, w_mix), (rate_far, rate_mat), (inlet_far, inlet_mat),
                (conv_far, conv_low), (down_far, down_own), (feed_sum.at[mine], feed_parts.at[mine]),
            )
        )
    ]
    streams = (
        ((pre_gate, gate_rows), (pre_rate, rate_rows), (states, state_rows)),
        ((pre_rate, rate_rows), (pre_inlet, inlet_rows), (states, state_rows), (branch, branch_rows)),
    )

    def row_copies(which, row):
        return [
            pltpu.make_async_copy(source.at[row], target.at[row % 2], row_sem.at[at, row % 2])
            for at, (source, target) in enumerate(streams[which])
        ]

    def row_start(which, row):
        for copy in row_copies(which, row):
            copy.start()

    def row_ready(which, row):
        for copy in row_copies(which, row):
            copy.wait()

        @pl.when(row + 1 < width)
        def _():
            row_start(which, row + 1)

        return row % 2

    def halo_copy():
        return send(halo_out, halo_in, (halo_sem.at[0], halo_sem.at[1]), peers[1])

    def state_copy(step):
        return send(state_out, state_all.at[step], (state_out_sem.at[step], state_in_sem.at[step]), peers[step])

    def fetch(at):
        return pltpu.make_async_copy(hidden.at[far - at], hidden_rows.at[at % 2], hidden_sem.at[at % 2])

    for copy in late[:4]:
        copy.start()
    fetch(0).start()
    for copy in late[4:]:
        copy.start()
    row_start(0, 0)
    for copy in late[:3]:
        copy.wait()

    values, arriving = middle[...], d_feed[...]
    scale = lax.rsqrt(jnp.mean(values * values, axis=-1, keepdims=True) + epsilon)
    normed = values * scale
    scaled = arriving * gains[1:2]
    gain_share[...] = jnp.sum(arriving * normed, axis=0, keepdims=True)
    total = cotangent[...].astype(full) + scale * (
        scaled - normed * jnp.mean(scaled * normed, axis=-1, keepdims=True)
    )
    d_middle[...] = total
    mix_rows[0] = total.astype(low)
    met()
    for k in range(1, chips):
        chips_copy(k).start()
    mate_copy(0).start()
    turn.start()

    def offer(at):
        slot = far - at
        fetch(at).wait()

        @pl.when(at < far)
        def _():
            fetch(at + 1).start()

        rows = hidden_rows[at % 2].reshape(2 * block, hidden.shape[-1])
        ring.offer(slot, jnp.dot(rows, w_down[...], preferred_element_type=full), at >= ring.held)

    late[3].wait()
    pl.loop(0, 3)(offer)
    ring.begin()
    ring.step(1, 0)
    pl.loop(3, count)(offer)
    for k in range(1, chips):
        chips_copy(k).wait_recv()
        mate_copy(k).start()
    for k in range(1, chips):
        cross(k).start()
    ring.step(1, 1)
    turn.hop(1)
    for copy in late[4:6]:
        copy.wait()
    for k in range(chips):
        mate_copy(k).wait_recv()
    tokens = width * block
    rows = mixed[...].reshape(tokens, channels)
    wide = depth // 4
    for at in range(4):
        part = lax.dot_general(
            rows,
            mix_rows[:, :, at * wide : (at + 1) * wide].reshape(tokens, wide),
            (TN, ((), ())),
            preferred_element_type=full,
        )
        for piece in range(count):
            mix_grads[piece, :, at * wide : (at + 1) * wide] = part[
                piece * own_channels : (piece + 1) * own_channels
            ].astype(low)
    scatter.begin()

    soft, soft_slope = chan[taps : taps + 1], chan[taps + 1 : taps + 2]
    state_out[0] = ends[1]
    state_out[1] = jnp.zeros_like(ends[1])
    sums[...] = jnp.zeros_like(sums)

    def adjoint_row(row):
        at = row_ready(0, row)
        column, real = keep_column(marks, row)
        keep[row, :8] = jnp.ones((8, 1), full)
        keep[row, 8:] = column
        sums[taps + 2 : taps + 3] += jnp.sum(real)
        d_mixed = lax.dot_general(mix_rows[row], w_mix[...], (NT, ((), ())), preferred_element_type=full)
        active, slope = gelu_and_slope(gate_rows[at])
        d_pre_gate[row] = (d_mixed * state_rows[at] * slope).astype(low)
        decay = jnp.exp(-8.0 * jax.nn.sigmoid(rate_rows[at]) * soft)
        sums[taps + 1 : taps + 2] += jnp.sum(decay * real, axis=0, keepdims=True)
        shift[:block] = decay * column
        shift[block:] = jnp.ones((8, channels), full)
        row_later, row_local = scan_rows(shift[1 : block + 1], d_mixed * active, True)
        later[row] = row_later
        local[row] = row_local
        state_out[1, pl.ds(row, 1)] = shift[:1] * row_local[:1]

    if half > 2:
        ring.step(2, 0)
    pl.loop(0, width // 2)(adjoint_row)
    if half > 2:
        ring.step(2, 1)
    pl.loop(width // 2, width)(adjoint_row)
    row_start(1, 0)
    for step in range(1, count):
        state_copy(step).start()
    scatter.onward(1)
    turn.hop(2)
    for copy in late[6:]:
        copy.wait()
    for step in range(1, count):
        state_copy(step).wait_recv()
    sums[8:16] = fold_states(count, state_all, True)

    def gate_row(row):
        at = row_ready(1, row)
        column = keep[row, 8:]
        rate, inlet, decay, _, root = gate_terms(rate_rows[at], inlet_rows[at], soft)
        conv = conv_low[row].astype(full)
        adjoint = local[row] + later[row] * sums[pl.ds(8 + row, 1)]
        shift[:8] = jnp.broadcast_to(ends[0, pl.ds(row, 1)], (8, channels))
        shift[8:] = state_rows[at]
        previous = shift[7 : 7 + block]
        mult = (1.0 - column) + column * root
        d_log = adjoint * column * (decay * previous - conv * inlet * decay * decay / root)
        rate_part = (d_log * (-8.0 * soft) * rate * (1.0 - rate)).astype(low)
        inlet_part = (adjoint * conv * mult * inlet * (1.0 - inlet)).astype(low)
        d_rate[row] = rate_part
        d_inlet[row] = inlet_part
        sums[taps : taps + 1] += jnp.sum(d_log * (-8.0 * rate), axis=0, keepdims=True) * soft_slope
        through = (
            adjoint * inlet * mult
            + jnp.dot(rate_part, rate_mat[...], preferred_element_type=full)
            + jnp.dot(inlet_part, inlet_mat[...], preferred_element_type=full)
        )
        ext[:8] = halo[row]
        ext[8:] = branch_rows[at].astype(full)
        place = lax.broadcasted_iota(jnp.int32, (8, 1), 0)
        valid = jnp.ones((block, 1), full)
        branch_part = jnp.zeros((block, channels), full)
        tail = jnp.zeros((8, channels), full)
        for tap in range(taps):
            moved = valid * through
            sums[tap : tap + 1] += jnp.sum(moved * ext[8 - tap : 8 - tap + block], axis=0, keepdims=True)
            moved = moved * chan[tap : tap + 1]
            if tap == 0:
                branch_part = moved
            else:
                shift[:block] = moved
                shift[block:] = jnp.zeros((8, channels), full)
                branch_part = branch_part + shift[tap : tap + block]
                for j in range(1, tap + 1):
                    tail = tail + jnp.where(place == 8 - j, moved[tap - j : tap - j + 1], 0.0)
            valid = valid * keep[row, 8 - tap : 8 - tap + block]
        local[row] = branch_part
        halo_out[row] = tail

    pl.loop(0, width // 2)(gate_row)
    if half > 2:
        scatter.onward(2)
    for step in range(3, half):
        ring.step(step, 0)
        ring.step(step, 1)
    if half > 2:
        turn.hop(3)
    pl.loop(width // 2, width)(gate_row)
    halo_copy().start()
    rows = conv_low[...].reshape(tokens, channels)
    both = [
        lax.dot_general(part[...].reshape(tokens, channels), rows, (TN, ((), ())), preferred_element_type=full)
        for part in (d_rate, d_inlet)
    ]
    for piece in range(count):
        first = piece * own_channels
        at = first // size * size
        gate_grads[piece] = jnp.concatenate(
            [part[first : first + own_channels, at : at + size] for part in both], axis=1
        ).astype(low)
    for step in range(3, half):
        scatter.onward(step)
        turn.hop(step + 1)
    halo_copy().wait_recv()

    @pl.loop(0, width)
    def _(row):
        column = keep[row, 8:]
        arriving = jnp.where(mine < count - 1, halo_in[row] * tail_factor(column, taps), 0.0)
        local[row, block - 8 :] += arriving
        d_branch[row] = local[row].astype(low)

    for piece in range(count):
        entries = sums[:8, piece * own_channels : (piece + 1) * own_channels]
        small_grads[piece] = jnp.concatenate([entries, jnp.zeros((8, 128 - own_channels), full)], axis=1)
    total = down_own[...].astype(full)
    for k in range(1, chips):
        cross(k).wait_recv()
        total = total + down_in[k - 1].astype(full)
    down_sum[...] = total.astype(low)
    _, real = keep_column(marks, 0)
    output[...] = ((middle[...] + ring.finish()) * real).astype(low)

    wide = feed_parts.shape[-1] // 2
    for target, columns in ((feed_gate, slice(0, wide)), (feed_up, slice(wide, 2 * wide))):
        parts = [feed_parts[at].astype(full)[:, columns] for at in range(count)]
        target[...] = jnp.concatenate(parts, axis=1).astype(low)
    grad_mix[...] = scatter.finish(0).astype(low)
    ring.drain()
    scatter.drain()
    turn.drain()
    halo_copy().wait_send()
    for step in range(1, count):
        state_copy(step).wait_send()
    for k in range(chips):
        mate_copy(k).wait_send()
    for k in range(1, chips):
        chips_copy(k).wait_send()
        cross(k).wait_send()


def mix_back(taps, size, near, late, rows, hidden, down_others, feed_sum):
    chan, middle = near[2], late[1]
    count, width = lax.axis_size("seq"), lax.axis_size("dp")
    chips = width // CORES
    block, depth = middle.shape
    channels = chan.shape[1]
    own_channels = channels // count
    whole = pl.BlockSpec(memory_space=pltpu.VMEM)
    far = pl.BlockSpec(memory_space=pl.ANY)
    dma = pltpu.SemaphoreType.DMA
    all_rows = (width, block, channels)
    shapes = [
        ((block, depth), low), ((block, depth), full), (all_rows, low), (all_rows, low),
        ((own_channels, depth), low), ((count, own_channels, 2 * size), low), ((count, 8, 128), full),
        ((1, depth), full), (late[-1].shape, low),
        *[((feed_sum.shape[1], feed_sum.shape[2] // 2 * count), low)] * 2,
    ]
    operands = (*near, *late, *rows, hidden, down_others, feed_sum)
    return pl.pallas_call(
        partial(back_kernel, count, width, taps),
        in_specs=[whole] * len(near) + [far] * (len(operands) - len(near)),
        out_specs=[whole] * len(shapes),
        out_shape=[jax.ShapeDtypeStruct(*shape) for shape in shapes],
        scratch_shapes=[
            *[pltpu.VMEM(each.shape, each.dtype) for each in late],
            *[pltpu.VMEM((2,) + each.shape[1:], each.dtype) for each in (*rows, hidden)],
            pltpu.VMEM((width, 8 + block, 1), full),
            pltpu.VMEM((width, block, depth), low),
            pltpu.VMEM((count, own_channels, depth), low),
            pltpu.VMEM(all_rows, full),
            pltpu.VMEM(all_rows, full),
            pltpu.VMEM((block + 8, channels), full),
            pltpu.VMEM((block + 8, channels), full),
            pltpu.VMEM(all_rows, low),
            pltpu.VMEM(all_rows, low),
            pltpu.VMEM((16, channels), full),
            pltpu.VMEM((width, 8, channels), full),
            pltpu.VMEM((width, 8, channels), full),
            pltpu.VMEM((2, 8, channels), full),
            pltpu.VMEM((count, 2, 8, channels), full),
            pltpu.VMEM(down_others.shape, low),
            pltpu.VMEM(feed_sum.shape, low),
            dma((len(late) + 1,)), dma((4, 2)), dma((2,)),
            *RingSum.scratch(count, block, depth),
            *RingScatter.scratch(count, [((own_channels, depth), low)]),
            dma((2,)), dma((count,)), dma((count,)), dma((chips,)), dma((chips,)), dma((chips,)), dma((chips,)),
            dma((chips,)), dma((chips,)),
            *RingTurn.scratch(count, *feed_sum.shape[1:]),
        ],
        compiler_params=pltpu.CompilerParams(collective_id=4, has_side_effects=True, vmem_limit_bytes=63 << 20),
        cost_estimate=pl.CostEstimate(
            flops=4 * width * block * channels * (depth + 2 * channels), bytes_accessed=60 << 20, transcendentals=0
        ),
    )(*operands)


def close_kernel(
    count, width, own, d_middle, gains, gain_share, gate_grads, small_grads, normed_far, d_pre_gate_far, d_branch_far,
    w_gate_far, w_x_far, d_inputs, out_gate, out_x, out_gates, out_small, out_gains,
    normed, d_pre_gate, d_branch, w_gate, w_x, late_sem, *rest
):
    travel, rest = rest[:10], rest[10:]
    core_out, core_in, chip_out, chip_in, gain_out, gain_width, gain_total, gain_seq = rest[:8]
    core_out_sem, core_in_sem, chip_out_sem, chip_in_sem, width_out, width_in, seq_out, seq_in = rest[8:16]
    half = count // 2
    chips = width // CORES
    block, depth = own.shape
    shard = out_gate.shape[0]
    share = depth // width
    my_width = lax.axis_index("dp")
    after, before = ring_sides(count)
    mate = core_mate()
    ahead = chip_mates(width, True)
    peers = [None] + [seq_peer(count, step) for step in range(1, count)]
    others = [None] + [lax.rem(my_width + step, width) for step in range(1, width)]
    met = greet(*[peer for peer, _ in peers[1:]], *[{"dp": place} for place in others[1:]])

    def product(grads):
        def at(index):
            columns = pl.ds(pl.multiple_of(index * shard, shard), shard)
            return lax.dot_general(normed[:, columns], grads[...], (TN, ((), ())), preferred_element_type=full)

        return at

    def stored(grads):
        return lambda index: grads[index].astype(full)

    values = (product(d_pre_gate), product(d_branch), stored(gate_grads), stored(small_grads))
    results = (out_gate, out_x, out_gates, out_small)
    items = list(zip(values, travel[:4], travel[4:8], ((0,), (1,), (1,), (0,))))
    scatter = RingScatter(count, items, travel[8:], after, before)

    late = [
        pltpu.make_async_copy(source, target, late_sem.at[at])
        for at, (source, target) in enumerate(
            (
                (normed_far, normed), (d_pre_gate_far, d_pre_gate), (d_branch_far, d_branch), (w_gate_far, w_gate),
                (w_x_far, w_x),
            )
        )
    ]

    def core_copy(k):
        return send(core_out.at[k], core_in.at[k], (core_out_sem.at[k], core_in_sem.at[k]), mate)

    def chip_copy(k):
        return send(chip_out.at[k], chip_in.at[k], (chip_out_sem.at[k], chip_in_sem.at[k]), ahead[k - 1])

    def width_copy(step):
        columns = pl.ds(pl.multiple_of(others[step] * share, share), share)
        sems = (width_out.at[step], width_in.at[step])
        return send(gain_out.at[:, columns], gain_width.at[step], sems, {"dp": others[step]})

    def seq_copy(step):
        return send(gain_total, gain_seq.at[step], (seq_out.at[step], seq_in.at[step]), peers[step][0])

    def through(row):
        return lax.dot_general(
            d_pre_gate[pl.ds(pl.multiple_of(row * block, block), block)],
            w_gate[...],
            (NT, ((), ())),
            preferred_element_type=full,
        ) + lax.dot_general(
            d_branch[pl.ds(pl.multiple_of(row * block, block), block)],
            w_x[...],
            (NT, ((), ())),
            preferred_element_type=full,
        )

    for copy in late:
        copy.start()
    for copy in late[:3]:
        copy.wait()
    scatter.begin(met)
    for copy in late[3:]:
        copy.wait()

    @pl.loop(0, chips)
    def _(at):
        k = chips - 1 - at
        core_out[k] = through(chips + k).astype(low)
        core_copy(k).start()

    scatter.onward(1)

    @pl.loop(0, chips - 1)
    def _(at):
        k = chips - 1 - at
        part = through(k)
        core_copy(k).wait_recv()
        chip_out[k] = (part + core_in[k].astype(full)).astype(low)

    for k in range(chips - 1, 0, -1):
        chip_copy(k).start()
    part = through(0)
    core_copy(0).wait_recv()
    total = part + core_in[0].astype(full)
    for k in range(1, chips):
        chip_copy(k).wait_recv()
        total = total + chip_in[k].astype(full)
    rows = own[...].astype(full)
    scale = lax.rsqrt(jnp.mean(rows * rows, axis=-1, keepdims=True) + epsilon)
    rows = rows * scale
    scaled = total * gains[:1]
    d_inputs[...] = (
        d_middle[...] + scale * (scaled - rows * jnp.mean(scaled * rows, axis=-1, keepdims=True))
    ).astype(low)
    gain_out[...] = jnp.zeros_like(gain_out)
    gain_out[:1] = jnp.sum(total * rows, axis=0, keepdims=True)
    gain_out[1:2] = gain_share[...]
    for step in range(1, width):
        width_copy(step).start()
    if half > 2:
        scatter.onward(2)
    columns = pl.ds(pl.multiple_of(my_width * share, share), share)
    gain_sum = gain_out[:, columns]
    for step in range(1, width):
        width_copy(step).wait_recv()
        gain_sum = gain_sum + gain_width[step]
    gain_total[...] = gain_sum
    for step in range(1, count):
        seq_copy(step).start()
    for step in range(3, half):
        scatter.onward(step)
    for step in range(1, count):
        seq_copy(step).wait_recv()
        gain_sum = gain_sum + gain_seq[step]
    out_gains[...] = gain_sum
    for item, result in enumerate(results):
        result[...] = scatter.finish(item).astype(result.dtype)
    scatter.drain()
    for step in range(1, count):
        seq_copy(step).wait_send()
    for step in range(1, width):
        width_copy(step).wait_send()
    for k in range(chips):
        core_copy(k).wait_send()
    for k in range(1, chips):
        chip_copy(k).wait_send()


def close(operands):
    own, _, _, _, gate_grads, small_grads, normed, d_pre_gate, d_branch, w_gate, w_x = operands
    count, width = lax.axis_size("seq"), lax.axis_size("dp")
    chips = width // CORES
    block, depth = own.shape
    channels = d_pre_gate.shape[1]
    shard, share = depth // count, depth // width
    whole = pl.BlockSpec(memory_space=pltpu.VMEM)
    dma = pltpu.SemaphoreType.DMA
    items = [
        ((shard, channels), low), ((shard, channels), low), (gate_grads.shape[1:], low), (small_grads.shape[1:], full),
    ]
    shapes = [
        ((block, depth), low), *[(shape, low if at < 2 else full) for at, (shape, _) in enumerate(items)],
        ((8, share), full),
    ]
    return pl.pallas_call(
        partial(close_kernel, count, width),
        in_specs=[whole] * (len(operands) - 5) + [pl.BlockSpec(memory_space=pl.ANY)] * 5,
        out_specs=[whole] * len(shapes),
        out_shape=[jax.ShapeDtypeStruct(*shape) for shape in shapes],
        scratch_shapes=[
            *[pltpu.VMEM(each.shape, low) for each in (normed, d_pre_gate, d_branch, w_gate, w_x)],
            dma((5,)),
            *RingScatter.scratch(count, items),
            *[pltpu.VMEM((chips, block, depth), low)] * 4,
            pltpu.VMEM((8, depth), full),
            pltpu.VMEM((width, 8, share), full),
            pltpu.VMEM((8, share), full),
            pltpu.VMEM((count, 8, share), full),
            dma((chips,)), dma((chips,)), dma((chips,)), dma((chips,)),
            dma((width,)), dma((width,)), dma((count,)), dma((count,)),
        ],
        compiler_params=pltpu.CompilerParams(collective_id=5, has_side_effects=True, vmem_limit_bytes=63 << 20),
        cost_estimate=pl.CostEstimate(
            flops=8 * normed.shape[0] * depth * channels, bytes_accessed=40 << 20, transcendentals=0
        ),
    )(*operands)


def lay_out_kernel(count, taps, *refs):
    for source, target in zip(refs[:8], refs[11:19]):
        target[...] = source[...].astype(target.dtype)
    gates, small, gains = refs[8:11]
    taps_out, rate_out, input_out, decay_out, log_out, mix_out, mlp_out = refs[19:]
    size = rate_out.shape[1]
    channels, share = decay_out.shape[1], mix_out.shape[1]
    rate_out[...] = gates[:, :size]
    input_out[...] = gates[:, size:]
    taps_out[...] = small[:taps, :channels]
    decay_out[...] = small[taps : taps + 1, :channels]
    log_out[...] = small[taps + 1 : taps + 2, :channels] / small[taps + 2 : taps + 3, :channels]
    mine = lax.axis_index("seq")
    total = jnp.zeros((8, share), full)
    for at in range(count):
        total = jnp.where(mine == at, gains[:, at * share : (at + 1) * share], total)
    mix_out[...] = total[:1]
    mlp_out[...] = total[1:2]


def lay_out(taps, arrays, gates, small, gains):
    count = lax.axis_size("seq")
    steps = 2

    def block(shape, by_rows):
        if by_rows:
            return pl.BlockSpec((shape[0] // steps, shape[1]), lambda at: (at, 0))
        return pl.BlockSpec((shape[0], shape[1] // steps), lambda at: (0, at))

    def whole(shape):
        return pl.BlockSpec(shape, lambda at: (0, 0))

    cuts = [block(array.shape, by_rows) for array, by_rows, _ in arrays]
    own_channels, both = gates.shape
    share = gains.shape[1] // count
    rest = [(taps, own_channels), (own_channels, both // 2), (own_channels, both // 2), (1, own_channels)]
    rest += [(1, own_channels), (1, share), (1, share)]
    return pl.pallas_call(
        partial(lay_out_kernel, count, taps),
        grid=(steps,),
        in_specs=cuts + [whole(each.shape) for each in (gates, small, gains)],
        out_specs=cuts + [whole(shape) for shape in rest],
        out_shape=[jax.ShapeDtypeStruct(array.shape, kind) for array, _, kind in arrays]
        + [jax.ShapeDtypeStruct(shape, full) for shape in rest],
        compiler_params=pltpu.CompilerParams(vmem_limit_bytes=63 << 20),
    )(*[array for array, _, _ in arrays], gates, small, gains)


def on_device(
    inputs,
    cotangent,
    resets,
    real_mask,
    gain_mix,
    w_branch_gate,
    w_branch_x,
    conv_kernel,
    gate_rate,
    gate_input,
    decay_param,
    w_mix_out,
    gain_mlp,
    w_mlp_gate,
    w_mlp_up,
    w_mlp_down,
):
    seq = lax.axis_size("seq")
    rows_own, length, depth = inputs.shape
    taps = conv_kernel.shape[1]
    block = rows_own * length
    tokens = block * lax.axis_size("dp")
    own_channels, size = gate_rate.shape
    shard, part_w = w_branch_x.shape
    rows = inputs.reshape(block, depth)
    (
        marks, w_both, gains, chan, cot_low, middle, feed_own, halo, ends, d_feed, w_down,
        w_gate_all, w_x_all, mixer_in, pre_gate, branch, w_mix_out, conv_low, pre_rate, pre_inlet, rate_mat, inlet_mat,
        states, mixed,
    ) = forward(
        rows, cotangent.reshape(block, depth), resets, real_mask, gain_mix, gain_mlp, conv_kernel.T,
        decay_param[None], gate_rate, gate_input, w_branch_gate, w_branch_x, w_mix_out, w_mlp_gate, w_mlp_up,
        w_mlp_down,
    )
    w_down = w_down.reshape(-1, depth)

    d_feed_own, feed_sum, down_own, down_others, hidden = feed_forward(feed_own, w_both, w_down, d_feed)

    (
        output, d_middle, d_pre_gate, d_branch, grad_mix_out, gate_grads, small_grads, gain_share, grad_down,
        feed_gate, feed_up,
    ) = mix_back(
        taps,
        size,
        (gains, marks, chan, halo, ends),
        (d_feed_own, middle, cot_low, w_down, w_mix_out, mixed, rate_mat, inlet_mat, conv_low, down_own),
        (pre_gate, pre_rate, pre_inlet, states, branch),
        hidden,
        down_others,
        feed_sum.reshape(seq, shard, -1),
    )

    grad_inputs, grad_gate, grad_x, grad_gates, grad_small, gains = close(
        (
            rows, d_middle, gains, gain_share, gate_grads, small_grads, mixer_in, d_pre_gate.reshape(tokens, part_w),
            d_branch.reshape(tokens, part_w), w_gate_all.reshape(depth, part_w), w_x_all.reshape(depth, part_w),
        )
    )
    (
        output, grad_inputs, grad_gate, grad_x, feed_gate, feed_up, grad_mix_out, grad_down,
        grad_taps, grad_rate, grad_input, grad_decay, decay_log, grad_gain_mix, grad_gain_mlp,
    ) = lay_out(
        taps,
        (
            (output, True, low), (grad_inputs, True, low), (grad_gate, True, full), (grad_x, True, full),
            (feed_gate, True, full), (feed_up, True, full), (grad_mix_out, False, full), (grad_down, False, full),
        ),
        grad_gates,
        grad_small,
        gains,
    )
    return (
        output[None],
        grad_inputs[None],
        grad_gain_mix[0],
        grad_gate,
        grad_x,
        grad_taps.T,
        grad_rate,
        grad_input,
        grad_decay[0],
        grad_mix_out,
        grad_gain_mlp[0],
        feed_gate,
        feed_up,
        grad_down,
        decay_log[0],
    )


def solution(mesh):
    placed = (
        P("dp", "seq", None),
        P("dp", "seq", None),
        P("dp", "seq"),
        P("dp", "seq"),
        P("seq"),
        P("seq", "dp"),
        P("seq", "dp"),
        P(("dp", "seq"), None),
        P(("dp", "seq"), None),
        P(("dp", "seq"), None),
        P(("dp", "seq")),
        P(("dp", "seq"), None),
        P("seq"),
        P("seq", "dp"),
        P("seq", "dp"),
        P(("dp", "seq"), None),
    )
    return jax.shard_map(
        on_device,
        mesh=mesh,
        in_specs=placed,
        out_specs=(
            P("dp", "seq", None),
            P("dp", "seq", None),
            P(("dp", "seq")),
            P("seq", "dp"),
            P("seq", "dp"),
            P(("dp", "seq"), None),
            P(("dp", "seq"), None),
            P(("dp", "seq"), None),
            P(("dp", "seq")),
            P(("dp", "seq"), None),
            P(("dp", "seq")),
            P("seq", "dp"),
            P("seq", "dp"),
            P(("dp", "seq"), None),
            P(("dp", "seq")),
        ),
        check_vma=False,
    )
```
